256 devices in a mesh: grp: 8 (over x, core), dev: 32 (over z, y).
Axes of the slice: x: 4, y: 4, z: 8, core: 2. Of those that a mesh axis runs over, the one named last changes fastest.
Arguments:
- inputs: bfloat16 [512, 8, 8, 512], P(('grp', 'dev')), may hold values from -6 to 6
- occupancy: int32 [512, 8, 64], P(('grp', 'dev')), may hold values 0 or 1
- neighbours: int32 [512, 26], P(('grp', 'dev')), may hold values from -1 to 511, as said below
- first_kernel: bfloat16 [1728, 64], replicated, may hold values from -0.15625 to 0.15625
- second_kernel: bfloat16 [1728, 64], replicated, may hold values from -0.15625 to 0.15625
- out_grads: bfloat16 [512, 8, 8, 512], P(('grp', 'dev')), may hold values from -6 to 6
Outputs:
- input_grads: bfloat16 [512, 8, 8, 512], P(('grp', 'dev'))
- first_kernel_grads: float32 [1728, 64], replicated
- second_kernel_grads: float32 [1728, 64], replicated
The draws below stay inside these ranges and needn't reach their ends.
Inputs may be any that keep to these rules, and one draw needn't show every extreme that they name: `neighbours`: column d names the brick beside brick k in direction d, the 26 directions (d_x, d_y, d_z) in the finite set (-1,0,1)^3 without (0,0,0) in lexicographic order, or -1 where there is no brick; the relation is symmetric and geometric. Brick k lies on device k // 2 of grp+dev, and a named brick lies on a device at most 4 away from brick k's device; that distance occurs in every draw.
All inputs are finite; a program needn't handle non-finite values. No bound on the sum of `occupancy` on one device may be relied on, other than what follows from the above.
Results may differ from the reference program's by a relative error of at most 0.005.
Values may be sent and summed in bfloat16 or wider, within the bound.
No kernel may reach another device: no remote copies, remote signals or barrier semaphores. Data moves between devices by JAX's collectives and lax.ppermute only.
A program may use at most 128 MiB of HBM per device.

```python
import math
import jax
import jax.numpy as jnp
from jax import lax

CHANNELS = 64
BRICK = 8
BRICKS_DEV = 2
BRICKS = 512


def directions_drawn():
    result = []
    for along_x in (-1, 0, 1):
        for along_y in (-1, 0, 1):
            for along_z in (-1, 0, 1):
                if along_x != 0 or along_y != 0 or along_z != 0:
                    result.append((along_x, along_y, along_z))
    return result


def draw_neighbours(key, part):
    strides = jax.random.randint(key, (BRICKS,), 1, 3)
    counter = jnp.arange(BRICKS, dtype=jnp.int32)
    strides = jnp.where(counter <= BRICKS_DEV + 8, 1, strides)
    strides = jnp.where(counter == 0, 0, strides)
    start_offset = (4 - (BRICKS_DEV - 1) % 4) % 4
    positions = start_offset + jnp.cumsum(strides)
    columns_list = []
    for along_x, along_y, along_z in directions_drawn():
        cell_x = positions // 4 + along_x
        cell_y = positions // 2 % 2 + along_y
        cell_z = positions % 2 + along_z
        inside = (cell_x >= 0) & (cell_y >= 0) & (cell_y <= 1) & (cell_z >= 0) & (cell_z <= 1)
        target = 4 * cell_x + 2 * cell_y + cell_z
        located = jnp.clip(jnp.searchsorted(positions, target), 0, BRICKS - 1)
        matched = inside & (positions[located] == target)
        columns_list.append(jnp.where(matched, located, -1))
    return jnp.stack(columns_list, axis=1).astype(jnp.int32)


def with_ends(array, stream_key, smallest, top_value):
    longest = array.shape.index(max(array.shape))
    spots = []
    for shift in (0, 1):
        where = [jax.random.randint(jax.random.fold_in(stream_key, axis), (), 0, length) for axis, length in enumerate(array.shape)]
        where[longest] = (where[longest] + shift) % array.shape[longest]
        spots.append(tuple(where))
    return array.at[spots[0]].set(smallest).at[spots[1]].set(top_value)


def block_levels(stream_key, dims, cuts, low, largest):
    def one(position, blocks):
        heights = jax.random.uniform(jax.random.fold_in(jax.random.fold_in(stream_key, 6), position), (blocks,), jnp.float32, low / len(cuts), largest / len(cuts))
        return jnp.repeat(jnp.exp(heights), dims[position] // blocks).reshape((-1,) + (1,) * (len(dims) - position - 1))

    loudness = one(*cuts[0])
    for cut in cuts[1:]:
        loudness = loudness * one(*cut)
    return loudness


def gaussian(key, shape, width, reach, cuts=(), kind=jnp.bfloat16):
    drawn = width * jax.random.normal(key, shape, jnp.float32)
    if cuts:
        drawn = drawn * block_levels(key, shape, cuts, -0.22, 0.18)
    return jnp.clip(drawn, -reach, reach).astype(kind)


def setup_inputs(seed: int = 0) -> dict:
    key_list = jax.random.split(jax.random.key(seed), 7)
    inputs = gaussian(key_list[0], (BRICKS, BRICK, BRICK, BRICK * CHANNELS), 1.0, 6.0, ((0, 256),))
    occupancy = with_ends((jax.random.randint(key_list[1], (BRICKS, BRICK, BRICK * BRICK), 0, 4) < 3).astype(jnp.int32), jax.random.fold_in(key_list[1], 1), 0, 1)
    neighbours = draw_neighbours(jax.random.fold_in(key_list[6], 71), 0)
    first_kernel = gaussian(key_list[3], (27 * CHANNELS, CHANNELS), (27 * CHANNELS) ** -0.5, 0.15625)
    second_kernel = gaussian(key_list[4], (27 * CHANNELS, CHANNELS), (27 * CHANNELS) ** -0.5, 0.15625)
    out_grads = gaussian(key_list[5], (BRICKS, BRICK, BRICK, BRICK * CHANNELS), 1.0, 6.0, ((0, 256),))
    return {"inputs": inputs, "occupancy": occupancy, "neighbours": neighbours, "first_kernel": first_kernel, "second_kernel": second_kernel, "out_grads": out_grads}


def directions():
    result = []
    for along_x in (-1, 0, 1):
        for along_y in (-1, 0, 1):
            for along_z in (-1, 0, 1):
                if along_x != 0 or along_y != 0 or along_z != 0:
                    result.append((along_x, along_y, along_z))
    return result

def source_range(offset, halo_depth, extent):
    if offset > 0:
        return slice(0, halo_depth)
    if offset < 0:
        return slice(extent - halo_depth, extent)
    return slice(0, extent)

def target_range(offset, halo_depth, extent):
    if offset < 0:
        return slice(0, halo_depth)
    if offset > 0:
        return slice(halo_depth + extent, 2 * halo_depth + extent)
    return slice(halo_depth, halo_depth + extent)

def columns(padded, shift_x, extent):
    channels = padded.shape[3]
    pieces = []
    for shift_y in range(3):
        for shift_z in range(3):
            pieces.append(padded[shift_x:shift_x + extent, shift_y:shift_y + extent, shift_z:shift_z + extent, :])
    return jnp.concatenate(pieces, axis=3).reshape(extent * extent * extent, 9 * channels)

def convolve(padded, kernel):
    extent = padded.shape[0] - 2
    block_rows = kernel.shape[0] // 3
    accumulated = jnp.zeros((extent ** 3, kernel.shape[1]), jnp.float32)
    for shift_x in range(3):
        accumulated = accumulated + jnp.dot(columns(padded, shift_x, extent), kernel[shift_x * block_rows:(shift_x + 1) * block_rows], preferred_element_type=jnp.float32)
    return accumulated

def kernel_grad(padded, gradients):
    extent = padded.shape[0] - 2
    blocks = []
    for shift_x in range(3):
        blocks.append(lax.dot_general(columns(padded, shift_x, extent), gradients, (((0,), (0,)), ((), ())), preferred_element_type=jnp.float32))
    return jnp.concatenate(blocks, axis=0)

def flipped(kernel):
    channels = kernel.shape[1]
    return jnp.transpose(kernel.reshape(27, channels, channels)[::-1], (0, 2, 1)).reshape(27 * channels, channels)

def silu_slope(pre_act):
    logistic = jax.nn.sigmoid(pre_act)
    return logistic * (1.0 + pre_act * (1.0 - logistic))

def padded_brick(source_field, neighbours, brick_index, halo_depth):
    extent = source_field.shape[1]
    channels = source_field.shape[4]
    padded_extent = extent + 2 * halo_depth
    padded = jnp.zeros((padded_extent, padded_extent, padded_extent, channels), source_field.dtype)
    inner = slice(halo_depth, halo_depth + extent)
    padded = padded.at[inner, inner, inner].set(source_field[brick_index])
    for number, (along_x, along_y, along_z) in enumerate(directions()):
        source = neighbours[brick_index, number]
        region = source_field[jnp.maximum(source, 0)]
        region = region[source_range(along_x, halo_depth, extent), source_range(along_y, halo_depth, extent), source_range(along_z, halo_depth, extent)]
        region = jnp.where(source >= 0, region, jnp.zeros_like(region))
        padded = padded.at[target_range(along_x, halo_depth, extent), target_range(along_y, halo_depth, extent), target_range(along_z, halo_depth, extent)].set(region)
    return padded

def reference(inputs, occupancy, neighbours, first_kernel, second_kernel, out_grads):
    bricks = inputs.shape[0]
    extent = inputs.shape[1]
    channels = first_kernel.shape[1]
    features = inputs.reshape(bricks, extent, extent, extent, channels)
    cotangent = out_grads.reshape(bricks, extent, extent, extent, channels)
    occupied = occupancy.reshape(bricks, extent ** 3, 1).astype(jnp.float32)
    masked = cotangent * occupancy.reshape(bricks, extent, extent, extent, 1).astype(cotangent.dtype)
    first_flip = flipped(first_kernel)
    second_flip = flipped(second_kernel)
    indices = jnp.arange(bricks, dtype=jnp.int32)

    def forward(brick_index):
        pre_act = convolve(padded_brick(features, neighbours, brick_index, 1), first_kernel)
        hidden = (jax.nn.silu(pre_act) * occupied[brick_index]).astype(jnp.bfloat16)
        return (pre_act, hidden)
    pre_acts, hidden = lax.map(forward, indices)
    hidden_field = hidden.reshape(bricks, extent, extent, extent, channels)

    def backward(brick_index):
        hidden_grad = convolve(padded_brick(masked, neighbours, brick_index, 1), second_flip)
        return (hidden_grad * silu_slope(pre_acts[brick_index]) * occupied[brick_index]).astype(jnp.bfloat16)
    pre_grads = lax.map(backward, indices)
    pre_field = pre_grads.reshape(bricks, extent, extent, extent, channels)

    def accumulate(sums_so_far, brick_index):
        first_sum, second_sum = sums_so_far
        second_sum = second_sum + kernel_grad(padded_brick(hidden_field, neighbours, brick_index, 1), masked[brick_index].reshape(extent ** 3, channels))
        first_sum = first_sum + kernel_grad(padded_brick(features, neighbours, brick_index, 1), pre_grads[brick_index])
        input_grad = (convolve(padded_brick(pre_field, neighbours, brick_index, 1), first_flip) * occupied[brick_index]).astype(jnp.bfloat16)
        return ((first_sum, second_sum), input_grad)
    zeros = jnp.zeros((27 * channels, channels), jnp.float32)
    (first_sum, second_sum), input_grads = lax.scan(accumulate, (zeros, zeros), indices)
    scaling = 1.0 / math.sqrt(BRICKS * BRICK ** 3)
    return (input_grads.reshape(bricks, extent, extent, extent * channels), first_sum * scaling, second_sum * scaling)
```

```python
import functools
import math

import jax
import jax.numpy as jnp
from jax import lax
from jax.experimental import pallas as pl
from jax.experimental.pallas import tpu as pltpu
from jax.sharding import PartitionSpec as P

AXES = ("grp", "dev")
GROUP = 8
EDGE = 8
WIDE = 512
PADDED = 640
ROWS = 24
PACKED = 2048
BF16 = jnp.bfloat16
F32 = jnp.float32


def directions():
    result = []
    for along_x in (-1, 0, 1):
        for along_y in (-1, 0, 1):
            for along_z in (-1, 0, 1):
                if along_x != 0 or along_y != 0 or along_z != 0:
                    result.append((along_x, along_y, along_z))
    return result


DIRECTIONS = directions()
NUMBER = {offset: number for number, offset in enumerate(DIRECTIONS)}


def locate(nb_ref, me, brick, number):
    other = nb_ref[brick, number]
    present = other >= 0
    owner = jnp.maximum(other, 0) >> 1
    same = (owner >> 3) == (me >> 3)
    box = jnp.where(same, owner & 7, 8 + ((owner + 4) & 7))
    return present, box, other & 1


def send_place(nb_ref, me, brick, number):
    present, box, slot = locate(nb_ref, me, brick, number)
    unused = (8 + ((me + 4) & 7)) * 4
    return jnp.where(present, box * 4 + brick * 2 + slot, unused)


def face_kind(offset):
    for axis in range(3):
        if offset[axis] != 0:
            return axis, 1 if offset[axis] > 0 else 0


def face_values(wide, index):
    faces = {}
    for side, at in ((0, 0), (1, EDGE - 1)):
        faces[0, side] = wide[index, at * EDGE : (at + 1) * EDGE, :]
        faces[1, side] = jnp.concatenate(
            [wide[index, x * EDGE + at : x * EDGE + at + 1, :] for x in range(EDGE)], axis=0
        )
        faces[2, side] = jnp.concatenate(
            [
                wide[index, x * EDGE : (x + 1) * EDGE, at * 64 : (at + 1) * 64]
                for x in range(EDGE)
            ],
            axis=1,
        )
    return faces


def spread(occ_ref):
    rows = []
    for x in range(EDGE):
        for brick in range(2):
            rows.append(jnp.broadcast_to(occ_ref[brick, x : x + 1, :].astype(F32), (EDGE, 64)))
    stacked = jnp.concatenate(rows, axis=0)
    row = lax.broadcasted_iota(jnp.int32, stacked.shape, 0)
    lane = lax.broadcasted_iota(jnp.int32, stacked.shape, 1)
    own = jnp.where((row & 7) == (lane >> 3), stacked, 0.0).astype(BF16)
    source = lax.broadcasted_iota(jnp.int32, (64, WIDE), 0)
    target = lax.broadcasted_iota(jnp.int32, (64, WIDE), 1)
    select = jnp.where((source & 7) == (target >> 6), 1.0, 0.0).astype(BF16)
    return jnp.dot(own, select, preferred_element_type=F32)


def pack_kernel(
    me_ref, nb_ref, x_ref, g_ref, occ_ref, even_ref, odd_ref, masked_ref, wide, boxes
):
    me = me_ref[0]
    occupied = spread(occ_ref)
    for x in range(EDGE):
        both = []
        for brick in range(2):
            wide[brick, x * EDGE : (x + 1) * EDGE, :] = x_ref[brick, x].astype(F32)
            at = (2 * x + brick) * EDGE
            piece = g_ref[brick, x].astype(F32) * occupied[at : at + EDGE]
            wide[2 + brick, x * EDGE : (x + 1) * EDGE, :] = piece
            both.append(piece)
        masked_ref[x] = jnp.concatenate(both, axis=0).astype(BF16)
    for brick in range(2):
        first = face_values(wide, brick)
        second = face_values(wide, 2 + brick)
        packets = {}
        for key in first:
            packets[key] = jnp.concatenate([first[key], second[key]], axis=0).astype(BF16)
        for number, offset in enumerate(DIRECTIONS):
            boxes[send_place(nb_ref, me, brick, number)] = packets[face_kind(offset)]
    even_ref[...] = boxes[0:32].reshape(8, 4, 16, WIDE)
    odd_ref[...] = boxes[32:64].reshape(8, 4, 16, WIDE)


def beside(low, middle, high):
    return jnp.concatenate([low, middle, high], axis=1)


def fill_padded(padded, own, pick):
    def planes(along_x, along_y):
        return (
            pick((along_x, along_y, -1))[:, WIDE - 64 :],
            pick((along_x, along_y, 0)),
            pick((along_x, along_y, 1))[:, :64],
        )

    below, above = pick((0, 0, -1)), pick((0, 0, 1))
    for x in range(EDGE):
        lanes = slice(x * 64, (x + 1) * 64)
        start = (x + 1) * ROWS + 8
        padded[start : start + EDGE, :] = beside(below[:, lanes], own(x), above[:, lanes])
    for along_y, row in ((-1, 7), (1, 16)):
        value = beside(*planes(0, along_y))
        for x in range(EDGE):
            start = (x + 1) * ROWS + row
            padded[start : start + 1, :] = value[x : x + 1]
    for along_x, at in ((-1, 0), (1, 9)):
        start = at * ROWS + 8
        padded[start : start + EDGE, :] = beside(*planes(along_x, 0))
        for along_y, row, source in ((-1, 7, 7), (1, 16, 0)):
            value = beside(*planes(along_x, along_y))
            padded[at * ROWS + row : at * ROWS + row + 1, :] = value[source : source + 1]


def fill_windows(first, second, shifted, windows):
    for along_y in range(3):
        for x in range(10):
            start = x * ROWS + 7 + along_y
            shifted[along_y, x] = jnp.concatenate(
                [first[start : start + EDGE, :], second[start : start + EDGE, :]], axis=0
            ).astype(BF16)
    for pair in range(4):
        for along_x in range(3):
            for along_y in range(3):
                place = (3 * along_x + along_y) * 256
                windows[pair * 128 : (pair + 1) * 128, place : place + 256] = shifted[
                    along_y, along_x : along_x + EDGE, :, pair * 128 : pair * 128 + 256
                ].reshape(128, 256)


def fill_direct(kernel_ref, direct):
    for group in range(9):
        block = kernel_ref[group * 192 : (group + 1) * 192, :]
        none = jnp.zeros((64, 64), BF16)
        direct[group * 256 : (group + 1) * 256, :] = jnp.concatenate(
            [
                jnp.concatenate([block, none], axis=0),
                jnp.concatenate([none, block], axis=0),
            ],
            axis=1,
        )


def fill_flipped(kernel_ref, flipped):
    none = jnp.zeros((64, 64), BF16)
    for group in range(9):
        base = 3 * (8 - group)
        blocks = [kernel_ref[(base + z) * 64 : (base + z + 1) * 64, :] for z in (2, 1, 0)]
        lanes = slice(group * 256, (group + 1) * 256)
        flipped[0:64, lanes] = jnp.concatenate(blocks + [none], axis=1)
        flipped[64:128, lanes] = jnp.concatenate([none] + blocks, axis=1)


def times_flipped(windows, flipped):
    return lax.dot_general(
        windows, flipped, (((1,), (1,)), ((), ())), preferred_element_type=F32
    )


def paired(natural):
    return jnp.concatenate([natural[:, p * 128 : (p + 1) * 128] for p in range(4)], axis=0)


def unpaired(value):
    return jnp.concatenate([value[p * 128 : (p + 1) * 128] for p in range(4)], axis=1)


def gather_blocks(product):
    pieces = []
    for group in range(9):
        at = group * 256
        pieces.append(product[0:64, at : at + 192] + product[64:128, at + 64 : at + 256])
    pieces.append(jnp.zeros((64, PACKED - 27 * 64), F32))
    return jnp.concatenate(pieces, axis=1)


def main_kernel(
    me_ref,
    nb_ref,
    x_ref,
    masked_ref,
    occ_ref,
    even_in,
    odd_in,
    first_ref,
    second_ref,
    grads_ref,
    even_ref,
    odd_ref,
    padded,
    shifted,
    windows,
    direct,
    flipped,
    product,
    wide,
    boxes,
):
    me = me_ref[0]
    for brick in range(2):
        values = {}
        for number, offset in enumerate(DIRECTIONS):
            present, box, slot = locate(nb_ref, me, brick, number)
            place = slot * 2 + brick
            low = even_in[box & 7, place].astype(F32)
            high = odd_in[box & 7, place].astype(F32)
            values[offset] = jnp.where(present, jnp.where(box < 8, low, high), 0.0)

        def own_first(x):
            return x_ref[brick, x].astype(F32)

        def own_second(x):
            return masked_ref[x].astype(F32)[brick * EDGE : (brick + 1) * EDGE]

        fill_padded(padded.at[0, brick], own_first, lambda offset: values[offset][0:8])
        fill_padded(padded.at[1, brick], own_second, lambda offset: values[offset][8:16])
    for field in range(2):
        fill_windows(padded.at[field, 0], padded.at[field, 1], shifted.at[field], windows.at[field])
    fill_direct(first_ref, direct)
    fill_flipped(second_ref, flipped)
    occupied = paired(spread(occ_ref))
    pre_act = jnp.dot(windows[0], direct[...], preferred_element_type=F32)
    logistic = 1.0 / (1.0 + jnp.exp(-pre_act))
    hidden = (pre_act * logistic * occupied).astype(BF16)
    slope = logistic * (1.0 + pre_act * (1.0 - logistic))
    hidden_grad = times_flipped(windows[1], flipped[...])
    pre_grads = (hidden_grad * slope * occupied).astype(BF16)

    natural = unpaired(pre_grads.astype(F32))
    for x in range(EDGE):
        grads_ref[x] = natural[16 * x : 16 * x + 16].astype(BF16)
        for brick in range(2):
            at = 16 * x + EDGE * brick
            wide[brick, x * EDGE : (x + 1) * EDGE, :] = natural[at : at + EDGE]
    for brick in range(2):
        faces = face_values(wide, brick)
        for number, offset in enumerate(DIRECTIONS):
            boxes[send_place(nb_ref, me, brick, number)] = faces[face_kind(offset)]
    for box in range(8):
        even_ref[box, 0:32, :] = boxes[4 * box : 4 * box + 4].reshape(32, WIDE).astype(BF16)
        odd_ref[box] = boxes[32 + 4 * box : 36 + 4 * box].reshape(32, WIDE).astype(BF16)

    for half, own, field in ((0, hidden, 1), (1, pre_grads, 0)):
        turned = own.astype(F32).T.astype(BF16)
        product[...] = jnp.dot(turned, windows[field], preferred_element_type=F32)
        packed = gather_blocks(product).astype(BF16)
        for chunk in range(4):
            for part in range(4):
                at = 32 + 16 * part
                even_ref[4 * half + chunk, at : at + 16, :] = packed[
                    16 * chunk : 16 * chunk + 16, part * WIDE : (part + 1) * WIDE
                ]


def first_sum_kernel(parts_ref, tiles_ref):
    total = parts_ref[0, 32:96, :].astype(F32)
    for member in range(1, GROUP):
        total = total + parts_ref[member, 32:96, :].astype(F32)
    for down in range(8):
        for along in range(4):
            tiles_ref[4 * down + along] = total[
                8 * down : 8 * down + 8, 128 * along : 128 * along + 128
            ]


def second_sum_kernel(scaling, parts_ref, tiles_ref):
    members = parts_ref.shape[0]
    total = parts_ref[0]
    for member in range(1, members):
        total = total + parts_ref[member]
    total = total * scaling
    for member in range(members):
        tiles_ref[member] = total


def share_kernel(tiles_ref, odd_ref, out_ref):
    rows = []
    for down in range(8):
        rows.append(
            jnp.concatenate([tiles_ref[4 * down + along] for along in range(4)], axis=1)
        )
    chunk = jnp.concatenate(rows, axis=0).astype(BF16)
    for member in range(GROUP):
        out_ref[member, 0:32, :] = odd_ref[member]
        out_ref[member, 32:96, :] = chunk


def last_kernel(
    me_ref,
    nb_ref,
    grads_ref,
    occ_ref,
    even_in,
    odd_in,
    first_ref,
    out_ref,
    first_out,
    second_out,
    padded,
    shifted,
    windows,
    flipped,
    boxes,
):
    me = me_ref[0]
    for box in range(8):
        boxes[4 * box : 4 * box + 4] = (
            even_in[box, 0:32, :].astype(F32).reshape(4, EDGE, WIDE)
        )
        boxes[32 + 4 * box : 36 + 4 * box] = (
            odd_in[box, 0:32, :].astype(F32).reshape(4, EDGE, WIDE)
        )
    for brick in range(2):
        values = {}
        for number, offset in enumerate(DIRECTIONS):
            present, box, slot = locate(nb_ref, me, brick, number)
            values[offset] = jnp.where(present, boxes[4 * box + slot * 2 + brick], 0.0)

        def own(x):
            return grads_ref[x].astype(F32)[brick * EDGE : (brick + 1) * EDGE]

        fill_padded(padded.at[brick], own, lambda offset: values[offset])
    fill_windows(padded.at[0], padded.at[1], shifted, windows)
    fill_flipped(first_ref, flipped)
    result = unpaired(times_flipped(windows[...], flipped[...])) * spread(occ_ref)
    for x in range(EDGE):
        for brick in range(2):
            at = 16 * x + EDGE * brick
            out_ref[brick, x] = result[at : at + EDGE].astype(BF16)

    halves = []
    for half in range(2):
        rows = []
        for chunk in range(4 * half, 4 * half + 4):
            slot = (chunk + 4) & 7
            rows.append(
                jnp.concatenate(
                    [odd_in[slot, 32 + 16 * part : 48 + 16 * part, :] for part in range(4)],
                    axis=1,
                )
            )
        halves.append(jnp.concatenate(rows, axis=0).astype(F32))
    for block in range(27):
        at = (26 - block) * 64
        second_out[at : at + 64, :] = halves[0][:, block * 64 : block * 64 + 64]
    for pair in range(14):
        turned = halves[1][:, pair * 128 : pair * 128 + 128].T
        count = min(128, 27 * 64 - pair * 128)
        first_out[pair * 128 : pair * 128 + count, :] = turned[:count]


def call(kernel, shapes, scratch, arguments, scalars=0, flops=0):
    specs = [pl.BlockSpec(memory_space=pltpu.SMEM)] * scalars
    specs += [pl.BlockSpec(memory_space=pltpu.VMEM)] * (len(arguments) - scalars)
    return pl.pallas_call(
        kernel,
        out_shape=[jax.ShapeDtypeStruct(shape, kind) for shape, kind in shapes],
        in_specs=specs,
        out_specs=[pl.BlockSpec(memory_space=pltpu.VMEM)] * len(shapes),
        scratch_shapes=[pltpu.VMEM(shape, kind) for shape, kind in scratch],
        compiler_params=pltpu.CompilerParams(vmem_limit_bytes=40 * 1024 * 1024),
    )(*arguments)


def per_device(inputs, occupancy, neighbours, first_kernel, second_kernel, out_grads):
    devices = lax.axis_size("grp") * lax.axis_size("dev")
    members = devices // GROUP
    scaling = 1.0 / math.sqrt(inputs.shape[0] * devices * EDGE**3)
    even = [[GROUP * k + j for j in range(GROUP)] for k in range(members)]
    odd = [[(GROUP * k + 4 + j) % devices for j in range(GROUP)] for k in range(members)]
    across = [[GROUP * j + k for j in range(members)] for k in range(GROUP)]
    me = (lax.axis_index("grp") * lax.axis_size("dev") + lax.axis_index("dev")).reshape(1)

    def swap(value, groups):
        return lax.all_to_all(value, AXES, 0, 0, axis_index_groups=groups, tiled=True)

    halo = ((GROUP, 4, 16, WIDE), BF16)
    even_out, odd_out, masked = call(
        pack_kernel,
        [halo, halo, ((EDGE, 16, WIDE), BF16)],
        [((4, 64, WIDE), F32), ((64, 16, WIDE), BF16)],
        [me, neighbours, inputs, out_grads, occupancy],
        scalars=2,
    )
    even_in = swap(even_out, even)
    odd_in = swap(odd_out, odd)
    pre_grads, even_out, odd_out = call(
        main_kernel,
        [
            ((EDGE, 16, WIDE), BF16),
            ((GROUP, 96, WIDE), BF16),
            ((GROUP, 32, WIDE), BF16),
        ],
        [
            ((2, 2, 10 * ROWS, PADDED), F32),
            ((2, 3, 10, 16, PADDED), BF16),
            ((2, 512, 2304), BF16),
            ((2304, 128), BF16),
            ((128, 2304), BF16),
            ((128, 2304), F32),
            ((2, 64, WIDE), F32),
            ((64, EDGE, WIDE), F32),
        ],
        [me, neighbours, inputs, masked, occupancy, even_in, odd_in, first_kernel, second_kernel],
        scalars=2,
    )
    even_in = swap(even_out, even)
    (tiles,) = call(first_sum_kernel, [((32, 8, 128), F32)], [], [even_in])
    across_shape = (members, 32 // members, 8, 128)
    tiles = swap(tiles.reshape(across_shape), across)
    (tiles,) = call(
        functools.partial(second_sum_kernel, scaling), [(across_shape, F32)], [], [tiles]
    )
    tiles = swap(tiles, across).reshape(32, 8, 128)
    (odd_out,) = call(share_kernel, [((GROUP, 96, WIDE), BF16)], [], [tiles, odd_out])
    odd_in = swap(odd_out, odd)
    return tuple(
        call(
            last_kernel,
            [
                ((2, EDGE, EDGE, WIDE), BF16),
                ((27 * 64, 64), F32),
                ((27 * 64, 64), F32),
            ],
            [
                ((2, 10 * ROWS, PADDED), F32),
                ((3, 10, 16, PADDED), BF16),
                ((512, 2304), BF16),
                ((128, 2304), BF16),
                ((64, EDGE, WIDE), F32),
            ],
            [me, neighbours, pre_grads, occupancy, even_in, odd_in, first_kernel],
            scalars=2,
        )
    )


def solution(mesh):
    in_specs = (
        P(("grp", "dev"), None, None, None),
        P(("grp", "dev"), None, None),
        P(("grp", "dev"), None),
        P(),
        P(),
        P(("grp", "dev"), None, None, None),
    )
    out_specs = (P(("grp", "dev"), None, None, None), P(), P())
    return jax.shard_map(
        per_device, mesh=mesh, in_specs=in_specs, out_specs=out_specs, check_vma=False
    )
```

```python
import functools
import math

import jax
import jax.numpy as jnp
from jax import lax
from jax.experimental import pallas as pl
from jax.experimental.pallas import tpu as pltpu
from jax.sharding import PartitionSpec as P

AXES = ("grp", "dev")
GROUP = 8
EDGE = 8
WIDE = 512
PADDED = 640
ROWS = 24
PACKED = 2048
BF16 = jnp.bfloat16
F32 = jnp.float32


def directions():
    result = []
    for along_x in (-1, 0, 1):
        for along_y in (-1, 0, 1):
            for along_z in (-1, 0, 1):
                if along_x != 0 or along_y != 0 or along_z != 0:
                    result.append((along_x, along_y, along_z))
    return result


DIRECTIONS = directions()
NUMBER = {offset: number for number, offset in enumerate(DIRECTIONS)}


def locate(nb_ref, me, brick, number):
    other = nb_ref[brick, number]
    present = other >= 0
    owner = jnp.maximum(other, 0) >> 1
    same = (owner >> 3) == (me >> 3)
    box = jnp.where(same, owner & 7, 8 + ((owner + 4) & 7))
    return present, box, other & 1


def send_place(nb_ref, me, brick, number):
    present, box, slot = locate(nb_ref, me, brick, number)
    unused = (8 + ((me + 4) & 7)) * 4
    return jnp.where(present, box * 4 + brick * 2 + slot, unused)


def face_kind(offset):
    for axis in range(3):
        if offset[axis] != 0:
            return axis, 1 if offset[axis] > 0 else 0


def face_values(wide, index):
    faces = {}
    for side, at in ((0, 0), (1, EDGE - 1)):
        faces[0, side] = wide[index, at * EDGE : (at + 1) * EDGE, :]
        faces[1, side] = jnp.concatenate(
            [wide[index, x * EDGE + at : x * EDGE + at + 1, :] for x in range(EDGE)], axis=0
        )
        faces[2, side] = jnp.concatenate(
            [
                wide[index, x * EDGE : (x + 1) * EDGE, at * 64 : (at + 1) * 64]
                for x in range(EDGE)
            ],
            axis=1,
        )
    return faces


def spread(occ_ref):
    rows = []
    for x in range(EDGE):
        for brick in range(2):
            rows.append(jnp.broadcast_to(occ_ref[brick, x : x + 1, :].astype(F32), (EDGE, 64)))
    stacked = jnp.concatenate(rows, axis=0)
    row = lax.broadcasted_iota(jnp.int32, stacked.shape, 0)
    lane = lax.broadcasted_iota(jnp.int32, stacked.shape, 1)
    own = jnp.where((row & 7) == (lane >> 3), stacked, 0.0).astype(BF16)
    source = lax.broadcasted_iota(jnp.int32, (64, WIDE), 0)
    target = lax.broadcasted_iota(jnp.int32, (64, WIDE), 1)
    select = jnp.where((source & 7) == (target >> 6), 1.0, 0.0).astype(BF16)
    return jnp.dot(own, select, preferred_element_type=F32)


def pack_kernel(
    me_ref,
    nb_ref,
    x_hbm,
    g_hbm,
    occ_hbm,
    even_ref,
    odd_ref,
    masked_ref,
    x_ref,
    g_ref,
    occ_ref,
    wide,
    boxes,
    sems,
):
    copies = [
        pltpu.make_async_copy(source, target, sems.at[number])
        for number, (source, target) in enumerate(
            ((occ_hbm, occ_ref), (g_hbm, g_ref), (x_hbm, x_ref))
        )
    ]
    for copy in copies:
        copy.start()
    me = me_ref[0]
    copies[0].wait()
    occupied = spread(occ_ref)
    copies[1].wait()
    copies[2].wait()
    for x in range(EDGE):
        both = []
        for brick in range(2):
            wide[brick, x * EDGE : (x + 1) * EDGE, :] = x_ref[brick, x].astype(F32)
            at = (2 * x + brick) * EDGE
            piece = g_ref[brick, x].astype(F32) * occupied[at : at + EDGE]
            wide[2 + brick, x * EDGE : (x + 1) * EDGE, :] = piece
            both.append(piece)
        masked_ref[x] = jnp.concatenate(both, axis=0).astype(BF16)
    for brick in range(2):
        first = face_values(wide, brick)
        second = face_values(wide, 2 + brick)
        packets = {}
        for key in first:
            packets[key] = jnp.concatenate([first[key], second[key]], axis=0).astype(BF16)
        for number, offset in enumerate(DIRECTIONS):
            boxes[send_place(nb_ref, me, brick, number)] = packets[face_kind(offset)]
    even_ref[...] = boxes[0:32].reshape(8, 4, 16, WIDE)
    odd_ref[...] = boxes[32:64].reshape(8, 4, 16, WIDE)


def beside(low, middle, high):
    return jnp.concatenate([low, middle, high], axis=1)


def fill_padded(padded, own, pick):
    def planes(along_x, along_y):
        return (
            pick((along_x, along_y, -1))[:, WIDE - 64 :],
            pick((along_x, along_y, 0)),
            pick((along_x, along_y, 1))[:, :64],
        )

    below, above = pick((0, 0, -1)), pick((0, 0, 1))
    for x in range(EDGE):
        lanes = slice(x * 64, (x + 1) * 64)
        start = (x + 1) * ROWS + 8
        padded[start : start + EDGE, :] = beside(below[:, lanes], own(x), above[:, lanes])
    for along_y, row in ((-1, 7), (1, 16)):
        value = beside(*planes(0, along_y))
        for x in range(EDGE):
            start = (x + 1) * ROWS + row
            padded[start : start + 1, :] = value[x : x + 1]
    for along_x, at in ((-1, 0), (1, 9)):
        start = at * ROWS + 8
        padded[start : start + EDGE, :] = beside(*planes(along_x, 0))
        for along_y, row, source in ((-1, 7, 7), (1, 16, 0)):
            value = beside(*planes(along_x, along_y))
            padded[at * ROWS + row : at * ROWS + row + 1, :] = value[source : source + 1]


def fill_windows(first, second, shifted, windows):
    for along_y in range(3):
        for x in range(10):
            start = x * ROWS + 7 + along_y
            shifted[along_y, x] = jnp.concatenate(
                [first[start : start + EDGE, :], second[start : start + EDGE, :]], axis=0
            ).astype(BF16)
    for pair in range(4):
        for along_x in range(3):
            for along_y in range(3):
                place = (3 * along_x + along_y) * 256
                windows[pair * 128 : (pair + 1) * 128, place : place + 256] = shifted[
                    along_y, along_x : along_x + EDGE, :, pair * 128 : pair * 128 + 256
                ].reshape(128, 256)


def fill_direct(kernel_ref, direct):
    for group in range(9):
        block = kernel_ref[group * 192 : (group + 1) * 192, :]
        none = jnp.zeros((64, 64), BF16)
        direct[group * 256 : (group + 1) * 256, :] = jnp.concatenate(
            [
                jnp.concatenate([block, none], axis=0),
                jnp.concatenate([none, block], axis=0),
            ],
            axis=1,
        )


def fill_flipped(kernel_ref, flipped):
    none = jnp.zeros((64, 64), BF16)
    for group in range(9):
        base = 3 * (8 - group)
        blocks = [kernel_ref[(base + z) * 64 : (base + z + 1) * 64, :] for z in (2, 1, 0)]
        lanes = slice(group * 256, (group + 1) * 256)
        flipped[0:64, lanes] = jnp.concatenate(blocks + [none], axis=1)
        flipped[64:128, lanes] = jnp.concatenate([none] + blocks, axis=1)


def times_flipped(windows, flipped):
    return lax.dot_general(
        windows, flipped, (((1,), (1,)), ((), ())), preferred_element_type=F32
    )


def paired(natural):
    return jnp.concatenate([natural[:, p * 128 : (p + 1) * 128] for p in range(4)], axis=0)


def unpaired(value):
    return jnp.concatenate([value[p * 128 : (p + 1) * 128] for p in range(4)], axis=1)


def gather_blocks(product):
    pieces = []
    for group in range(9):
        at = group * 256
        pieces.append(product[0:64, at : at + 192] + product[64:128, at + 64 : at + 256])
    pieces.append(jnp.zeros((64, PACKED - 27 * 64), F32))
    return jnp.concatenate(pieces, axis=1)


def main_kernel(
    me_ref,
    nb_ref,
    x_ref,
    masked_ref,
    occ_ref,
    even_in,
    odd_in,
    first_ref,
    second_ref,
    grads_ref,
    even_ref,
    odd_ref,
    padded,
    shifted,
    windows,
    direct,
    flipped,
    product,
    wide,
    boxes,
):
    me = me_ref[0]
    for brick in range(2):
        values = {}
        for number, offset in enumerate(DIRECTIONS):
            present, box, slot = locate(nb_ref, me, brick, number)
            place = slot * 2 + brick
            low = even_in[box & 7, place].astype(F32)
            high = odd_in[box & 7, place].astype(F32)
            values[offset] = jnp.where(present, jnp.where(box < 8, low, high), 0.0)

        def own_first(x):
            return x_ref[brick, x].astype(F32)

        def own_second(x):
            return masked_ref[x].astype(F32)[brick * EDGE : (brick + 1) * EDGE]

        fill_padded(padded.at[0, brick], own_first, lambda offset: values[offset][0:8])
        fill_padded(padded.at[1, brick], own_second, lambda offset: values[offset][8:16])
    for field in range(2):
        fill_windows(padded.at[field, 0], padded.at[field, 1], shifted.at[field], windows.at[field])
    fill_direct(first_ref, direct)
    fill_flipped(second_ref, flipped)
    occupied = paired(spread(occ_ref))
    pre_act = jnp.dot(windows[0], direct[...], preferred_element_type=F32)
    logistic = 1.0 / (1.0 + jnp.exp(-pre_act))
    hidden = (pre_act * logistic * occupied).astype(BF16)
    slope = logistic * (1.0 + pre_act * (1.0 - logistic))
    hidden_grad = times_flipped(windows[1], flipped[...])
    pre_grads = (hidden_grad * slope * occupied).astype(BF16)

    natural = unpaired(pre_grads.astype(F32))
    for x in range(EDGE):
        grads_ref[x] = natural[16 * x : 16 * x + 16].astype(BF16)
        for brick in range(2):
            at = 16 * x + EDGE * brick
            wide[brick, x * EDGE : (x + 1) * EDGE, :] = natural[at : at + EDGE]
    for brick in range(2):
        faces = face_values(wide, brick)
        for number, offset in enumerate(DIRECTIONS):
            boxes[send_place(nb_ref, me, brick, number)] = faces[face_kind(offset)]
    for box in range(8):
        even_ref[box, 0:32, :] = boxes[4 * box : 4 * box + 4].reshape(32, WIDE).astype(BF16)
        odd_ref[box] = boxes[32 + 4 * box : 36 + 4 * box].reshape(32, WIDE).astype(BF16)

    for half, own, field in ((0, hidden, 1), (1, pre_grads, 0)):
        turned = own.astype(F32).T.astype(BF16)
        product[...] = jnp.dot(turned, windows[field], preferred_element_type=F32)
        packed = gather_blocks(product).astype(BF16)
        for chunk in range(4):
            for part in range(4):
                at = 32 + 16 * part
                even_ref[4 * half + chunk, at : at + 16, :] = packed[
                    16 * chunk : 16 * chunk + 16, part * WIDE : (part + 1) * WIDE
                ]


def first_sum_kernel(parts_ref, pieces_ref):
    total = parts_ref[0, 32:96, :].astype(F32)
    for member in range(1, GROUP):
        total = total + parts_ref[member, 32:96, :].astype(F32)
    for member in range(GROUP):
        rows = total[EDGE * member : EDGE * member + EDGE]
        pieces_ref[member] = jnp.concatenate([rows[:, :256], rows[:, 256:]], axis=0).astype(BF16)


def next_sum_kernel(scaling, parts_ref, copies_ref):
    total = parts_ref[0].astype(F32)
    for member in range(1, parts_ref.shape[0]):
        total = total + parts_ref[member].astype(F32)
    total = total * scaling
    for member in range(copies_ref.shape[0]):
        copies_ref[member] = total.astype(copies_ref.dtype)


def share_kernel(pieces_ref, odd_ref, out_ref):
    rows = []
    for member in range(GROUP):
        piece = pieces_ref[member].astype(F32)
        rows.append(jnp.concatenate([piece[:EDGE], piece[EDGE:]], axis=1))
    chunk = jnp.concatenate(rows, axis=0).astype(BF16)
    for member in range(GROUP):
        out_ref[member, 0:32, :] = odd_ref[member]
        out_ref[member, 32:96, :] = chunk


def last_kernel(
    me_ref,
    nb_ref,
    grads_ref,
    occ_ref,
    even_in,
    odd_in,
    first_ref,
    out_ref,
    first_out,
    second_out,
    padded,
    shifted,
    windows,
    flipped,
    boxes,
):
    me = me_ref[0]
    for box in range(8):
        boxes[4 * box : 4 * box + 4] = (
            even_in[box, 0:32, :].astype(F32).reshape(4, EDGE, WIDE)
        )
        boxes[32 + 4 * box : 36 + 4 * box] = (
            odd_in[box, 0:32, :].astype(F32).reshape(4, EDGE, WIDE)
        )
    for brick in range(2):
        values = {}
        for number, offset in enumerate(DIRECTIONS):
            present, box, slot = locate(nb_ref, me, brick, number)
            values[offset] = jnp.where(present, boxes[4 * box + slot * 2 + brick], 0.0)

        def own(x):
            return grads_ref[x].astype(F32)[brick * EDGE : (brick + 1) * EDGE]

        fill_padded(padded.at[brick], own, lambda offset: values[offset])
    fill_windows(padded.at[0], padded.at[1], shifted, windows)
    fill_flipped(first_ref, flipped)
    result = unpaired(times_flipped(windows[...], flipped[...])) * spread(occ_ref)
    for x in range(EDGE):
        for brick in range(2):
            at = 16 * x + EDGE * brick
            out_ref[brick, x] = result[at : at + EDGE].astype(BF16)

    halves = []
    for half in range(2):
        rows = []
        for chunk in range(4 * half, 4 * half + 4):
            slot = (chunk + 4) & 7
            rows.append(
                jnp.concatenate(
                    [odd_in[slot, 32 + 16 * part : 48 + 16 * part, :] for part in range(4)],
                    axis=1,
                )
            )
        halves.append(jnp.concatenate(rows, axis=0).astype(F32))
    first_out[...] = halves[1][:, : 27 * 64]
    blocks = []
    for pair in range(14):
        turned = halves[0][:, pair * 128 : pair * 128 + 128].T
        blocks += [turned[0:64], turned[64:128]]
    second_out[...] = jnp.concatenate(blocks[26::-1], axis=1)


def call(kernel, shapes, scratch, arguments, scalars=0, outside=0, megabytes=40):
    specs = [pl.BlockSpec(memory_space=pltpu.SMEM)] * scalars
    specs += [pl.BlockSpec(memory_space=pl.ANY)] * outside
    specs += [pl.BlockSpec(memory_space=pltpu.VMEM)] * (len(arguments) - len(specs))
    return pl.pallas_call(
        kernel,
        out_shape=[jax.ShapeDtypeStruct(shape, kind) for shape, kind in shapes],
        in_specs=specs,
        out_specs=[pl.BlockSpec(memory_space=pltpu.VMEM)] * len(shapes),
        scratch_shapes=scratch,
        compiler_params=pltpu.CompilerParams(vmem_limit_bytes=megabytes * 2**20),
    )(*arguments)


def per_device(inputs, occupancy, neighbours, first_kernel, second_kernel, out_grads):
    devices = lax.axis_size("grp") * lax.axis_size("dev")
    members = devices // GROUP
    scaling = 1.0 / math.sqrt(inputs.shape[0] * devices * EDGE**3)
    even = [[GROUP * k + j for j in range(GROUP)] for k in range(members)]
    odd = [[(GROUP * k + 4 + j) % devices for j in range(GROUP)] for k in range(members)]
    quarters = lax.axis_size("dev") // GROUP
    strided = [
        [lax.axis_size("dev") * grp + GROUP * quarter + member for quarter in range(quarters)]
        for grp in range(lax.axis_size("grp"))
        for member in range(GROUP)
    ]
    me = (lax.axis_index("grp") * lax.axis_size("dev") + lax.axis_index("dev")).reshape(1)

    def swap(value, groups):
        return lax.all_to_all(value, AXES, 0, 0, axis_index_groups=groups, tiled=True)

    vmem = pltpu.VMEM
    halo = ((GROUP, 4, 16, WIDE), BF16)
    even_out, odd_out, masked = call(
        pack_kernel,
        [halo, halo, ((EDGE, 16, WIDE), BF16)],
        [
            vmem((2, EDGE, EDGE, WIDE), BF16),
            vmem((2, EDGE, EDGE, WIDE), BF16),
            vmem((2, EDGE, 64), jnp.int32),
            vmem((4, 64, WIDE), F32),
            vmem((64, 16, WIDE), BF16),
            pltpu.SemaphoreType.DMA((3,)),
        ],
        [me, neighbours, inputs, out_grads, occupancy],
        scalars=2,
        outside=3,
        megabytes=60,
    )
    even_in = swap(even_out, even)
    odd_in = swap(odd_out, odd)
    pre_grads, even_out, odd_out = call(
        main_kernel,
        [
            ((EDGE, 16, WIDE), BF16),
            ((GROUP, 96, WIDE), BF16),
            ((GROUP, 32, WIDE), BF16),
        ],
        [
            vmem((2, 2, 10 * ROWS, PADDED), F32),
            vmem((2, 3, 10, 16, PADDED), BF16),
            vmem((2, 512, 2304), BF16),
            vmem((2304, 128), BF16),
            vmem((128, 2304), BF16),
            vmem((128, 2304), F32),
            vmem((2, 64, WIDE), F32),
            vmem((64, EDGE, WIDE), F32),
        ],
        [me, neighbours, inputs, masked, occupancy, even_in, odd_in, first_kernel, second_kernel],
        scalars=2,
    )
    even_in = swap(even_out, even)
    piece = (16, 256)
    (pieces,) = call(first_sum_kernel, [((GROUP,) + piece, BF16)], [], [even_in])
    pieces = lax.all_to_all(pieces, "grp", 0, 0, tiled=True)
    (pieces,) = call(
        functools.partial(next_sum_kernel, 1.0), [((quarters,) + piece, BF16)], [], [pieces]
    )
    pieces = swap(pieces, strided)
    (pieces,) = call(
        functools.partial(next_sum_kernel, scaling), [((GROUP,) + piece, BF16)], [], [pieces]
    )
    pieces = lax.all_to_all(pieces, "grp", 0, 0, tiled=True)
    (odd_out,) = call(share_kernel, [((GROUP, 96, WIDE), BF16)], [], [pieces, odd_out])
    odd_in = swap(odd_out, odd)
    input_grads, first_grads, second_grads = call(
        last_kernel,
        [
            ((2, EDGE, EDGE, WIDE), BF16),
            ((64, 27 * 64), F32),
            ((64, 27 * 64), F32),
        ],
        [
            vmem((2, 10 * ROWS, PADDED), F32),
            vmem((3, 10, 16, PADDED), BF16),
            vmem((512, 2304), BF16),
            vmem((128, 2304), BF16),
            vmem((64, EDGE, WIDE), F32),
        ],
        [me, neighbours, pre_grads, occupancy, even_in, odd_in, first_kernel],
        scalars=2,
    )
    return input_grads, first_grads.T, second_grads.T


def solution(mesh):
    in_specs = (
        P(("grp", "dev"), None, None, None),
        P(("grp", "dev"), None, None),
        P(("grp", "dev"), None),
        P(),
        P(),
        P(("grp", "dev"), None, None, None),
    )
    out_specs = (P(("grp", "dev"), None, None, None), P(), P())
    return jax.shard_map(
        per_device, mesh=mesh, in_specs=in_specs, out_specs=out_specs, check_vma=False
    )
```

```python
import functools
import math

import jax
import jax.numpy as jnp
from jax import lax
from jax.experimental import pallas as pl
from jax.experimental.pallas import tpu as pltpu
from jax.sharding import PartitionSpec as P

AXES = ("grp", "dev")
EDGE = 8
WIDE = 512
PADDED = 640
ROWS = 24
PACKED = 2048
BF16 = jnp.bfloat16
F32 = jnp.float32


def directions():
    result = []
    for along_x in (-1, 0, 1):
        for along_y in (-1, 0, 1):
            for along_z in (-1, 0, 1):
                if along_x != 0 or along_y != 0 or along_z != 0:
                    result.append((along_x, along_y, along_z))
    return result


DIRECTIONS = directions()
NUMBER = {offset: number for number, offset in enumerate(DIRECTIONS)}


def locate(nb_ref, me, brick, number):
    other = nb_ref[brick, number]
    present = other >= 0
    owner = jnp.maximum(other, 0) >> 1
    return present, owner & 3, (owner >> 2) - (me >> 2), owner == me, other & 1


def send_place(nb_ref, me, brick, number):
    present, member, up, own, slot = locate(nb_ref, me, brick, number)
    relayed = (up > 0) | ((up < 0) & (member != (me & 3)))
    place = jnp.where(own, 32, member * 8 + jnp.where(relayed, 4, 0))
    return jnp.where(present, place + brick * 2 + slot, 32)


def take_place(nb_ref, me, brick, number):
    present, member, up, own, slot = locate(nb_ref, me, brick, number)
    place = member * 4 + jnp.where(up == 0, 0, jnp.where(up < 0, 16, 32))
    return present, jnp.where(own, 48, place) + slot * 2 + brick


def face_kind(offset):
    for axis in range(3):
        if offset[axis] != 0:
            return axis, 1 if offset[axis] > 0 else 0


def face_values(wide, index):
    faces = {}
    for side, at in ((0, 0), (1, EDGE - 1)):
        faces[0, side] = wide[index, at * EDGE : (at + 1) * EDGE, :]
        faces[1, side] = jnp.concatenate(
            [wide[index, x * EDGE + at : x * EDGE + at + 1, :] for x in range(EDGE)], axis=0
        )
        faces[2, side] = jnp.concatenate(
            [
                wide[index, x * EDGE : (x + 1) * EDGE, at * 64 : (at + 1) * 64]
                for x in range(EDGE)
            ],
            axis=1,
        )
    return faces


def spread(occ_ref):
    rows = []
    for x in range(EDGE):
        for brick in range(2):
            rows.append(jnp.broadcast_to(occ_ref[brick, x : x + 1, :].astype(F32), (EDGE, 64)))
    stacked = jnp.concatenate(rows, axis=0)
    row = lax.broadcasted_iota(jnp.int32, stacked.shape, 0)
    lane = lax.broadcasted_iota(jnp.int32, stacked.shape, 1)
    own = jnp.where((row & 7) == (lane >> 3), stacked, 0.0).astype(BF16)
    source = lax.broadcasted_iota(jnp.int32, (64, WIDE), 0)
    target = lax.broadcasted_iota(jnp.int32, (64, WIDE), 1)
    select = jnp.where((source & 7) == (target >> 6), 1.0, 0.0).astype(BF16)
    return jnp.dot(own, select, preferred_element_type=F32)


def pack_kernel(
    me_ref,
    nb_ref,
    x_hbm,
    g_hbm,
    occ_hbm,
    near_ref,
    kept_ref,
    masked_ref,
    x_ref,
    g_ref,
    occ_ref,
    wide,
    boxes,
    sems,
):
    copies = [
        pltpu.make_async_copy(source, target, sems.at[number])
        for number, (source, target) in enumerate(
            ((occ_hbm, occ_ref), (g_hbm, g_ref), (x_hbm, x_ref))
        )
    ]
    for copy in copies:
        copy.start()
    me = me_ref[0]
    copies[0].wait()
    occupied = spread(occ_ref)
    copies[1].wait()
    copies[2].wait()
    for x in range(EDGE):
        both = []
        for brick in range(2):
            wide[brick, x * EDGE : (x + 1) * EDGE, :] = x_ref[brick, x].astype(F32)
            at = (2 * x + brick) * EDGE
            piece = g_ref[brick, x].astype(F32) * occupied[at : at + EDGE]
            wide[2 + brick, x * EDGE : (x + 1) * EDGE, :] = piece
            both.append(piece)
        masked_ref[x] = jnp.concatenate(both, axis=0).astype(BF16)
    for brick in range(2):
        first = face_values(wide, brick)
        second = face_values(wide, 2 + brick)
        packets = {}
        for key in first:
            packets[key] = jnp.concatenate([first[key], second[key]], axis=0).astype(BF16)
        for number, offset in enumerate(DIRECTIONS):
            boxes[send_place(nb_ref, me, brick, number)] = packets[face_kind(offset)]
    near_ref[...] = boxes[0:32].reshape(4, 128, WIDE)
    kept_ref[...] = boxes[32:36]


def route_kernel(me_ref, near_ref, above_ref, below_ref):
    size = above_ref.shape[1]
    own = me_ref[0] & 3
    above_ref[...] = near_ref[:, size : 2 * size, :]
    below_ref[...] = near_ref[:, size : 2 * size, :]
    below_ref[own] = near_ref[own, 0:size, :]


def beside(low, middle, high):
    return jnp.concatenate([low, middle, high], axis=1)


def fill_padded(padded, own, pick):
    def planes(along_x, along_y):
        return (
            pick((along_x, along_y, -1))[:, WIDE - 64 :],
            pick((along_x, along_y, 0)),
            pick((along_x, along_y, 1))[:, :64],
        )

    below, above = pick((0, 0, -1)), pick((0, 0, 1))
    for x in range(EDGE):
        lanes = slice(x * 64, (x + 1) * 64)
        start = (x + 1) * ROWS + 8
        padded[start : start + EDGE, :] = beside(below[:, lanes], own(x), above[:, lanes])
    for along_y, row in ((-1, 7), (1, 16)):
        value = beside(*planes(0, along_y))
        for x in range(EDGE):
            start = (x + 1) * ROWS + row
            padded[start : start + 1, :] = value[x : x + 1]
    for along_x, at in ((-1, 0), (1, 9)):
        start = at * ROWS + 8
        padded[start : start + EDGE, :] = beside(*planes(along_x, 0))
        for along_y, row, source in ((-1, 7, 7), (1, 16, 0)):
            value = beside(*planes(along_x, along_y))
            padded[at * ROWS + row : at * ROWS + row + 1, :] = value[source : source + 1]


def fill_windows(first, second, shifted, windows):
    for along_y in range(3):
        for x in range(10):
            start = x * ROWS + 7 + along_y
            shifted[along_y, x] = jnp.concatenate(
                [first[start : start + EDGE, :], second[start : start + EDGE, :]], axis=0
            ).astype(BF16)
    for pair in range(4):
        for along_x in range(3):
            for along_y in range(3):
                place = (3 * along_x + along_y) * 256
                windows[pair * 128 : (pair + 1) * 128, place : place + 256] = shifted[
                    along_y, along_x : along_x + EDGE, :, pair * 128 : pair * 128 + 256
                ].reshape(128, 256)


def fill_direct(kernel_ref, direct):
    for group in range(9):
        block = kernel_ref[group * 192 : (group + 1) * 192, :]
        none = jnp.zeros((64, 64), BF16)
        direct[group * 256 : (group + 1) * 256, :] = jnp.concatenate(
            [
                jnp.concatenate([block, none], axis=0),
                jnp.concatenate([none, block], axis=0),
            ],
            axis=1,
        )


def fill_flipped(kernel_ref, flipped):
    none = jnp.zeros((64, 64), BF16)
    for group in range(9):
        base = 3 * (8 - group)
        blocks = [kernel_ref[(base + z) * 64 : (base + z + 1) * 64, :] for z in (2, 1, 0)]
        lanes = slice(group * 256, (group + 1) * 256)
        flipped[0:64, lanes] = jnp.concatenate(blocks + [none], axis=1)
        flipped[64:128, lanes] = jnp.concatenate([none] + blocks, axis=1)


def times_flipped(windows, flipped):
    return lax.dot_general(
        windows, flipped, (((1,), (1,)), ((), ())), preferred_element_type=F32
    )


def paired(natural):
    return jnp.concatenate([natural[:, p * 128 : (p + 1) * 128] for p in range(4)], axis=0)


def unpaired(value):
    return jnp.concatenate([value[p * 128 : (p + 1) * 128] for p in range(4)], axis=1)


def gather_blocks(product):
    pieces = []
    for group in range(9):
        at = group * 256
        pieces.append(product[0:64, at : at + 192] + product[64:128, at + 64 : at + 256])
    pieces.append(jnp.zeros((64, PACKED - 27 * 64), F32))
    return jnp.concatenate(pieces, axis=1)


def main_kernel(
    me_ref,
    nb_ref,
    x_ref,
    masked_ref,
    occ_ref,
    near_ref,
    below_ref,
    above_ref,
    kept_in,
    first_ref,
    second_ref,
    grads_ref,
    out_ref,
    kept_ref,
    taken,
    padded,
    shifted,
    windows,
    direct,
    flipped,
    product,
    wide,
    boxes,
):
    me = me_ref[0]
    for member in range(4):
        at = 4 * member
        taken[at : at + 4] = near_ref[member, 0:64, :].reshape(4, 16, WIDE)
        taken[at + 16 : at + 20] = below_ref[member].reshape(4, 16, WIDE)
        taken[at + 32 : at + 36] = above_ref[member].reshape(4, 16, WIDE)
    taken[48:52] = kept_in[...]
    for brick in range(2):
        values = {}
        for number, offset in enumerate(DIRECTIONS):
            present, place = take_place(nb_ref, me, brick, number)
            values[offset] = jnp.where(present, taken[place].astype(F32), 0.0)

        def own_first(x):
            return x_ref[brick, x].astype(F32)

        def own_second(x):
            return masked_ref[x].astype(F32)[brick * EDGE : (brick + 1) * EDGE]

        fill_padded(padded.at[0, brick], own_first, lambda offset: values[offset][0:8])
        fill_padded(padded.at[1, brick], own_second, lambda offset: values[offset][8:16])
    for field in range(2):
        fill_windows(padded.at[field, 0], padded.at[field, 1], shifted.at[field], windows.at[field])
    fill_direct(first_ref, direct)
    fill_flipped(second_ref, flipped)
    occupied = paired(spread(occ_ref))
    pre_act = jnp.dot(windows[0], direct[...], preferred_element_type=F32)
    logistic = 1.0 / (1.0 + jnp.exp(-pre_act))
    hidden = (pre_act * logistic * occupied).astype(BF16)
    slope = logistic * (1.0 + pre_act * (1.0 - logistic))
    hidden_grad = times_flipped(windows[1], flipped[...])
    pre_grads = (hidden_grad * slope * occupied).astype(BF16)

    natural = unpaired(pre_grads.astype(F32))
    for x in range(EDGE):
        grads_ref[x] = natural[16 * x : 16 * x + 16].astype(BF16)
        for brick in range(2):
            at = 16 * x + EDGE * brick
            wide[brick, x * EDGE : (x + 1) * EDGE, :] = natural[at : at + EDGE]
    for brick in range(2):
        faces = face_values(wide, brick)
        for number, offset in enumerate(DIRECTIONS):
            boxes[send_place(nb_ref, me, brick, number)] = faces[face_kind(offset)]
    for member in range(4):
        out_ref[member, 0:64, :] = (
            boxes[8 * member : 8 * member + 8].reshape(64, WIDE).astype(BF16)
        )
    kept_ref[...] = boxes[32:36]

    for half, own, field in ((0, hidden, 1), (1, pre_grads, 0)):
        turned = own.astype(F32).T.astype(BF16)
        product[...] = jnp.dot(turned, windows[field], preferred_element_type=F32)
        packed = gather_blocks(product).astype(BF16)
        for chunk in range(2):
            for part in range(4):
                at = 64 + 32 * part
                out_ref[2 * half + chunk, at : at + 32, :] = packed[
                    32 * chunk : 32 * chunk + 32, part * WIDE : (part + 1) * WIDE
                ]


def first_sum_kernel(parts_ref, pieces_ref):
    total = parts_ref[0, 64:192, :].astype(F32)
    for member in range(1, 4):
        total = total + parts_ref[member, 64:192, :].astype(F32)
    pieces_ref[...] = total.astype(BF16).reshape(pieces_ref.shape)


def next_sum_kernel(scaling, arrived_ref, parts_ref, copies_ref):
    del arrived_ref
    total = parts_ref[0].astype(F32)
    for member in range(1, parts_ref.shape[0]):
        total = total + parts_ref[member].astype(F32)
    total = total * scaling
    for member in range(copies_ref.shape[0]):
        copies_ref[member] = total.astype(copies_ref.dtype)


def share_kernel(pieces_ref, copies_ref):
    chunk = pieces_ref[...].reshape(128, WIDE)
    for member in range(4):
        copies_ref[member] = chunk


def input_grads_kernel(
    me_ref,
    nb_ref,
    grads_ref,
    occ_ref,
    near_ref,
    below_ref,
    above_ref,
    kept_ref,
    first_ref,
    out_ref,
    taken,
    padded,
    shifted,
    windows,
    flipped,
):
    me = me_ref[0]
    for member in range(4):
        at = 4 * member
        taken[at : at + 4] = near_ref[member, 0:32, :].astype(F32).reshape(4, EDGE, WIDE)
        taken[at + 16 : at + 20] = below_ref[member].astype(F32).reshape(4, EDGE, WIDE)
        taken[at + 32 : at + 36] = above_ref[member].astype(F32).reshape(4, EDGE, WIDE)
    taken[48:52] = kept_ref[...]
    for brick in range(2):
        values = {}
        for number, offset in enumerate(DIRECTIONS):
            present, place = take_place(nb_ref, me, brick, number)
            values[offset] = jnp.where(present, taken[place], 0.0)

        def own(x):
            return grads_ref[x].astype(F32)[brick * EDGE : (brick + 1) * EDGE]

        fill_padded(padded.at[brick], own, lambda offset: values[offset])
    fill_windows(padded.at[0], padded.at[1], shifted, windows)
    fill_flipped(first_ref, flipped)
    result = unpaired(times_flipped(windows[...], flipped[...])) * spread(occ_ref)
    for x in range(EDGE):
        for brick in range(2):
            at = 16 * x + EDGE * brick
            out_ref[brick, x] = result[at : at + EDGE].astype(BF16)


def unpack_kernel(parts_ref, first_out, second_out):
    halves = []
    for half in range(2):
        rows = []
        for chunk in (2 * half, 2 * half + 1):
            rows.append(
                jnp.concatenate(
                    [parts_ref[chunk, 32 * part : 32 * part + 32, :] for part in range(4)],
                    axis=1,
                )
            )
        halves.append(jnp.concatenate(rows, axis=0).astype(F32))
    first_out[...] = halves[1][:, : 27 * 64]
    blocks = []
    for pair in range(14):
        turned = halves[0][:, pair * 128 : pair * 128 + 128].T
        blocks += [turned[0:64], turned[64:128]]
    second_out[...] = jnp.concatenate(blocks[26::-1], axis=1)


def call(kernel, shapes, scratch, arguments, scalars=0, outside=0, megabytes=40, flops=0):
    specs = [pl.BlockSpec(memory_space=pltpu.SMEM)] * scalars
    specs += [pl.BlockSpec(memory_space=pl.ANY)] * outside
    specs += [pl.BlockSpec(memory_space=pltpu.VMEM)] * (len(arguments) - len(specs))
    return pl.pallas_call(
        kernel,
        out_shape=[jax.ShapeDtypeStruct(shape, kind) for shape, kind in shapes],
        in_specs=specs,
        out_specs=[pl.BlockSpec(memory_space=pltpu.VMEM)] * len(shapes),
        scratch_shapes=scratch,
        cost_estimate=pl.CostEstimate(flops=flops, bytes_accessed=2**19, transcendentals=0),
        compiler_params=pltpu.CompilerParams(vmem_limit_bytes=megabytes * 2**20),
    )(*arguments)


def per_device(inputs, occupancy, neighbours, first_kernel, second_kernel, out_grads):
    along_grp, along_dev = lax.axis_size("grp"), lax.axis_size("dev")
    devices = along_grp * along_dev
    scaling = 1.0 / math.sqrt(inputs.shape[0] * devices * EDGE**3)
    fours = [[4 * row + member for member in range(4)] for row in range(devices // 4)]
    rows = along_dev // 4
    stacks = [
        [along_dev * grp + 4 * row + member for row in range(rows)]
        for grp in range(along_grp)
        for member in range(4)
    ]
    me = (lax.axis_index("grp") * along_dev + lax.axis_index("dev")).reshape(1)
    vmem = pltpu.VMEM

    def swap(value, members):
        return lax.all_to_all(value, AXES, 0, 0, axis_index_groups=members, tiled=True)

    def send_on(near, size):
        packets = ((4, size, WIDE), BF16)
        above, below = call(route_kernel, [packets, packets], [], [me, near], scalars=1)
        from_below = lax.ppermute(above, AXES, [(i, i + 4) for i in range(devices - 4)])
        from_above = lax.ppermute(below, AXES, [(i + 4, i) for i in range(devices - 4)])
        return from_below, from_above

    near, kept, masked = call(
        pack_kernel,
        [((4, 128, WIDE), BF16), ((4, 16, WIDE), BF16), ((EDGE, 16, WIDE), BF16)],
        [
            vmem((2, EDGE, EDGE, WIDE), BF16),
            vmem((2, EDGE, EDGE, WIDE), BF16),
            vmem((2, EDGE, 64), jnp.int32),
            vmem((4, 64, WIDE), F32),
            vmem((36, 16, WIDE), BF16),
            pltpu.SemaphoreType.DMA((3,)),
        ],
        [me, neighbours, inputs, out_grads, occupancy],
        scalars=2,
        outside=3,
        megabytes=60,
    )
    near = swap(near, fours)
    below, above = send_on(near, 64)
    pre_grads, near, kept = call(
        main_kernel,
        [((EDGE, 16, WIDE), BF16), ((4, 192, WIDE), BF16), ((4, EDGE, WIDE), F32)],
        [
            vmem((52, 16, WIDE), BF16),
            vmem((2, 2, 10 * ROWS, PADDED), F32),
            vmem((2, 3, 10, 16, PADDED), BF16),
            vmem((2, 512, 2304), BF16),
            vmem((2304, 128), BF16),
            vmem((128, 2304), BF16),
            vmem((128, 2304), F32),
            vmem((2, 64, WIDE), F32),
            vmem((36, EDGE, WIDE), F32),
        ],
        [
            me,
            neighbours,
            inputs,
            masked,
            occupancy,
            near,
            below,
            above,
            kept,
            first_kernel,
            second_kernel,
        ],
        scalars=2,
        flops=2**30,
    )
    near = swap(near, fours)
    below, above = send_on(near, 32)
    piece = (128 // along_grp, WIDE)
    (sums,) = call(first_sum_kernel, [((along_grp,) + piece, BF16)], [], [near])
    sums = lax.all_to_all(sums, "grp", 0, 0, tiled=True)
    (sums,) = call(
        functools.partial(next_sum_kernel, 1.0),
        [((rows,) + piece, BF16)],
        [],
        [below, sums],
        outside=1,
    )
    sums = swap(sums, stacks)
    (sums,) = call(
        functools.partial(next_sum_kernel, scaling),
        [((along_grp,) + piece, BF16)],
        [],
        [above, sums],
        outside=1,
    )
    sums = lax.all_to_all(sums, "grp", 0, 0, tiled=True)
    (sums,) = call(share_kernel, [((4, 128, WIDE), BF16)], [], [sums])
    sums = swap(sums, fours)
    (input_grads,) = call(
        input_grads_kernel,
        [((2, EDGE, EDGE, WIDE), BF16)],
        [
            vmem((52, EDGE, WIDE), F32),
            vmem((2, 10 * ROWS, PADDED), F32),
            vmem((3, 10, 16, PADDED), BF16),
            vmem((512, 2304), BF16),
            vmem((128, 2304), BF16),
        ],
        [me, neighbours, pre_grads, occupancy, near, below, above, kept, first_kernel],
        scalars=2,
        flops=2**28,
    )
    first_grads, second_grads = call(
        unpack_kernel, [((64, 27 * 64), F32), ((64, 27 * 64), F32)], [], [sums]
    )
    return input_grads, first_grads.T, second_grads.T


def solution(mesh):
    in_specs = (
        P(("grp", "dev"), None, None, None),
        P(("grp", "dev"), None, None),
        P(("grp", "dev"), None),
        P(),
        P(),
        P(("grp", "dev"), None, None, None),
    )
    out_specs = (P(("grp", "dev"), None, None, None), P(), P())
    return jax.shard_map(
        per_device, mesh=mesh, in_specs=in_specs, out_specs=out_specs, check_vma=False
    )
```

```python
import functools
import math

import jax
import jax.numpy as jnp
from jax import lax
from jax.experimental import pallas as pl
from jax.experimental.pallas import tpu as pltpu
from jax.sharding import PartitionSpec as P

AXES = ("grp", "dev")
EDGE = 8
WIDE = 512
PADDED = 640
ROWS = 24
PACKED = 2048
BF16 = jnp.bfloat16
F32 = jnp.float32


def directions():
    result = []
    for along_x in (-1, 0, 1):
        for along_y in (-1, 0, 1):
            for along_z in (-1, 0, 1):
                if along_x != 0 or along_y != 0 or along_z != 0:
                    result.append((along_x, along_y, along_z))
    return result


DIRECTIONS = directions()
NUMBER = {offset: number for number, offset in enumerate(DIRECTIONS)}


def locate(nb_ref, me, brick, number):
    other = nb_ref[brick, number]
    present = other >= 0
    owner = jnp.maximum(other, 0) >> 1
    return present, owner & 3, (owner >> 2) - (me >> 2), owner == me, other & 1


def send_place(nb_ref, me, brick, number):
    present, member, up, own, slot = locate(nb_ref, me, brick, number)
    relayed = (up > 0) | ((up < 0) & (member != (me & 3)))
    place = jnp.where(own, 32, member * 8 + jnp.where(relayed, 4, 0))
    return jnp.where(present, place + brick * 2 + slot, 32)


def take_place(nb_ref, me, brick, number):
    present, member, up, own, slot = locate(nb_ref, me, brick, number)
    place = member * 4 + jnp.where(up == 0, 0, jnp.where(up < 0, 16, 32))
    return present, jnp.where(own, 48, place) + slot * 2 + brick


def face_kind(offset):
    for axis in range(3):
        if offset[axis] != 0:
            return axis, 1 if offset[axis] > 0 else 0


def face_values(wide, index):
    faces = {}
    for side, at in ((0, 0), (1, EDGE - 1)):
        faces[0, side] = wide[index, at * EDGE : (at + 1) * EDGE, :]
        faces[1, side] = jnp.concatenate(
            [wide[index, x * EDGE + at : x * EDGE + at + 1, :] for x in range(EDGE)], axis=0
        )
        faces[2, side] = jnp.concatenate(
            [
                wide[index, x * EDGE : (x + 1) * EDGE, at * 64 : (at + 1) * 64]
                for x in range(EDGE)
            ],
            axis=1,
        )
    return faces


def spread(occ_ref):
    rows = []
    for x in range(EDGE):
        for brick in range(2):
            rows.append(jnp.broadcast_to(occ_ref[brick, x : x + 1, :].astype(F32), (EDGE, 64)))
    stacked = jnp.concatenate(rows, axis=0)
    row = lax.broadcasted_iota(jnp.int32, stacked.shape, 0)
    lane = lax.broadcasted_iota(jnp.int32, stacked.shape, 1)
    own = jnp.where((row & 7) == (lane >> 3), stacked, 0.0).astype(BF16)
    source = lax.broadcasted_iota(jnp.int32, (64, WIDE), 0)
    target = lax.broadcasted_iota(jnp.int32, (64, WIDE), 1)
    select = jnp.where((source & 7) == (target >> 6), 1.0, 0.0).astype(BF16)
    return jnp.dot(own, select, preferred_element_type=F32)


def pack_kernel(
    me_ref,
    nb_ref,
    x_hbm,
    g_hbm,
    occ_hbm,
    near_ref,
    kept_ref,
    masked_ref,
    x_ref,
    g_ref,
    occ_ref,
    wide,
    boxes,
    sems,
):
    copies = [
        pltpu.make_async_copy(source, target, sems.at[number])
        for number, (source, target) in enumerate(
            ((occ_hbm, occ_ref), (g_hbm, g_ref), (x_hbm, x_ref))
        )
    ]
    for copy in copies:
        copy.start()
    me = me_ref[0]
    copies[0].wait()
    occupied = spread(occ_ref)
    copies[1].wait()
    copies[2].wait()
    for x in range(EDGE):
        both = []
        for brick in range(2):
            wide[brick, x * EDGE : (x + 1) * EDGE, :] = x_ref[brick, x].astype(F32)
            at = (2 * x + brick) * EDGE
            piece = g_ref[brick, x].astype(F32) * occupied[at : at + EDGE]
            wide[2 + brick, x * EDGE : (x + 1) * EDGE, :] = piece
            both.append(piece)
        masked_ref[x] = jnp.concatenate(both, axis=0).astype(BF16)
    for brick in range(2):
        first = face_values(wide, brick)
        second = face_values(wide, 2 + brick)
        packets = {}
        for key in first:
            packets[key] = jnp.concatenate([first[key], second[key]], axis=0).astype(BF16)
        for number, offset in enumerate(DIRECTIONS):
            boxes[send_place(nb_ref, me, brick, number)] = packets[face_kind(offset)]
    near_ref[...] = boxes[0:32].reshape(4, 128, WIDE)
    kept_ref[...] = boxes[32:36]


def route_kernel(me_ref, near_ref, above_ref, below_ref):
    size = above_ref.shape[1]
    own = me_ref[0] & 3
    above_ref[...] = near_ref[:, size : 2 * size, :]
    below_ref[...] = near_ref[:, size : 2 * size, :]
    below_ref[own] = near_ref[own, 0:size, :]


def beside(low, middle, high):
    return jnp.concatenate([low, middle, high], axis=1)


def fill_padded(padded, own, pick):
    def planes(along_x, along_y):
        return (
            pick((along_x, along_y, -1))[:, WIDE - 64 :],
            pick((along_x, along_y, 0)),
            pick((along_x, along_y, 1))[:, :64],
        )

    below, above = pick((0, 0, -1)), pick((0, 0, 1))
    for x in range(EDGE):
        lanes = slice(x * 64, (x + 1) * 64)
        start = (x + 1) * ROWS + 8
        padded[start : start + EDGE, :] = beside(below[:, lanes], own(x), above[:, lanes])
    for along_y, row in ((-1, 7), (1, 16)):
        value = beside(*planes(0, along_y))
        for x in range(EDGE):
            start = (x + 1) * ROWS + row
            padded[start : start + 1, :] = value[x : x + 1]
    for along_x, at in ((-1, 0), (1, 9)):
        start = at * ROWS + 8
        padded[start : start + EDGE, :] = beside(*planes(along_x, 0))
        for along_y, row, source in ((-1, 7, 7), (1, 16, 0)):
            value = beside(*planes(along_x, along_y))
            padded[at * ROWS + row : at * ROWS + row + 1, :] = value[source : source + 1]


def fill_windows(first, second, shifted, windows):
    for along_y in range(3):
        for x in range(10):
            start = x * ROWS + 7 + along_y
            shifted[along_y, x] = jnp.concatenate(
                [first[start : start + EDGE, :], second[start : start + EDGE, :]], axis=0
            ).astype(BF16)
    for pair in range(4):
        for along_x in range(3):
            for along_y in range(3):
                place = (3 * along_x + along_y) * 256
                windows[pair * 128 : (pair + 1) * 128, place : place + 256] = shifted[
                    along_y, along_x : along_x + EDGE, :, pair * 128 : pair * 128 + 256
                ].reshape(128, 256)


def fill_direct(kernel_ref, direct):
    for group in range(9):
        block = kernel_ref[group * 192 : (group + 1) * 192, :]
        none = jnp.zeros((64, 64), BF16)
        direct[group * 256 : (group + 1) * 256, :] = jnp.concatenate(
            [
                jnp.concatenate([block, none], axis=0),
                jnp.concatenate([none, block], axis=0),
            ],
            axis=1,
        )


def fill_flipped(kernel_ref, flipped):
    none = jnp.zeros((64, 64), BF16)
    for group in range(9):
        base = 3 * (8 - group)
        blocks = [kernel_ref[(base + z) * 64 : (base + z + 1) * 64, :] for z in (2, 1, 0)]
        lanes = slice(group * 256, (group + 1) * 256)
        flipped[0:64, lanes] = jnp.concatenate(blocks + [none], axis=1)
        flipped[64:128, lanes] = jnp.concatenate([none] + blocks, axis=1)


def times_flipped(windows, flipped):
    return lax.dot_general(
        windows, flipped, (((1,), (1,)), ((), ())), preferred_element_type=F32
    )


def paired(natural):
    return jnp.concatenate([natural[:, p * 128 : (p + 1) * 128] for p in range(4)], axis=0)


def unpaired(value):
    return jnp.concatenate([value[p * 128 : (p + 1) * 128] for p in range(4)], axis=1)


def gather_blocks(product):
    pieces = []
    for group in range(9):
        at = group * 256
        pieces.append(product[0:64, at : at + 192] + product[64:128, at + 64 : at + 256])
    pieces.append(jnp.zeros((64, PACKED - 27 * 64), F32))
    return jnp.concatenate(pieces, axis=1)


def main_kernel(
    me_ref,
    nb_ref,
    x_ref,
    masked_ref,
    occ_ref,
    near_ref,
    below_ref,
    above_ref,
    kept_in,
    first_ref,
    second_ref,
    grads_ref,
    out_ref,
    kept_ref,
    taken,
    padded,
    shifted,
    windows,
    direct,
    flipped,
    product,
    wide,
    boxes,
):
    me = me_ref[0]
    for member in range(4):
        at = 4 * member
        taken[at : at + 4] = near_ref[member, 0:64, :].reshape(4, 16, WIDE)
        taken[at + 16 : at + 20] = below_ref[member].reshape(4, 16, WIDE)
        taken[at + 32 : at + 36] = above_ref[member].reshape(4, 16, WIDE)
    taken[48:52] = kept_in[...]
    for brick in range(2):
        values = {}
        for number, offset in enumerate(DIRECTIONS):
            present, place = take_place(nb_ref, me, brick, number)
            values[offset] = jnp.where(present, taken[place].astype(F32), 0.0)

        def own_first(x):
            return x_ref[brick, x].astype(F32)

        def own_second(x):
            return masked_ref[x].astype(F32)[brick * EDGE : (brick + 1) * EDGE]

        fill_padded(padded.at[0, brick], own_first, lambda offset: values[offset][0:8])
        fill_padded(padded.at[1, brick], own_second, lambda offset: values[offset][8:16])
    for field in range(2):
        fill_windows(padded.at[field, 0], padded.at[field, 1], shifted.at[field], windows.at[field])
    fill_direct(first_ref, direct)
    fill_flipped(second_ref, flipped)
    occupied = paired(spread(occ_ref))
    pre_act = jnp.dot(windows[0], direct[...], preferred_element_type=F32)
    logistic = 1.0 / (1.0 + jnp.exp(-pre_act))
    hidden = (pre_act * logistic * occupied).astype(BF16)
    slope = logistic * (1.0 + pre_act * (1.0 - logistic))
    hidden_grad = times_flipped(windows[1], flipped[...])
    pre_grads = (hidden_grad * slope * occupied).astype(BF16)

    natural = unpaired(pre_grads.astype(F32))
    for x in range(EDGE):
        grads_ref[x] = natural[16 * x : 16 * x + 16].astype(BF16)
        for brick in range(2):
            at = 16 * x + EDGE * brick
            wide[brick, x * EDGE : (x + 1) * EDGE, :] = natural[at : at + EDGE]
    for brick in range(2):
        faces = face_values(wide, brick)
        for number, offset in enumerate(DIRECTIONS):
            boxes[send_place(nb_ref, me, brick, number)] = faces[face_kind(offset)]
    for member in range(4):
        out_ref[member, 0:64, :] = (
            boxes[8 * member : 8 * member + 8].reshape(64, WIDE).astype(BF16)
        )
    kept_ref[...] = boxes[32:36]

    for half, own, field in ((0, hidden, 1), (1, pre_grads, 0)):
        turned = own.astype(F32).T.astype(BF16)
        product[...] = jnp.dot(turned, windows[field], preferred_element_type=F32)
        packed = gather_blocks(product).astype(BF16)
        for chunk in range(2):
            for part in range(4):
                at = 64 + 32 * part
                out_ref[2 * half + chunk, at : at + 32, :] = packed[
                    32 * chunk : 32 * chunk + 32, part * WIDE : (part + 1) * WIDE
                ]


def first_sum_kernel(parts_ref, pieces_ref):
    total = parts_ref[0, 64:192, :].astype(F32)
    for member in range(1, 4):
        total = total + parts_ref[member, 64:192, :].astype(F32)
    pieces_ref[...] = total.astype(BF16).reshape(pieces_ref.shape)


def next_sum_kernel(scaling, parts_ref, copies_ref):
    total = parts_ref[0].astype(F32)
    for member in range(1, parts_ref.shape[0]):
        total = total + parts_ref[member].astype(F32)
    total = total * scaling
    for member in range(copies_ref.shape[0]):
        copies_ref[member] = total.astype(copies_ref.dtype)


def input_grads_kernel(
    me_ref,
    nb_ref,
    grads_ref,
    occ_ref,
    near_ref,
    below_ref,
    above_ref,
    kept_ref,
    first_ref,
    out_ref,
    taken,
    padded,
    shifted,
    windows,
    flipped,
):
    me = me_ref[0]
    for member in range(4):
        at = 4 * member
        taken[at : at + 4] = near_ref[member, 0:32, :].astype(F32).reshape(4, EDGE, WIDE)
        taken[at + 16 : at + 20] = below_ref[member].astype(F32).reshape(4, EDGE, WIDE)
        taken[at + 32 : at + 36] = above_ref[member].astype(F32).reshape(4, EDGE, WIDE)
    taken[48:52] = kept_ref[...]
    for brick in range(2):
        values = {}
        for number, offset in enumerate(DIRECTIONS):
            present, place = take_place(nb_ref, me, brick, number)
            values[offset] = jnp.where(present, taken[place], 0.0)

        def own(x):
            return grads_ref[x].astype(F32)[brick * EDGE : (brick + 1) * EDGE]

        fill_padded(padded.at[brick], own, lambda offset: values[offset])
    fill_windows(padded.at[0], padded.at[1], shifted, windows)
    fill_flipped(first_ref, flipped)
    result = unpaired(times_flipped(windows[...], flipped[...])) * spread(occ_ref)
    for x in range(EDGE):
        for brick in range(2):
            at = 16 * x + EDGE * brick
            out_ref[brick, x] = result[at : at + EDGE].astype(BF16)


def unpack_kernel(parts_ref, first_out, second_out):
    halves = []
    for half in range(2):
        rows = []
        for chunk in (2 * half, 2 * half + 1):
            rows.append(
                jnp.concatenate(
                    [
                        jnp.concatenate(
                            [parts_ref[4 * piece + chunk] for piece in (2 * part, 2 * part + 1)],
                            axis=0,
                        )
                        for part in range(4)
                    ],
                    axis=1,
                )
            )
        halves.append(jnp.concatenate(rows, axis=0).astype(F32))
    first_out[...] = halves[1][:, : 27 * 64]
    blocks = []
    for pair in range(14):
        turned = halves[0][:, pair * 128 : pair * 128 + 128].T
        blocks += [turned[0:64], turned[64:128]]
    second_out[...] = jnp.concatenate(blocks[26::-1], axis=1)


def call(kernel, shapes, scratch, arguments, scalars=0, outside=0, megabytes=40, flops=0):
    specs = [pl.BlockSpec(memory_space=pltpu.SMEM)] * scalars
    specs += [pl.BlockSpec(memory_space=pl.ANY)] * outside
    specs += [pl.BlockSpec(memory_space=pltpu.VMEM)] * (len(arguments) - len(specs))
    return pl.pallas_call(
        kernel,
        out_shape=[jax.ShapeDtypeStruct(shape, kind) for shape, kind in shapes],
        in_specs=specs,
        out_specs=[pl.BlockSpec(memory_space=pltpu.VMEM)] * len(shapes),
        scratch_shapes=scratch,
        cost_estimate=pl.CostEstimate(flops=flops, bytes_accessed=2**19, transcendentals=0),
        compiler_params=pltpu.CompilerParams(vmem_limit_bytes=megabytes * 2**20),
    )(*arguments)


def per_device(inputs, occupancy, neighbours, first_kernel, second_kernel, out_grads):
    along_grp, along_dev = lax.axis_size("grp"), lax.axis_size("dev")
    devices = along_grp * along_dev
    scaling = 1.0 / math.sqrt(inputs.shape[0] * devices * EDGE**3)
    fours = [[4 * row + member for member in range(4)] for row in range(devices // 4)]
    rows = along_dev // 4
    stacks = [
        [along_dev * grp + 4 * row + member for row in range(rows)]
        for grp in range(along_grp)
        for member in range(4)
    ]
    planes = [
        [along_dev * grp + 4 * row + member for grp in range(along_grp) for member in range(4)]
        for row in range(rows)
    ]
    me = (lax.axis_index("grp") * along_dev + lax.axis_index("dev")).reshape(1)
    vmem = pltpu.VMEM

    def swap(value, members):
        return lax.all_to_all(value, AXES, 0, 0, axis_index_groups=members, tiled=True)

    def send_on(near, size):
        packets = ((4, size, WIDE), BF16)
        above, below = call(route_kernel, [packets, packets], [], [me, near], scalars=1)
        from_below = lax.ppermute(above, AXES, [(i, i + 4) for i in range(devices - 4)])
        from_above = lax.ppermute(below, AXES, [(i + 4, i) for i in range(devices - 4)])
        return from_below, from_above

    near, kept, masked = call(
        pack_kernel,
        [((4, 128, WIDE), BF16), ((4, 16, WIDE), BF16), ((EDGE, 16, WIDE), BF16)],
        [
            vmem((2, EDGE, EDGE, WIDE), BF16),
            vmem((2, EDGE, EDGE, WIDE), BF16),
            vmem((2, EDGE, 64), jnp.int32),
            vmem((4, 64, WIDE), F32),
            vmem((36, 16, WIDE), BF16),
            pltpu.SemaphoreType.DMA((3,)),
        ],
        [me, neighbours, inputs, out_grads, occupancy],
        scalars=2,
        outside=3,
        megabytes=60,
    )
    near = swap(near, fours)
    below, above = send_on(near, 64)
    pre_grads, near, kept = call(
        main_kernel,
        [((EDGE, 16, WIDE), BF16), ((4, 192, WIDE), BF16), ((4, EDGE, WIDE), F32)],
        [
            vmem((52, 16, WIDE), BF16),
            vmem((2, 2, 10 * ROWS, PADDED), F32),
            vmem((2, 3, 10, 16, PADDED), BF16),
            vmem((2, 512, 2304), BF16),
            vmem((2304, 128), BF16),
            vmem((128, 2304), BF16),
            vmem((128, 2304), F32),
            vmem((2, 64, WIDE), F32),
            vmem((36, EDGE, WIDE), F32),
        ],
        [
            me,
            neighbours,
            inputs,
            masked,
            occupancy,
            near,
            below,
            above,
            kept,
            first_kernel,
            second_kernel,
        ],
        scalars=2,
        flops=2**30,
    )
    near = swap(near, fours)
    below, above = send_on(near, 32)
    piece = (128 // along_grp, WIDE)
    (sums,) = call(first_sum_kernel, [((along_grp,) + piece, BF16)], [], [near])
    sums = lax.all_to_all(sums, "grp", 0, 0, tiled=True)
    (sums,) = call(functools.partial(next_sum_kernel, 1.0), [((rows,) + piece, BF16)], [], [sums])
    sums = swap(sums, stacks)
    (sums,) = call(
        functools.partial(next_sum_kernel, scaling), [((4 * along_grp,) + piece, BF16)], [], [sums]
    )
    sums = swap(sums, planes)
    (input_grads,) = call(
        input_grads_kernel,
        [((2, EDGE, EDGE, WIDE), BF16)],
        [
            vmem((52, EDGE, WIDE), F32),
            vmem((2, 10 * ROWS, PADDED), F32),
            vmem((3, 10, 16, PADDED), BF16),
            vmem((512, 2304), BF16),
            vmem((128, 2304), BF16),
        ],
        [me, neighbours, pre_grads, occupancy, near, below, above, kept, first_kernel],
        scalars=2,
        flops=2**28,
    )
    first_grads, second_grads = call(
        unpack_kernel, [((64, 27 * 64), F32), ((64, 27 * 64), F32)], [], [sums]
    )
    return input_grads, first_grads.T, second_grads.T


def solution(mesh):
    in_specs = (
        P(("grp", "dev"), None, None, None),
        P(("grp", "dev"), None, None),
        P(("grp", "dev"), None),
        P(),
        P(),
        P(("grp", "dev"), None, None, None),
    )
    out_specs = (P(("grp", "dev"), None, None, None), P(), P())
    return jax.shard_map(
        per_device, mesh=mesh, in_specs=in_specs, out_specs=out_specs, check_vma=False
    )
```

```python
import functools
import math

import jax
import jax.numpy as jnp
from jax import lax
from jax.experimental import pallas as pl
from jax.experimental.pallas import tpu as pltpu
from jax.sharding import PartitionSpec as P

AXES = ("grp", "dev")
EDGE = 8
WIDE = 512
PADDED = 640
ROWS = 24
PACKED = 1792
BF16 = jnp.bfloat16
F32 = jnp.float32


def directions():
    result = []
    for along_x in (-1, 0, 1):
        for along_y in (-1, 0, 1):
            for along_z in (-1, 0, 1):
                if along_x != 0 or along_y != 0 or along_z != 0:
                    result.append((along_x, along_y, along_z))
    return result


DIRECTIONS = directions()
NUMBER = {offset: number for number, offset in enumerate(DIRECTIONS)}


def locate(nb_ref, me, brick, number):
    other = nb_ref[brick, number]
    present = other >= 0
    owner = jnp.maximum(other, 0) >> 1
    return present, owner & 3, (owner >> 2) - (me >> 2), owner == me, other & 1


def send_place(nb_ref, me, brick, number):
    present, member, up, own, slot = locate(nb_ref, me, brick, number)
    relayed = (up > 0) | ((up < 0) & (member != (me & 3)))
    place = jnp.where(own, 32, member * 8 + jnp.where(relayed, 4, 0))
    return jnp.where(present, place + brick * 2 + slot, 32)


def take_place(nb_ref, me, brick, number):
    present, member, up, own, slot = locate(nb_ref, me, brick, number)
    place = member * 4 + jnp.where(up == 0, 0, jnp.where(up < 0, 16, 32))
    return present, jnp.where(own, 48, place) + slot * 2 + brick


def face_kind(offset):
    for axis in range(3):
        if offset[axis] != 0:
            return axis, 1 if offset[axis] > 0 else 0


def face_values(wide, index):
    faces = {}
    for side, at in ((0, 0), (1, EDGE - 1)):
        faces[0, side] = wide[index, at * EDGE : (at + 1) * EDGE, :]
        faces[1, side] = jnp.concatenate(
            [wide[index, x * EDGE + at : x * EDGE + at + 1, :] for x in range(EDGE)], axis=0
        )
        faces[2, side] = jnp.concatenate(
            [
                wide[index, x * EDGE : (x + 1) * EDGE, at * 64 : (at + 1) * 64]
                for x in range(EDGE)
            ],
            axis=1,
        )
    return faces


def spread(occ_ref):
    rows = []
    for x in range(EDGE):
        for brick in range(2):
            rows.append(jnp.broadcast_to(occ_ref[brick, x : x + 1, :].astype(F32), (EDGE, 64)))
    stacked = jnp.concatenate(rows, axis=0)
    row = lax.broadcasted_iota(jnp.int32, stacked.shape, 0)
    lane = lax.broadcasted_iota(jnp.int32, stacked.shape, 1)
    own = jnp.where((row & 7) == (lane >> 3), stacked, 0.0).astype(BF16)
    source = lax.broadcasted_iota(jnp.int32, (64, WIDE), 0)
    target = lax.broadcasted_iota(jnp.int32, (64, WIDE), 1)
    select = jnp.where((source & 7) == (target >> 6), 1.0, 0.0).astype(BF16)
    return jnp.dot(own, select, preferred_element_type=F32)


def pack_kernel(
    me_ref,
    nb_ref,
    x_hbm,
    g_hbm,
    occ_hbm,
    near_ref,
    kept_ref,
    masked_ref,
    x_ref,
    g_ref,
    occ_ref,
    wide,
    boxes,
    sems,
):
    copies = [
        pltpu.make_async_copy(source, target, sems.at[number])
        for number, (source, target) in enumerate(
            ((occ_hbm, occ_ref), (g_hbm, g_ref), (x_hbm, x_ref))
        )
    ]
    for copy in copies:
        copy.start()
    me = me_ref[0]
    copies[0].wait()
    occupied = spread(occ_ref)
    copies[1].wait()
    copies[2].wait()
    for x in range(EDGE):
        both = []
        for brick in range(2):
            wide[brick, x * EDGE : (x + 1) * EDGE, :] = x_ref[brick, x].astype(F32)
            at = (2 * x + brick) * EDGE
            piece = g_ref[brick, x].astype(F32) * occupied[at : at + EDGE]
            wide[2 + brick, x * EDGE : (x + 1) * EDGE, :] = piece
            both.append(piece)
        masked_ref[x] = jnp.concatenate(both, axis=0).astype(BF16)
    for brick in range(2):
        first = face_values(wide, brick)
        second = face_values(wide, 2 + brick)
        packets = {}
        for key in first:
            packets[key] = jnp.concatenate([first[key], second[key]], axis=0).astype(BF16)
        for number, offset in enumerate(DIRECTIONS):
            boxes[send_place(nb_ref, me, brick, number)] = packets[face_kind(offset)]
    near_ref[...] = boxes[0:32].reshape(4, 128, WIDE)
    kept_ref[...] = boxes[32:36]


def route_kernel(me_ref, near_ref, above_ref, below_ref):
    size = above_ref.shape[1]
    own = me_ref[0] & 3
    above_ref[...] = near_ref[:, size : 2 * size, :]
    below_ref[...] = near_ref[:, size : 2 * size, :]
    below_ref[own] = near_ref[own, 0:size, :]


def beside(low, middle, high):
    return jnp.concatenate([low, middle, high], axis=1)


def fill_padded(padded, own, pick):
    def planes(along_x, along_y):
        return (
            pick((along_x, along_y, -1))[:, WIDE - 64 :],
            pick((along_x, along_y, 0)),
            pick((along_x, along_y, 1))[:, :64],
        )

    below, above = pick((0, 0, -1)), pick((0, 0, 1))
    for x in range(EDGE):
        lanes = slice(x * 64, (x + 1) * 64)
        start = (x + 1) * ROWS + 8
        padded[start : start + EDGE, :] = beside(below[:, lanes], own(x), above[:, lanes])
    for along_y, row in ((-1, 7), (1, 16)):
        value = beside(*planes(0, along_y))
        for x in range(EDGE):
            start = (x + 1) * ROWS + row
            padded[start : start + 1, :] = value[x : x + 1]
    for along_x, at in ((-1, 0), (1, 9)):
        start = at * ROWS + 8
        padded[start : start + EDGE, :] = beside(*planes(along_x, 0))
        for along_y, row, source in ((-1, 7, 7), (1, 16, 0)):
            value = beside(*planes(along_x, along_y))
            padded[at * ROWS + row : at * ROWS + row + 1, :] = value[source : source + 1]


def fill_windows(first, second, shifted, windows):
    for along_y in range(3):
        for x in range(10):
            start = x * ROWS + 7 + along_y
            shifted[along_y, x] = jnp.concatenate(
                [first[start : start + EDGE, :], second[start : start + EDGE, :]], axis=0
            ).astype(BF16)
    for pair in range(4):
        for along_x in range(3):
            for along_y in range(3):
                place = (3 * along_x + along_y) * 256
                windows[pair * 128 : (pair + 1) * 128, place : place + 256] = shifted[
                    along_y, along_x : along_x + EDGE, :, pair * 128 : pair * 128 + 256
                ].reshape(128, 256)


def fill_direct(kernel_ref, direct):
    for group in range(9):
        block = kernel_ref[group * 192 : (group + 1) * 192, :]
        none = jnp.zeros((64, 64), BF16)
        direct[group * 256 : (group + 1) * 256, :] = jnp.concatenate(
            [
                jnp.concatenate([block, none], axis=0),
                jnp.concatenate([none, block], axis=0),
            ],
            axis=1,
        )


def fill_flipped(kernel_ref, flipped):
    none = jnp.zeros((64, 64), BF16)
    for group in range(9):
        base = 3 * (8 - group)
        blocks = [kernel_ref[(base + z) * 64 : (base + z + 1) * 64, :] for z in (2, 1, 0)]
        lanes = slice(group * 256, (group + 1) * 256)
        flipped[0:64, lanes] = jnp.concatenate(blocks + [none], axis=1)
        flipped[64:128, lanes] = jnp.concatenate([none] + blocks, axis=1)


def spread_kernel(
    first_ref,
    second_ref,
    occ_ref,
    nb_ref,
    direct_ref,
    flipped_ref,
    first_flipped_ref,
    occupied_ref,
    near_nb_ref,
):
    near_nb_ref[...] = nb_ref[...]
    occupied_ref[...] = spread(occ_ref)
    fill_direct(first_ref, direct_ref)
    fill_flipped(second_ref, flipped_ref)
    fill_flipped(first_ref, first_flipped_ref)


def times_flipped(windows, flipped):
    return lax.dot_general(
        windows, flipped, (((1,), (1,)), ((), ())), preferred_element_type=F32
    )


def paired(natural):
    return jnp.concatenate([natural[:, p * 128 : (p + 1) * 128] for p in range(4)], axis=0)


def unpaired(value):
    return jnp.concatenate([value[p * 128 : (p + 1) * 128] for p in range(4)], axis=1)


def gather_blocks(product):
    pieces = []
    for group in range(9):
        at = group * 256
        pieces.append(product[0:64, at : at + 192] + product[64:128, at + 64 : at + 256])
    pieces.append(jnp.zeros((64, PACKED - 27 * 64), F32))
    return jnp.concatenate(pieces, axis=1)


def tile_place(chunk, tile):
    row, lane = EDGE * (tile // 4), 128 * (tile % 4)
    if row < 96:
        return 32 * chunk + row % 32, WIDE * (row // 32) + lane
    return 32 * chunk + row - 96 + 16 * (lane // 256), 3 * WIDE + lane % 256


def main_kernel(
    me_ref,
    nb_ref,
    x_ref,
    masked_ref,
    occupied_ref,
    near_ref,
    below_ref,
    above_ref,
    kept_in,
    direct,
    flipped,
    grads_ref,
    out_ref,
    kept_ref,
    taken,
    padded,
    shifted,
    windows,
    product,
    wide,
    boxes,
):
    me = me_ref[0]
    for member in range(4):
        at = 4 * member
        taken[at : at + 4] = near_ref[member, 0:64, :].reshape(4, 16, WIDE)
        taken[at + 16 : at + 20] = below_ref[member].reshape(4, 16, WIDE)
        taken[at + 32 : at + 36] = above_ref[member].reshape(4, 16, WIDE)
    taken[48:52] = kept_in[...]
    for brick in range(2):
        values = {}
        for number, offset in enumerate(DIRECTIONS):
            present, place = take_place(nb_ref, me, brick, number)
            values[offset] = jnp.where(present, taken[place].astype(F32), 0.0)

        def own_first(x):
            return x_ref[brick, x].astype(F32)

        def own_second(x):
            return masked_ref[x].astype(F32)[brick * EDGE : (brick + 1) * EDGE]

        fill_padded(padded.at[0, brick], own_first, lambda offset: values[offset][0:8])
        fill_padded(padded.at[1, brick], own_second, lambda offset: values[offset][8:16])
    for field in range(2):
        fill_windows(padded.at[field, 0], padded.at[field, 1], shifted.at[field], windows.at[field])
    occupied = paired(occupied_ref[...])
    pre_act = jnp.dot(windows[0], direct[...], preferred_element_type=F32)
    logistic = 1.0 / (1.0 + jnp.exp(-pre_act))
    hidden = (pre_act * logistic * occupied).astype(BF16)
    slope = logistic * (1.0 + pre_act * (1.0 - logistic))
    hidden_grad = times_flipped(windows[1], flipped[...])
    pre_grads = (hidden_grad * slope * occupied).astype(BF16)

    natural = unpaired(pre_grads.astype(F32))
    for x in range(EDGE):
        grads_ref[x] = natural[16 * x : 16 * x + 16].astype(BF16)
        for brick in range(2):
            at = 16 * x + EDGE * brick
            wide[brick, x * EDGE : (x + 1) * EDGE, :] = natural[at : at + EDGE]
    for brick in range(2):
        faces = face_values(wide, brick)
        for number, offset in enumerate(DIRECTIONS):
            boxes[send_place(nb_ref, me, brick, number)] = faces[face_kind(offset)]
    for member in range(4):
        out_ref[member, 0:64, :] = (
            boxes[8 * member : 8 * member + 8].reshape(64, WIDE).astype(BF16)
        )
    kept_ref[...] = boxes[32:36]

    for half, own, field in ((0, hidden, 1), (1, pre_grads, 0)):
        turned = own.astype(F32).T.astype(BF16)
        product[...] = jnp.dot(turned, windows[field], preferred_element_type=F32)
        packed = gather_blocks(product).astype(BF16)
        for chunk in range(2):
            start = 32 * chunk
            for part in range(3):
                at = 64 + 32 * part
                out_ref[2 * half + chunk, at : at + 32, :] = packed[
                    start : start + 32, part * WIDE : (part + 1) * WIDE
                ]
            rest = packed[start : start + 32, 3 * WIDE :]
            out_ref[2 * half + chunk, 160:176, :] = jnp.concatenate(
                [rest[0:16], rest[16:32]], axis=1
            )


def first_sum_kernel(parts_ref, pieces_ref):
    total = parts_ref[0, 64:176, :].astype(F32)
    for member in range(1, 4):
        total = total + parts_ref[member, 64:176, :].astype(F32)
    count = pieces_ref.shape[1]
    for tile in range(56):
        row, lane = EDGE * (tile // 4), 128 * (tile % 4)
        pieces_ref[tile // count, tile % count] = total[
            row : row + EDGE, lane : lane + 128
        ].astype(BF16)


def next_sum_kernel(scaling, parts_ref, copies_ref):
    total = parts_ref[0].astype(F32)
    for member in range(1, parts_ref.shape[0]):
        total = total + parts_ref[member].astype(F32)
    total = total * scaling
    for member in range(copies_ref.shape[0]):
        copies_ref[member] = total.astype(copies_ref.dtype)


def input_grads_kernel(
    me_ref,
    nb_ref,
    grads_ref,
    occupied_ref,
    near_ref,
    below_ref,
    above_ref,
    kept_ref,
    flipped,
    out_ref,
    taken,
    padded,
    shifted,
    windows,
):
    me = me_ref[0]
    for member in range(4):
        at = 4 * member
        taken[at : at + 4] = near_ref[member, 0:32, :].astype(F32).reshape(4, EDGE, WIDE)
        taken[at + 16 : at + 20] = below_ref[member].astype(F32).reshape(4, EDGE, WIDE)
        taken[at + 32 : at + 36] = above_ref[member].astype(F32).reshape(4, EDGE, WIDE)
    taken[48:52] = kept_ref[...]
    for brick in range(2):
        values = {}
        for number, offset in enumerate(DIRECTIONS):
            present, place = take_place(nb_ref, me, brick, number)
            values[offset] = jnp.where(present, taken[place], 0.0)

        def own(x):
            return grads_ref[x].astype(F32)[brick * EDGE : (brick + 1) * EDGE]

        fill_padded(padded.at[brick], own, lambda offset: values[offset])
    fill_windows(padded.at[0], padded.at[1], shifted, windows)
    result = unpaired(times_flipped(windows[...], flipped[...])) * occupied_ref[...]
    for x in range(EDGE):
        for brick in range(2):
            at = 16 * x + EDGE * brick
            out_ref[brick, x] = result[at : at + EDGE].astype(BF16)


def unpack_kernel(parts_ref, first_hbm, second_hbm, first_out, second_out, halves, sems):
    count = parts_ref.shape[1]
    for chunk in (2, 3, 0, 1):
        for tile in range(56):
            row, lane = tile_place(chunk, tile)
            halves[row : row + EDGE, lane : lane + 128] = parts_ref[
                4 * (tile // count) + chunk, tile % count
            ].astype(F32)
    first_out[...] = halves[64:128, : 27 * 64]
    first_copy = pltpu.make_async_copy(first_out, first_hbm, sems.at[0])
    first_copy.start()
    blocks = []
    for pair in range(14):
        turned = halves[0:64, pair * 128 : pair * 128 + 128].T
        blocks += [turned[0:64], turned[64:128]]
    second_out[...] = jnp.concatenate(blocks[26::-1], axis=1)
    second_copy = pltpu.make_async_copy(second_out, second_hbm, sems.at[1])
    second_copy.start()
    first_copy.wait()
    second_copy.wait()


def call(kernel, shapes, scratch, arguments, scalars=0, outside=0, leaving=False, megabytes=40, flops=0):
    specs = [pl.BlockSpec(memory_space=pltpu.SMEM)] * scalars
    specs += [pl.BlockSpec(memory_space=pltpu.HBM)] * outside
    specs += [pl.BlockSpec(memory_space=pltpu.VMEM)] * (len(arguments) - len(specs))
    return pl.pallas_call(
        kernel,
        out_shape=[jax.ShapeDtypeStruct(shape, kind) for shape, kind in shapes],
        in_specs=specs,
        out_specs=[pl.BlockSpec(memory_space=pltpu.HBM if leaving else pltpu.VMEM)] * len(shapes),
        scratch_shapes=scratch,
        cost_estimate=pl.CostEstimate(flops=flops, bytes_accessed=2**19, transcendentals=0),
        compiler_params=pltpu.CompilerParams(vmem_limit_bytes=megabytes * 2**20),
    )(*arguments)


def per_device(inputs, occupancy, neighbours, first_kernel, second_kernel, out_grads):
    along_grp, along_dev = lax.axis_size("grp"), lax.axis_size("dev")
    devices = along_grp * along_dev
    scaling = 1.0 / math.sqrt(inputs.shape[0] * devices * EDGE**3)
    fours = [[4 * row + member for member in range(4)] for row in range(devices // 4)]
    rows = along_dev // 4
    stacks = [
        [along_dev * grp + 4 * row + member for row in range(rows)]
        for grp in range(along_grp)
        for member in range(4)
    ]
    planes = [
        [along_dev * grp + 4 * row + member for grp in range(along_grp) for member in range(4)]
        for row in range(rows)
    ]
    me = (lax.axis_index("grp") * along_dev + lax.axis_index("dev")).reshape(1)
    vmem = pltpu.VMEM

    def swap(value, members):
        return lax.all_to_all(value, AXES, 0, 0, axis_index_groups=members, tiled=True)

    def send_on(near, size):
        packets = ((4, size, WIDE), BF16)
        above, below = call(route_kernel, [packets, packets], [], [me, near], scalars=1)
        from_below = lax.ppermute(above, AXES, [(i, i + 4) for i in range(devices - 4)])
        from_above = lax.ppermute(below, AXES, [(i + 4, i) for i in range(devices - 4)])
        return from_below, from_above

    near, kept, masked = call(
        pack_kernel,
        [
            ((4, 128, WIDE), BF16),
            ((4, 16, WIDE), BF16),
            ((EDGE, 16, WIDE), BF16),
        ],
        [
            vmem((2, EDGE, EDGE, WIDE), BF16),
            vmem((2, EDGE, EDGE, WIDE), BF16),
            vmem((2, EDGE, 64), jnp.int32),
            vmem((4, 64, WIDE), F32),
            vmem((36, 16, WIDE), BF16),
            pltpu.SemaphoreType.DMA((3,)),
        ],
        [me, neighbours, inputs, out_grads, occupancy],
        scalars=2,
        outside=3,
        megabytes=60,
    )
    near = swap(near, fours)
    below, above = send_on(near, 64)
    direct, flipped, first_flipped, occupied, near_nb = call(
        spread_kernel,
        [
            ((2304, 128), BF16),
            ((128, 2304), BF16),
            ((128, 2304), BF16),
            ((128, WIDE), F32),
            ((2, 26), jnp.int32),
        ],
        [],
        [first_kernel, second_kernel, occupancy, neighbours],
    )
    pre_grads, near, kept = call(
        main_kernel,
        [((EDGE, 16, WIDE), BF16), ((4, 176, WIDE), BF16), ((4, EDGE, WIDE), F32)],
        [
            vmem((52, 16, WIDE), BF16),
            vmem((2, 2, 10 * ROWS, PADDED), F32),
            vmem((2, 3, 10, 16, PADDED), BF16),
            vmem((2, 512, 2304), BF16),
            vmem((128, 2304), F32),
            vmem((2, 64, WIDE), F32),
            vmem((36, EDGE, WIDE), F32),
        ],
        [me, near_nb, inputs, masked, occupied, near, below, above, kept, direct, flipped],
        scalars=2,
        flops=2**30,
    )
    near = swap(near, fours)
    below, above = send_on(near, 32)
    piece = (56 // along_grp, EDGE, 128)
    (sums,) = call(first_sum_kernel, [((along_grp,) + piece, BF16)], [], [near])
    sums = lax.all_to_all(sums, "grp", 0, 0, tiled=True)
    (sums,) = call(functools.partial(next_sum_kernel, 1.0), [((rows,) + piece, BF16)], [], [sums])
    sums = swap(sums, stacks)
    (sums,) = call(
        functools.partial(next_sum_kernel, scaling), [((4 * along_grp,) + piece, BF16)], [], [sums]
    )
    sums = swap(sums, planes)
    (input_grads,) = call(
        input_grads_kernel,
        [((2, EDGE, EDGE, WIDE), BF16)],
        [
            vmem((52, EDGE, WIDE), F32),
            vmem((2, 10 * ROWS, PADDED), F32),
            vmem((3, 10, 16, PADDED), BF16),
            vmem((512, 2304), BF16),
        ],
        [me, near_nb, pre_grads, occupied, near, below, above, kept, first_flipped],
        scalars=2,
        flops=2**28,
    )
    first_grads, second_grads = call(
        unpack_kernel,
        [((64, 27 * 64), F32), ((64, 27 * 64), F32)],
        [
            vmem((64, 27 * 64), F32),
            vmem((64, 27 * 64), F32),
            vmem((128, PACKED), F32),
            pltpu.SemaphoreType.DMA((2,)),
        ],
        [sums],
        leaving=True,
    )
    return input_grads, first_grads.T, second_grads.T


def solution(mesh):
    in_specs = (
        P(("grp", "dev"), None, None, None),
        P(("grp", "dev"), None, None),
        P(("grp", "dev"), None),
        P(),
        P(),
        P(("grp", "dev"), None, None, None),
    )
    out_specs = (P(("grp", "dev"), None, None, None), P(), P())
    return jax.shard_map(
        per_device, mesh=mesh, in_specs=in_specs, out_specs=out_specs, check_vma=False
    )
```

```python
import functools
import math

import jax
import jax.numpy as jnp
from jax import lax
from jax.experimental import pallas as pl
from jax.experimental.pallas import tpu as pltpu
from jax.sharding import PartitionSpec as P

AXES = ("grp", "dev")
EDGE = 8
WIDE = 512
PADDED = 640
ROWS = 24
PACKED = 1792
BF16 = jnp.bfloat16
F32 = jnp.float32


def directions():
    result = []
    for along_x in (-1, 0, 1):
        for along_y in (-1, 0, 1):
            for along_z in (-1, 0, 1):
                if along_x != 0 or along_y != 0 or along_z != 0:
                    result.append((along_x, along_y, along_z))
    return result


DIRECTIONS = directions()
NUMBER = {offset: number for number, offset in enumerate(DIRECTIONS)}


def locate(nb_ref, me, brick, number):
    other = nb_ref[brick, number]
    present = other >= 0
    owner = jnp.maximum(other, 0) >> 1
    return present, owner & 3, (owner >> 2) - (me >> 2), owner == me, other & 1


def send_place(nb_ref, me, brick, number):
    present, member, up, own, slot = locate(nb_ref, me, brick, number)
    relayed = (up > 0) | ((up < 0) & (member != (me & 3)))
    place = jnp.where(own, 32, member * 8 + jnp.where(relayed, 4, 0))
    return jnp.where(present, place + brick * 2 + slot, 32)


def take_place(nb_ref, me, brick, number):
    present, member, up, own, slot = locate(nb_ref, me, brick, number)
    longer = (up < 0) == ((me & 3) < 2)
    relayed = jnp.where(longer, 16 + 4 * member, 32 + 4 * (member & 1))
    place = jnp.where(up == 0, 4 * member, relayed)
    return present, jnp.where(own, 40, place) + slot * 2 + brick


def face_kind(offset):
    for axis in range(3):
        if offset[axis] != 0:
            return axis, 1 if offset[axis] > 0 else 0


def face_values(wide, index):
    faces = {}
    for side, at in ((0, 0), (1, EDGE - 1)):
        faces[0, side] = wide[index, at * EDGE : (at + 1) * EDGE, :]
        faces[1, side] = jnp.concatenate(
            [wide[index, x * EDGE + at : x * EDGE + at + 1, :] for x in range(EDGE)], axis=0
        )
        faces[2, side] = jnp.concatenate(
            [
                wide[index, x * EDGE : (x + 1) * EDGE, at * 64 : (at + 1) * 64]
                for x in range(EDGE)
            ],
            axis=1,
        )
    return faces


def spread(occ_ref):
    rows = []
    for x in range(EDGE):
        for brick in range(2):
            rows.append(jnp.broadcast_to(occ_ref[brick, x : x + 1, :].astype(F32), (EDGE, 64)))
    stacked = jnp.concatenate(rows, axis=0)
    row = lax.broadcasted_iota(jnp.int32, stacked.shape, 0)
    lane = lax.broadcasted_iota(jnp.int32, stacked.shape, 1)
    own = jnp.where((row & 7) == (lane >> 3), stacked, 0.0).astype(BF16)
    source = lax.broadcasted_iota(jnp.int32, (64, WIDE), 0)
    target = lax.broadcasted_iota(jnp.int32, (64, WIDE), 1)
    select = jnp.where((source & 7) == (target >> 6), 1.0, 0.0).astype(BF16)
    return jnp.dot(own, select, preferred_element_type=F32)


def pack_kernel(
    me_ref,
    nb_hbm,
    x_hbm,
    g_hbm,
    occ_hbm,
    near_ref,
    kept_ref,
    masked_ref,
    x_ref,
    g_ref,
    occ_ref,
    wide,
    boxes,
    nb_ref,
    sems,
):
    copies = [
        pltpu.make_async_copy(source, target, sems.at[number])
        for number, (source, target) in enumerate(
            ((occ_hbm, occ_ref), (g_hbm, g_ref), (x_hbm, x_ref), (nb_hbm, nb_ref))
        )
    ]
    for copy in copies:
        copy.start()
    me = me_ref[0]
    copies[0].wait()
    occupied = spread(occ_ref)
    copies[1].wait()
    copies[2].wait()
    for x in range(EDGE):
        both = []
        for brick in range(2):
            wide[brick, x * EDGE : (x + 1) * EDGE, :] = x_ref[brick, x].astype(F32)
            at = (2 * x + brick) * EDGE
            piece = g_ref[brick, x].astype(F32) * occupied[at : at + EDGE]
            wide[2 + brick, x * EDGE : (x + 1) * EDGE, :] = piece
            both.append(piece)
        masked_ref[x] = jnp.concatenate(both, axis=0).astype(BF16)
    copies[3].wait()
    for brick in range(2):
        first = face_values(wide, brick)
        second = face_values(wide, 2 + brick)
        packets = {}
        for key in first:
            packets[key] = jnp.concatenate([first[key], second[key]], axis=0).astype(BF16)
        for number, offset in enumerate(DIRECTIONS):
            boxes[send_place(nb_ref, me, brick, number)] = packets[face_kind(offset)]
    near_ref[...] = boxes[0:32].reshape(4, 128, WIDE)
    kept_ref[...] = boxes[32:36]


def route_kernel(me_ref, near_ref, longer_ref, shorter_ref):
    size = longer_ref.shape[1]
    own = me_ref[0] & 3
    longer_ref[...] = near_ref[:, size : 2 * size, :]
    for number in range(2):
        shorter_ref[number] = near_ref[(own & 2) + number, size : 2 * size, :]

    @pl.when(own >= 2)
    def _():
        longer_ref[own] = near_ref[own, 0:size, :]

    @pl.when(own < 2)
    def _():
        shorter_ref[own & 1] = near_ref[own, 0:size, :]


def beside(low, middle, high):
    return jnp.concatenate([low, middle, high], axis=1)


def fill_padded(padded, own, pick):
    def planes(along_x, along_y):
        return (
            pick((along_x, along_y, -1))[:, WIDE - 64 :],
            pick((along_x, along_y, 0)),
            pick((along_x, along_y, 1))[:, :64],
        )

    below, above = pick((0, 0, -1)), pick((0, 0, 1))
    for x in range(EDGE):
        lanes = slice(x * 64, (x + 1) * 64)
        start = (x + 1) * ROWS + 8
        padded[start : start + EDGE, :] = beside(below[:, lanes], own(x), above[:, lanes])
    for along_y, row in ((-1, 7), (1, 16)):
        value = beside(*planes(0, along_y))
        for x in range(EDGE):
            start = (x + 1) * ROWS + row
            padded[start : start + 1, :] = value[x : x + 1]
    for along_x, at in ((-1, 0), (1, 9)):
        start = at * ROWS + 8
        padded[start : start + EDGE, :] = beside(*planes(along_x, 0))
        for along_y, row, source in ((-1, 7, 7), (1, 16, 0)):
            value = beside(*planes(along_x, along_y))
            padded[at * ROWS + row : at * ROWS + row + 1, :] = value[source : source + 1]


def fill_windows(first, second, shifted, windows):
    for along_y in range(3):
        for x in range(10):
            start = x * ROWS + 7 + along_y
            shifted[along_y, x] = jnp.concatenate(
                [first[start : start + EDGE, :], second[start : start + EDGE, :]], axis=0
            ).astype(BF16)
    for pair in range(4):
        for along_x in range(3):
            for along_y in range(3):
                place = (3 * along_x + along_y) * 256
                windows[pair * 128 : (pair + 1) * 128, place : place + 256] = shifted[
                    along_y, along_x : along_x + EDGE, :, pair * 128 : pair * 128 + 256
                ].reshape(128, 256)


def fill_direct(kernel_ref, direct):
    for group in range(9):
        block = kernel_ref[group * 192 : (group + 1) * 192, :]
        none = jnp.zeros((64, 64), BF16)
        direct[group * 256 : (group + 1) * 256, :] = jnp.concatenate(
            [
                jnp.concatenate([block, none], axis=0),
                jnp.concatenate([none, block], axis=0),
            ],
            axis=1,
        )


def fill_flipped(kernel_ref, flipped):
    none = jnp.zeros((64, 64), BF16)
    for group in range(9):
        base = 3 * (8 - group)
        blocks = [kernel_ref[(base + z) * 64 : (base + z + 1) * 64, :] for z in (2, 1, 0)]
        lanes = slice(group * 256, (group + 1) * 256)
        flipped[0:64, lanes] = jnp.concatenate(blocks + [none], axis=1)
        flipped[64:128, lanes] = jnp.concatenate([none] + blocks, axis=1)


def spread_kernel(
    first_ref,
    second_ref,
    occ_ref,
    nb_ref,
    direct_ref,
    flipped_ref,
    first_flipped_ref,
    occupied_ref,
    near_nb_ref,
):
    near_nb_ref[...] = nb_ref[...]
    occupied_ref[...] = spread(occ_ref)
    fill_direct(first_ref, direct_ref)
    fill_flipped(second_ref, flipped_ref)
    fill_flipped(first_ref, first_flipped_ref)


def times_flipped(windows, flipped):
    return lax.dot_general(
        windows, flipped, (((1,), (1,)), ((), ())), preferred_element_type=F32
    )


def paired(natural):
    return jnp.concatenate([natural[:, p * 128 : (p + 1) * 128] for p in range(4)], axis=0)


def unpaired(value):
    return jnp.concatenate([value[p * 128 : (p + 1) * 128] for p in range(4)], axis=1)


def gather_blocks(product):
    pieces = []
    for group in range(9):
        at = group * 256
        pieces.append(product[0:64, at : at + 192] + product[64:128, at + 64 : at + 256])
    pieces.append(jnp.zeros((64, PACKED - 27 * 64), F32))
    return jnp.concatenate(pieces, axis=1)


def tile_place(chunk, tile):
    row, lane = EDGE * (tile // 4), 128 * (tile % 4)
    if row < 96:
        return 32 * chunk + row % 32, WIDE * (row // 32) + lane
    return 32 * chunk + row - 96 + 16 * (lane // 256), 3 * WIDE + lane % 256


def main_kernel(
    me_ref,
    nb_ref,
    x_ref,
    masked_ref,
    occupied_ref,
    near_ref,
    longer_ref,
    shorter_ref,
    kept_in,
    direct,
    flipped,
    grads_ref,
    out_ref,
    kept_ref,
    taken,
    padded,
    shifted,
    windows,
    product,
    wide,
    boxes,
):
    me = me_ref[0]
    for member in range(4):
        at = 4 * member
        taken[at : at + 4] = near_ref[member, 0:64, :].reshape(4, 16, WIDE)
        taken[at + 16 : at + 20] = longer_ref[member].reshape(4, 16, WIDE)
    for number in range(2):
        taken[32 + 4 * number : 36 + 4 * number] = shorter_ref[number].reshape(4, 16, WIDE)
    taken[40:44] = kept_in[...]
    for brick in range(2):
        values = {}
        for number, offset in enumerate(DIRECTIONS):
            present, place = take_place(nb_ref, me, brick, number)
            values[offset] = jnp.where(present, taken[place].astype(F32), 0.0)

        def own_first(x):
            return x_ref[brick, x].astype(F32)

        def own_second(x):
            return masked_ref[x].astype(F32)[brick * EDGE : (brick + 1) * EDGE]

        fill_padded(padded.at[0, brick], own_first, lambda offset: values[offset][0:8])
        fill_padded(padded.at[1, brick], own_second, lambda offset: values[offset][8:16])
    for field in range(2):
        fill_windows(padded.at[field, 0], padded.at[field, 1], shifted.at[field], windows.at[field])
    occupied = paired(occupied_ref[...])
    pre_act = jnp.dot(windows[0], direct[...], preferred_element_type=F32)
    logistic = 1.0 / (1.0 + jnp.exp(-pre_act))
    hidden = (pre_act * logistic * occupied).astype(BF16)
    slope = logistic * (1.0 + pre_act * (1.0 - logistic))
    hidden_grad = times_flipped(windows[1], flipped[...])
    pre_grads = (hidden_grad * slope * occupied).astype(BF16)

    natural = unpaired(pre_grads.astype(F32))
    for x in range(EDGE):
        grads_ref[x] = natural[16 * x : 16 * x + 16].astype(BF16)
        for brick in range(2):
            at = 16 * x + EDGE * brick
            wide[brick, x * EDGE : (x + 1) * EDGE, :] = natural[at : at + EDGE]
    for brick in range(2):
        faces = face_values(wide, brick)
        for number, offset in enumerate(DIRECTIONS):
            boxes[send_place(nb_ref, me, brick, number)] = faces[face_kind(offset)]
    for member in range(4):
        out_ref[member, 0:64, :] = (
            boxes[8 * member : 8 * member + 8].reshape(64, WIDE).astype(BF16)
        )
    kept_ref[...] = boxes[32:36]

    for half, own, field in ((0, hidden, 1), (1, pre_grads, 0)):
        turned = own.astype(F32).T.astype(BF16)
        product[...] = jnp.dot(turned, windows[field], preferred_element_type=F32)
        packed = gather_blocks(product).astype(BF16)
        for chunk in range(2):
            start = 32 * chunk
            for part in range(3):
                at = 64 + 32 * part
                out_ref[2 * half + chunk, at : at + 32, :] = packed[
                    start : start + 32, part * WIDE : (part + 1) * WIDE
                ]
            rest = packed[start : start + 32, 3 * WIDE :]
            out_ref[2 * half + chunk, 160:176, :] = jnp.concatenate(
                [rest[0:16], rest[16:32]], axis=1
            )


def first_sum_kernel(parts_ref, pieces_ref):
    total = parts_ref[0, 64:176, :].astype(F32)
    for member in range(1, 4):
        total = total + parts_ref[member, 64:176, :].astype(F32)
    count = pieces_ref.shape[1]
    for tile in range(56):
        row, lane = EDGE * (tile // 4), 128 * (tile % 4)
        pieces_ref[tile // count, tile % count] = total[
            row : row + EDGE, lane : lane + 128
        ].astype(BF16)


def next_sum_kernel(scaling, parts_ref, copies_ref):
    total = parts_ref[0].astype(F32)
    for member in range(1, parts_ref.shape[0]):
        total = total + parts_ref[member].astype(F32)
    total = total * scaling
    for member in range(copies_ref.shape[0]):
        copies_ref[member] = total.astype(copies_ref.dtype)


def input_grads_kernel(
    me_ref,
    nb_ref,
    grads_ref,
    occupied_ref,
    near_ref,
    longer_ref,
    shorter_ref,
    kept_ref,
    flipped,
    out_ref,
    taken,
    padded,
    shifted,
    windows,
):
    me = me_ref[0]
    for member in range(4):
        at = 4 * member
        taken[at : at + 4] = near_ref[member, 0:32, :].astype(F32).reshape(4, EDGE, WIDE)
        taken[at + 16 : at + 20] = longer_ref[member].astype(F32).reshape(4, EDGE, WIDE)
    for number in range(2):
        taken[32 + 4 * number : 36 + 4 * number] = (
            shorter_ref[number].astype(F32).reshape(4, EDGE, WIDE)
        )
    taken[40:44] = kept_ref[...]
    for brick in range(2):
        values = {}
        for number, offset in enumerate(DIRECTIONS):
            present, place = take_place(nb_ref, me, brick, number)
            values[offset] = jnp.where(present, taken[place], 0.0)

        def own(x):
            return grads_ref[x].astype(F32)[brick * EDGE : (brick + 1) * EDGE]

        fill_padded(padded.at[brick], own, lambda offset: values[offset])
    fill_windows(padded.at[0], padded.at[1], shifted, windows)
    result = unpaired(times_flipped(windows[...], flipped[...])) * occupied_ref[...]
    for x in range(EDGE):
        for brick in range(2):
            at = 16 * x + EDGE * brick
            out_ref[brick, x] = result[at : at + EDGE].astype(BF16)


def unpack_kernel(parts_ref, first_hbm, second_hbm, first_out, second_out, halves, sems):
    count = parts_ref.shape[1]
    for chunk in (2, 3, 0, 1):
        for tile in range(56):
            row, lane = tile_place(chunk, tile)
            halves[row : row + EDGE, lane : lane + 128] = parts_ref[
                4 * (tile // count) + chunk, tile % count
            ].astype(F32)
    first_out[...] = halves[64:128, : 27 * 64]
    first_copy = pltpu.make_async_copy(first_out, first_hbm, sems.at[0])
    first_copy.start()
    blocks = []
    for pair in range(14):
        turned = halves[0:64, pair * 128 : pair * 128 + 128].T
        blocks += [turned[0:64], turned[64:128]]
    second_out[...] = jnp.concatenate(blocks[26::-1], axis=1)
    second_copy = pltpu.make_async_copy(second_out, second_hbm, sems.at[1])
    second_copy.start()
    first_copy.wait()
    second_copy.wait()


def call(kernel, shapes, scratch, arguments, scalars=0, outside=0, leaving=False, megabytes=40, flops=0):
    specs = [pl.BlockSpec(memory_space=pltpu.SMEM)] * scalars
    specs += [pl.BlockSpec(memory_space=pltpu.HBM)] * outside
    specs += [pl.BlockSpec(memory_space=pltpu.VMEM)] * (len(arguments) - len(specs))
    return pl.pallas_call(
        kernel,
        out_shape=[jax.ShapeDtypeStruct(shape, kind) for shape, kind in shapes],
        in_specs=specs,
        out_specs=[pl.BlockSpec(memory_space=pltpu.HBM if leaving else pltpu.VMEM)] * len(shapes),
        scratch_shapes=scratch,
        cost_estimate=pl.CostEstimate(flops=flops, bytes_accessed=2**19, transcendentals=0),
        compiler_params=pltpu.CompilerParams(vmem_limit_bytes=megabytes * 2**20),
    )(*arguments)


def per_device(inputs, occupancy, neighbours, first_kernel, second_kernel, out_grads):
    along_grp, along_dev = lax.axis_size("grp"), lax.axis_size("dev")
    devices = along_grp * along_dev
    scaling = 1.0 / math.sqrt(inputs.shape[0] * devices * EDGE**3)
    fours = [[4 * row + member for member in range(4)] for row in range(devices // 4)]
    rows = along_dev // 4
    stacks = [
        [along_dev * grp + 4 * row + member for row in range(rows)]
        for grp in range(along_grp)
        for member in range(4)
    ]
    planes = [
        [along_dev * grp + 4 * row + member for grp in range(along_grp) for member in range(4)]
        for row in range(rows)
    ]
    me = (lax.axis_index("grp") * along_dev + lax.axis_index("dev")).reshape(1)
    vmem = pltpu.VMEM

    def swap(value, members):
        return lax.all_to_all(value, AXES, 0, 0, axis_index_groups=members, tiled=True)

    longer_way = [(i, i + 4 if i & 2 == 0 else i - 4) for i in range(devices)]
    shorter_way = [(i, i - 4 if i & 2 == 0 else i + 4) for i in range(devices)]

    def send_on(near, size):
        longer, shorter = call(
            route_kernel,
            [((4, size, WIDE), BF16), ((2, size, WIDE), BF16)],
            [],
            [me, near],
            scalars=1,
        )
        return [
            lax.ppermute(value, AXES, [(i, j) for i, j in way if 0 <= j < devices])
            for value, way in ((longer, longer_way), (shorter, shorter_way))
        ]

    near, kept, masked = call(
        pack_kernel,
        [
            ((4, 128, WIDE), BF16),
            ((4, 16, WIDE), BF16),
            ((EDGE, 16, WIDE), BF16),
        ],
        [
            vmem((2, EDGE, EDGE, WIDE), BF16),
            vmem((2, EDGE, EDGE, WIDE), BF16),
            vmem((2, EDGE, 64), jnp.int32),
            vmem((4, 64, WIDE), F32),
            vmem((36, 16, WIDE), BF16),
            pltpu.SMEM((2, 26), jnp.int32),
            pltpu.SemaphoreType.DMA((4,)),
        ],
        [me, neighbours, inputs, out_grads, occupancy],
        scalars=1,
        outside=4,
        megabytes=60,
    )
    near = swap(near, fours)
    longer, shorter = send_on(near, 64)
    direct, flipped, first_flipped, occupied, near_nb = call(
        spread_kernel,
        [
            ((2304, 128), BF16),
            ((128, 2304), BF16),
            ((128, 2304), BF16),
            ((128, WIDE), F32),
            ((2, 26), jnp.int32),
        ],
        [],
        [first_kernel, second_kernel, occupancy, neighbours],
    )
    pre_grads, near, kept = call(
        main_kernel,
        [((EDGE, 16, WIDE), BF16), ((4, 176, WIDE), BF16), ((4, EDGE, WIDE), F32)],
        [
            vmem((44, 16, WIDE), BF16),
            vmem((2, 2, 10 * ROWS, PADDED), F32),
            vmem((2, 3, 10, 16, PADDED), BF16),
            vmem((2, 512, 2304), BF16),
            vmem((128, 2304), F32),
            vmem((2, 64, WIDE), F32),
            vmem((36, EDGE, WIDE), F32),
        ],
        [me, near_nb, inputs, masked, occupied, near, longer, shorter, kept, direct, flipped],
        scalars=2,
        flops=2**30,
    )
    near = swap(near, fours)
    longer, shorter = send_on(near, 32)
    piece = (56 // along_grp, EDGE, 128)
    (sums,) = call(first_sum_kernel, [((along_grp,) + piece, BF16)], [], [near])
    sums = lax.all_to_all(sums, "grp", 0, 0, tiled=True)
    (sums,) = call(functools.partial(next_sum_kernel, 1.0), [((rows,) + piece, BF16)], [], [sums])
    sums = swap(sums, stacks)
    (sums,) = call(
        functools.partial(next_sum_kernel, scaling), [((4 * along_grp,) + piece, BF16)], [], [sums]
    )
    sums = swap(sums, planes)
    (input_grads,) = call(
        input_grads_kernel,
        [((2, EDGE, EDGE, WIDE), BF16)],
        [
            vmem((44, EDGE, WIDE), F32),
            vmem((2, 10 * ROWS, PADDED), F32),
            vmem((3, 10, 16, PADDED), BF16),
            vmem((512, 2304), BF16),
        ],
        [me, near_nb, pre_grads, occupied, near, longer, shorter, kept, first_flipped],
        scalars=2,
        flops=2**28,
    )
    first_grads, second_grads = call(
        unpack_kernel,
        [((64, 27 * 64), F32), ((64, 27 * 64), F32)],
        [
            vmem((64, 27 * 64), F32),
            vmem((64, 27 * 64), F32),
            vmem((128, PACKED), F32),
            pltpu.SemaphoreType.DMA((2,)),
        ],
        [sums],
        leaving=True,
    )
    return input_grads, first_grads.T, second_grads.T


def solution(mesh):
    in_specs = (
        P(("grp", "dev"), None, None, None),
        P(("grp", "dev"), None, None),
        P(("grp", "dev"), None),
        P(),
        P(),
        P(("grp", "dev"), None, None, None),
    )
    out_specs = (P(("grp", "dev"), None, None, None), P(), P())
    return jax.shard_map(
        per_device, mesh=mesh, in_specs=in_specs, out_specs=out_specs, check_vma=False
    )
```

```python
import functools
import math

import jax
import jax.numpy as jnp
from jax import lax
from jax.experimental import pallas as pl
from jax.experimental.pallas import tpu as pltpu
from jax.sharding import PartitionSpec as P

AXES = ("grp", "dev")
EDGE = 8
WIDE = 512
PADDED = 640
ROWS = 24
PACKED = 1792
BF16 = jnp.bfloat16
F32 = jnp.float32


def directions():
    result = []
    for along_x in (-1, 0, 1):
        for along_y in (-1, 0, 1):
            for along_z in (-1, 0, 1):
                if along_x != 0 or along_y != 0 or along_z != 0:
                    result.append((along_x, along_y, along_z))
    return result


DIRECTIONS = directions()
NUMBER = {offset: number for number, offset in enumerate(DIRECTIONS)}


def locate(nb_ref, me, brick, number):
    other = nb_ref[brick, number]
    present = other >= 0
    owner = jnp.maximum(other, 0) >> 1
    return present, owner & 3, (owner >> 2) - (me >> 2), owner == me, other & 1


def send_place(nb_ref, me, brick, number):
    present, member, up, own, slot = locate(nb_ref, me, brick, number)
    relayed = (up > 0) | ((up < 0) & (member != (me & 3)))
    place = jnp.where(own, 32, member * 8 + jnp.where(relayed, 4, 0))
    return jnp.where(present, place + brick * 2 + slot, 32)


def take_place(nb_ref, me, brick, number):
    present, member, up, own, slot = locate(nb_ref, me, brick, number)
    longer = (up < 0) == ((me & 3) < 2)
    relayed = jnp.where(longer, 16 + 4 * member, 32 + 4 * (member & 1))
    place = jnp.where(up == 0, 4 * member, relayed)
    return present, jnp.where(own, 40, place) + slot * 2 + brick


def face_kind(offset):
    for axis in range(3):
        if offset[axis] != 0:
            return axis, 1 if offset[axis] > 0 else 0


def face_values(wide, index):
    faces = {}
    for side, at in ((0, 0), (1, EDGE - 1)):
        faces[0, side] = wide[index, at * EDGE : (at + 1) * EDGE, :]
        faces[1, side] = jnp.concatenate(
            [wide[index, x * EDGE + at : x * EDGE + at + 1, :] for x in range(EDGE)], axis=0
        )
        faces[2, side] = jnp.concatenate(
            [
                wide[index, x * EDGE : (x + 1) * EDGE, at * 64 : (at + 1) * 64]
                for x in range(EDGE)
            ],
            axis=1,
        )
    return faces


def spread(occ_ref):
    rows = []
    for x in range(EDGE):
        for brick in range(2):
            rows.append(jnp.broadcast_to(occ_ref[brick, x : x + 1, :].astype(F32), (EDGE, 64)))
    stacked = jnp.concatenate(rows, axis=0)
    row = lax.broadcasted_iota(jnp.int32, stacked.shape, 0)
    lane = lax.broadcasted_iota(jnp.int32, stacked.shape, 1)
    own = jnp.where((row & 7) == (lane >> 3), stacked, 0.0).astype(BF16)
    source = lax.broadcasted_iota(jnp.int32, (64, WIDE), 0)
    target = lax.broadcasted_iota(jnp.int32, (64, WIDE), 1)
    select = jnp.where((source & 7) == (target >> 6), 1.0, 0.0).astype(BF16)
    return jnp.dot(own, select, preferred_element_type=F32)


def pack_kernel(
    me_ref,
    nb_hbm,
    x_hbm,
    g_hbm,
    occ_hbm,
    near_ref,
    kept_ref,
    masked_ref,
    x_ref,
    g_ref,
    occ_ref,
    wide,
    boxes,
    nb_ref,
    sems,
):
    copies = [
        pltpu.make_async_copy(source, target, sems.at[number])
        for number, (source, target) in enumerate(
            ((occ_hbm, occ_ref), (g_hbm, g_ref), (x_hbm, x_ref), (nb_hbm, nb_ref))
        )
    ]
    for copy in copies:
        copy.start()
    me = me_ref[0]
    copies[0].wait()
    occupied = spread(occ_ref)
    copies[1].wait()
    copies[2].wait()
    for x in range(EDGE):
        both = []
        for brick in range(2):
            wide[brick, x * EDGE : (x + 1) * EDGE, :] = x_ref[brick, x].astype(F32)
            at = (2 * x + brick) * EDGE
            piece = g_ref[brick, x].astype(F32) * occupied[at : at + EDGE]
            wide[2 + brick, x * EDGE : (x + 1) * EDGE, :] = piece
            both.append(piece)
        masked_ref[x] = jnp.concatenate(both, axis=0).astype(BF16)
    copies[3].wait()
    for brick in range(2):
        first = face_values(wide, brick)
        second = face_values(wide, 2 + brick)
        packets = {}
        for key in first:
            packets[key] = jnp.concatenate([first[key], second[key]], axis=0).astype(BF16)
        for number, offset in enumerate(DIRECTIONS):
            boxes[send_place(nb_ref, me, brick, number)] = packets[face_kind(offset)]
    near_ref[...] = boxes[0:32].reshape(4, 128, WIDE)
    kept_ref[...] = boxes[32:36]


def route_kernel(me_ref, near_ref, longer_ref, shorter_ref):
    size = longer_ref.shape[1]
    own = me_ref[0] & 3
    longer_ref[...] = near_ref[:, size : 2 * size, :]
    for number in range(2):
        shorter_ref[number] = near_ref[(own & 2) + number, size : 2 * size, :]

    @pl.when(own >= 2)
    def _():
        longer_ref[own] = near_ref[own, 0:size, :]

    @pl.when(own < 2)
    def _():
        shorter_ref[own & 1] = near_ref[own, 0:size, :]


def beside(low, middle, high):
    return jnp.concatenate([low, middle, high], axis=1)


def fill_padded(padded, own, pick):
    def planes(along_x, along_y):
        return (
            pick((along_x, along_y, -1))[:, WIDE - 64 :],
            pick((along_x, along_y, 0)),
            pick((along_x, along_y, 1))[:, :64],
        )

    below, above = pick((0, 0, -1)), pick((0, 0, 1))
    for x in range(EDGE):
        lanes = slice(x * 64, (x + 1) * 64)
        start = (x + 1) * ROWS + 8
        padded[start : start + EDGE, :] = beside(below[:, lanes], own(x), above[:, lanes])
    for along_y, row in ((-1, 7), (1, 16)):
        value = beside(*planes(0, along_y))
        for x in range(EDGE):
            start = (x + 1) * ROWS + row
            padded[start : start + 1, :] = value[x : x + 1]
    for along_x, at in ((-1, 0), (1, 9)):
        start = at * ROWS + 8
        padded[start : start + EDGE, :] = beside(*planes(along_x, 0))
        for along_y, row, source in ((-1, 7, 7), (1, 16, 0)):
            value = beside(*planes(along_x, along_y))
            padded[at * ROWS + row : at * ROWS + row + 1, :] = value[source : source + 1]


def fill_windows(first, second, shifted, windows):
    for along_y in range(3):
        for x in range(10):
            start = x * ROWS + 7 + along_y
            shifted[along_y, x] = jnp.concatenate(
                [first[start : start + EDGE, :], second[start : start + EDGE, :]], axis=0
            ).astype(BF16)
    for pair in range(4):
        for along_y in range(3):
            windows[pair * 160 : (pair + 1) * 160, along_y * 256 : along_y * 256 + 256] = shifted[
                along_y, :, :, pair * 128 : pair * 128 + 256
            ].reshape(160, 256)


def add_shifted(product):
    pairs = []
    for pair in range(4):
        total = None
        for along_x in range(3):
            at = pair * 160 + along_x * 16
            part = product[at : at + 128, along_x * 128 : along_x * 128 + 128]
            total = part if total is None else total + part
        pairs.append(total)
    return jnp.concatenate(pairs, axis=0)


def fill_direct(kernel_ref, direct):
    for group in range(9):
        block = kernel_ref[group * 192 : (group + 1) * 192, :]
        none = jnp.zeros((64, 64), BF16)
        along_x, along_y = group // 3, group % 3
        direct[
            along_y * 256 : along_y * 256 + 256, along_x * 128 : along_x * 128 + 128
        ] = jnp.concatenate(
            [
                jnp.concatenate([block, none], axis=0),
                jnp.concatenate([none, block], axis=0),
            ],
            axis=1,
        )


def fill_flipped(kernel_ref, flipped):
    none = jnp.zeros((64, 64), BF16)
    for group in range(9):
        base = 3 * (8 - group)
        blocks = [kernel_ref[(base + z) * 64 : (base + z + 1) * 64, :] for z in (2, 1, 0)]
        row = group // 3 * 128
        lanes = slice(group % 3 * 256, group % 3 * 256 + 256)
        flipped[row : row + 64, lanes] = jnp.concatenate(blocks + [none], axis=1)
        flipped[row + 64 : row + 128, lanes] = jnp.concatenate([none] + blocks, axis=1)


def spread_kernel(
    first_ref,
    second_ref,
    occ_ref,
    nb_ref,
    direct_ref,
    flipped_ref,
    first_flipped_ref,
    occupied_ref,
    near_nb_ref,
):
    near_nb_ref[...] = nb_ref[...]
    occupied_ref[...] = spread(occ_ref)
    fill_direct(first_ref, direct_ref)
    fill_flipped(second_ref, flipped_ref)
    fill_flipped(first_ref, first_flipped_ref)


def times_flipped(windows, flipped):
    return lax.dot_general(
        windows, flipped, (((1,), (1,)), ((), ())), preferred_element_type=F32
    )


def paired(natural):
    return jnp.concatenate([natural[:, p * 128 : (p + 1) * 128] for p in range(4)], axis=0)


def unpaired(value):
    return jnp.concatenate([value[p * 128 : (p + 1) * 128] for p in range(4)], axis=1)


def gather_blocks(product):
    pieces = []
    for group in range(9):
        at = group * 256
        pieces.append(product[0:64, at : at + 192] + product[64:128, at + 64 : at + 256])
    pieces.append(jnp.zeros((64, PACKED - 27 * 64), F32))
    return jnp.concatenate(pieces, axis=1)


def tile_place(chunk, tile):
    row, lane = EDGE * (tile // 4), 128 * (tile % 4)
    if row < 96:
        return 32 * chunk + row % 32, WIDE * (row // 32) + lane
    return 32 * chunk + row - 96 + 16 * (lane // 256), 3 * WIDE + lane % 256


def main_kernel(
    me_ref,
    nb_ref,
    x_ref,
    masked_ref,
    occupied_ref,
    near_ref,
    longer_ref,
    shorter_ref,
    kept_in,
    direct,
    flipped,
    grads_ref,
    out_ref,
    kept_ref,
    taken,
    padded,
    shifted,
    windows,
    product,
    wide,
    boxes,
):
    me = me_ref[0]
    for member in range(4):
        at = 4 * member
        taken[at : at + 4] = near_ref[member, 0:64, :].reshape(4, 16, WIDE)
        taken[at + 16 : at + 20] = longer_ref[member].reshape(4, 16, WIDE)
    for number in range(2):
        taken[32 + 4 * number : 36 + 4 * number] = shorter_ref[number].reshape(4, 16, WIDE)
    taken[40:44] = kept_in[...]
    for brick in range(2):
        values = {}
        for number, offset in enumerate(DIRECTIONS):
            present, place = take_place(nb_ref, me, brick, number)
            values[offset] = jnp.where(present, taken[place].astype(F32), 0.0)

        def own_first(x):
            return x_ref[brick, x].astype(F32)

        def own_second(x):
            return masked_ref[x].astype(F32)[brick * EDGE : (brick + 1) * EDGE]

        fill_padded(padded.at[0, brick], own_first, lambda offset: values[offset][0:8])
        fill_padded(padded.at[1, brick], own_second, lambda offset: values[offset][8:16])
    for field in range(2):
        fill_windows(padded.at[field, 0], padded.at[field, 1], shifted.at[field], windows.at[field])
    occupied = paired(occupied_ref[...])
    pre_act = add_shifted(jnp.dot(windows[0], direct[...], preferred_element_type=F32))
    logistic = 1.0 / (1.0 + jnp.exp(-pre_act))
    hidden = (pre_act * logistic * occupied).astype(BF16)
    slope = logistic * (1.0 + pre_act * (1.0 - logistic))
    hidden_grad = add_shifted(times_flipped(windows[1], flipped[...]))
    pre_grads = (hidden_grad * slope * occupied).astype(BF16)

    natural = unpaired(pre_grads.astype(F32))
    for x in range(EDGE):
        grads_ref[x] = natural[16 * x : 16 * x + 16].astype(BF16)
        for brick in range(2):
            at = 16 * x + EDGE * brick
            wide[brick, x * EDGE : (x + 1) * EDGE, :] = natural[at : at + EDGE]
    for brick in range(2):
        faces = face_values(wide, brick)
        for number, offset in enumerate(DIRECTIONS):
            boxes[send_place(nb_ref, me, brick, number)] = faces[face_kind(offset)]
    for member in range(4):
        out_ref[member, 0:64, :] = (
            boxes[8 * member : 8 * member + 8].reshape(64, WIDE).astype(BF16)
        )
    kept_ref[...] = boxes[32:36]

    for half, own, field in ((0, hidden, 1), (1, pre_grads, 0)):
        turned = own.astype(F32).T.astype(BF16)
        for along_x in range(3):
            rows = [160 * pair + 16 * along_x for pair in range(4)]
            moved = jnp.concatenate([windows[field, at : at + 128, :] for at in rows], axis=0)
            product[:, along_x * 768 : along_x * 768 + 768] = jnp.dot(
                turned, moved, preferred_element_type=F32
            )
        packed = gather_blocks(product).astype(BF16)
        for chunk in range(2):
            start = 32 * chunk
            for part in range(3):
                at = 64 + 32 * part
                out_ref[2 * half + chunk, at : at + 32, :] = packed[
                    start : start + 32, part * WIDE : (part + 1) * WIDE
                ]
            rest = packed[start : start + 32, 3 * WIDE :]
            out_ref[2 * half + chunk, 160:176, :] = jnp.concatenate(
                [rest[0:16], rest[16:32]], axis=1
            )


def first_sum_kernel(parts_ref, pieces_ref):
    total = parts_ref[0, 64:176, :].astype(F32)
    for member in range(1, 4):
        total = total + parts_ref[member, 64:176, :].astype(F32)
    count = pieces_ref.shape[1]
    for tile in range(56):
        row, lane = EDGE * (tile // 4), 128 * (tile % 4)
        pieces_ref[tile // count, tile % count] = total[
            row : row + EDGE, lane : lane + 128
        ].astype(BF16)


def next_sum_kernel(scaling, parts_ref, copies_ref):
    total = parts_ref[0].astype(F32)
    for member in range(1, parts_ref.shape[0]):
        total = total + parts_ref[member].astype(F32)
    total = total * scaling
    for member in range(copies_ref.shape[0]):
        copies_ref[member] = total.astype(copies_ref.dtype)


def last_kernel(
    me_ref,
    nb_ref,
    grads_ref,
    occupied_ref,
    near_ref,
    longer_ref,
    shorter_ref,
    kept_ref,
    flipped,
    parts_ref,
    out_hbm,
    first_hbm,
    second_hbm,
    out_ref,
    first_out,
    second_out,
    halves,
    taken,
    padded,
    shifted,
    windows,
    sems,
):
    count = parts_ref.shape[1]
    for chunk in (2, 3, 0, 1):
        for tile in range(56):
            row, lane = tile_place(chunk, tile)
            halves[row : row + EDGE, lane : lane + 128] = parts_ref[
                4 * (tile // count) + chunk, tile % count
            ].astype(F32)
    first_out[...] = halves[64:128, : 27 * 64]
    first_copy = pltpu.make_async_copy(first_out, first_hbm, sems.at[0])
    first_copy.start()
    blocks = []
    for pair in range(14):
        turned = halves[0:64, pair * 128 : pair * 128 + 128].T
        blocks += [turned[0:64], turned[64:128]]
    second_out[...] = jnp.concatenate(blocks[26::-1], axis=1)
    second_copy = pltpu.make_async_copy(second_out, second_hbm, sems.at[1])
    second_copy.start()

    me = me_ref[0]
    for member in range(4):
        at = 4 * member
        taken[at : at + 4] = near_ref[member, 0:32, :].astype(F32).reshape(4, EDGE, WIDE)
        taken[at + 16 : at + 20] = longer_ref[member].astype(F32).reshape(4, EDGE, WIDE)
    for number in range(2):
        taken[32 + 4 * number : 36 + 4 * number] = (
            shorter_ref[number].astype(F32).reshape(4, EDGE, WIDE)
        )
    taken[40:44] = kept_ref[...]
    for brick in range(2):
        values = {}
        for number, offset in enumerate(DIRECTIONS):
            present, place = take_place(nb_ref, me, brick, number)
            values[offset] = jnp.where(present, taken[place], 0.0)

        def own(x):
            return grads_ref[x].astype(F32)[brick * EDGE : (brick + 1) * EDGE]

        fill_padded(padded.at[brick], own, lambda offset: values[offset])
    fill_windows(padded.at[0], padded.at[1], shifted, windows)
    result = unpaired(add_shifted(times_flipped(windows[...], flipped[...]))) * occupied_ref[...]
    for x in range(EDGE):
        for brick in range(2):
            at = 16 * x + EDGE * brick
            out_ref[brick, x] = result[at : at + EDGE].astype(BF16)
    out_copy = pltpu.make_async_copy(out_ref, out_hbm, sems.at[2])
    out_copy.start()
    first_copy.wait()
    second_copy.wait()
    out_copy.wait()


def call(kernel, shapes, scratch, arguments, scalars=0, outside=0, leaving=False, megabytes=40, flops=0):
    specs = [pl.BlockSpec(memory_space=pltpu.SMEM)] * scalars
    specs += [pl.BlockSpec(memory_space=pltpu.HBM)] * outside
    specs += [pl.BlockSpec(memory_space=pltpu.VMEM)] * (len(arguments) - len(specs))
    return pl.pallas_call(
        kernel,
        out_shape=[jax.ShapeDtypeStruct(shape, kind) for shape, kind in shapes],
        in_specs=specs,
        out_specs=[pl.BlockSpec(memory_space=pltpu.HBM if leaving else pltpu.VMEM)] * len(shapes),
        scratch_shapes=scratch,
        cost_estimate=pl.CostEstimate(flops=flops, bytes_accessed=2**19, transcendentals=0),
        compiler_params=pltpu.CompilerParams(vmem_limit_bytes=megabytes * 2**20),
    )(*arguments)


def per_device(inputs, occupancy, neighbours, first_kernel, second_kernel, out_grads):
    along_grp, along_dev = lax.axis_size("grp"), lax.axis_size("dev")
    devices = along_grp * along_dev
    scaling = 1.0 / math.sqrt(inputs.shape[0] * devices * EDGE**3)
    fours = [[4 * row + member for member in range(4)] for row in range(devices // 4)]
    rows = along_dev // 4
    stacks = [
        [along_dev * grp + 4 * row + member for row in range(rows)]
        for grp in range(along_grp)
        for member in range(4)
    ]
    planes = [
        [along_dev * grp + 4 * row + member for grp in range(along_grp) for member in range(4)]
        for row in range(rows)
    ]
    me = (lax.axis_index("grp") * along_dev + lax.axis_index("dev")).reshape(1)
    vmem = pltpu.VMEM

    def swap(value, members):
        return lax.all_to_all(value, AXES, 0, 0, axis_index_groups=members, tiled=True)

    longer_way = [(i, i + 4 if i & 2 == 0 else i - 4) for i in range(devices)]
    shorter_way = [(i, i - 4 if i & 2 == 0 else i + 4) for i in range(devices)]

    def send_on(near, size):
        longer, shorter = call(
            route_kernel,
            [((4, size, WIDE), BF16), ((2, size, WIDE), BF16)],
            [],
            [me, near],
            scalars=1,
        )
        return [
            lax.ppermute(value, AXES, [(i, j) for i, j in way if 0 <= j < devices])
            for value, way in ((longer, longer_way), (shorter, shorter_way))
        ]

    near, kept, masked = call(
        pack_kernel,
        [
            ((4, 128, WIDE), BF16),
            ((4, 16, WIDE), BF16),
            ((EDGE, 16, WIDE), BF16),
        ],
        [
            vmem((2, EDGE, EDGE, WIDE), BF16),
            vmem((2, EDGE, EDGE, WIDE), BF16),
            vmem((2, EDGE, 64), jnp.int32),
            vmem((4, 64, WIDE), F32),
            vmem((36, 16, WIDE), BF16),
            pltpu.SMEM((2, 26), jnp.int32),
            pltpu.SemaphoreType.DMA((4,)),
        ],
        [me, neighbours, inputs, out_grads, occupancy],
        scalars=1,
        outside=4,
        megabytes=60,
    )
    near = swap(near, fours)
    longer, shorter = send_on(near, 64)
    direct, flipped, first_flipped, occupied, near_nb = call(
        spread_kernel,
        [
            ((768, 384), BF16),
            ((384, 768), BF16),
            ((384, 768), BF16),
            ((128, WIDE), F32),
            ((2, 26), jnp.int32),
        ],
        [],
        [first_kernel, second_kernel, occupancy, neighbours],
    )
    pre_grads, near, kept = call(
        main_kernel,
        [((EDGE, 16, WIDE), BF16), ((4, 176, WIDE), BF16), ((4, EDGE, WIDE), F32)],
        [
            vmem((44, 16, WIDE), BF16),
            vmem((2, 2, 10 * ROWS, PADDED), F32),
            vmem((2, 3, 10, 16, PADDED), BF16),
            vmem((2, 640, 768), BF16),
            vmem((128, 2304), F32),
            vmem((2, 64, WIDE), F32),
            vmem((36, EDGE, WIDE), F32),
        ],
        [me, near_nb, inputs, masked, occupied, near, longer, shorter, kept, direct, flipped],
        scalars=2,
        flops=2**30,
    )
    near = swap(near, fours)
    longer, shorter = send_on(near, 32)
    piece = (56 // along_grp, EDGE, 128)
    (sums,) = call(first_sum_kernel, [((along_grp,) + piece, BF16)], [], [near])
    sums = lax.all_to_all(sums, "grp", 0, 0, tiled=True)
    (sums,) = call(functools.partial(next_sum_kernel, 1.0), [((rows,) + piece, BF16)], [], [sums])
    sums = swap(sums, stacks)
    (sums,) = call(
        functools.partial(next_sum_kernel, scaling), [((4 * along_grp,) + piece, BF16)], [], [sums]
    )
    sums = swap(sums, planes)
    input_grads, first_grads, second_grads = call(
        last_kernel,
        [((2, EDGE, EDGE, WIDE), BF16), ((64, 27 * 64), F32), ((64, 27 * 64), F32)],
        [
            vmem((2, EDGE, EDGE, WIDE), BF16),
            vmem((64, 27 * 64), F32),
            vmem((64, 27 * 64), F32),
            vmem((128, PACKED), F32),
            vmem((44, EDGE, WIDE), F32),
            vmem((2, 10 * ROWS, PADDED), F32),
            vmem((3, 10, 16, PADDED), BF16),
            vmem((640, 768), BF16),
            pltpu.SemaphoreType.DMA((3,)),
        ],
        [
            me,
            near_nb,
            pre_grads,
            occupied,
            near,
            longer,
            shorter,
            kept,
            first_flipped,
            sums,
        ],
        scalars=2,
        leaving=True,
        flops=2**28,
    )
    return input_grads, first_grads.T, second_grads.T


def solution(mesh):
    in_specs = (
        P(("grp", "dev"), None, None, None),
        P(("grp", "dev"), None, None),
        P(("grp", "dev"), None),
        P(),
        P(),
        P(("grp", "dev"), None, None, None),
    )
    out_specs = (P(("grp", "dev"), None, None, None), P(), P())
    return jax.shard_map(
        per_device, mesh=mesh, in_specs=in_specs, out_specs=out_specs, check_vma=False
    )
```

```python
import functools
import math

import jax
import jax.numpy as jnp
from jax import lax
from jax.experimental import pallas as pl
from jax.experimental.pallas import tpu as pltpu
from jax.sharding import PartitionSpec as P

AXES = ("grp", "dev")
EDGE = 8
WIDE = 512
PADDED = 640
ROWS = 24
PACKED = 1792
BF16 = jnp.bfloat16
F32 = jnp.float32


def directions():
    result = []
    for along_x in (-1, 0, 1):
        for along_y in (-1, 0, 1):
            for along_z in (-1, 0, 1):
                if along_x != 0 or along_y != 0 or along_z != 0:
                    result.append((along_x, along_y, along_z))
    return result


DIRECTIONS = directions()
NUMBER = {offset: number for number, offset in enumerate(DIRECTIONS)}


def locate(nb_ref, me, brick, number):
    other = nb_ref[brick, number]
    present = other >= 0
    owner = jnp.maximum(other, 0) >> 1
    return present, owner & 3, (owner >> 2) - (me >> 2), owner == me, other & 1


def send_place(nb_ref, me, brick, number):
    present, member, up, own, slot = locate(nb_ref, me, brick, number)
    relayed = (up > 0) | ((up < 0) & (member != (me & 3)))
    place = jnp.where(own, 32, member * 8 + jnp.where(relayed, 4, 0))
    return jnp.where(present, place + brick * 2 + slot, 32)


def take_place(nb_ref, me, brick, number):
    present, member, up, own, slot = locate(nb_ref, me, brick, number)
    longer = (up < 0) == ((me & 3) < 2)
    relayed = jnp.where(longer, 16 + 4 * member, 32 + 4 * (member & 1))
    place = jnp.where(up == 0, 4 * member, relayed)
    return present, jnp.where(own, 40, place) + slot * 2 + brick


def face_kind(offset):
    for axis in range(3):
        if offset[axis] != 0:
            return axis, 1 if offset[axis] > 0 else 0


def face_values(wide, index):
    faces = {}
    for side, at in ((0, 0), (1, EDGE - 1)):
        faces[0, side] = wide[index, at * EDGE : (at + 1) * EDGE, :]
        faces[1, side] = jnp.concatenate(
            [wide[index, x * EDGE + at : x * EDGE + at + 1, :] for x in range(EDGE)], axis=0
        )
        faces[2, side] = jnp.concatenate(
            [
                wide[index, x * EDGE : (x + 1) * EDGE, at * 64 : (at + 1) * 64]
                for x in range(EDGE)
            ],
            axis=1,
        )
    return faces


def spread(occ_ref):
    rows = []
    for x in range(EDGE):
        for brick in range(2):
            rows.append(jnp.broadcast_to(occ_ref[brick, x : x + 1, :].astype(F32), (EDGE, 64)))
    stacked = jnp.concatenate(rows, axis=0)
    row = lax.broadcasted_iota(jnp.int32, stacked.shape, 0)
    lane = lax.broadcasted_iota(jnp.int32, stacked.shape, 1)
    own = jnp.where((row & 7) == (lane >> 3), stacked, 0.0).astype(BF16)
    source = lax.broadcasted_iota(jnp.int32, (64, WIDE), 0)
    target = lax.broadcasted_iota(jnp.int32, (64, WIDE), 1)
    select = jnp.where((source & 7) == (target >> 6), 1.0, 0.0).astype(BF16)
    return jnp.dot(own, select, preferred_element_type=F32)


def pack_kernel(
    me_ref,
    nb_hbm,
    x_hbm,
    g_hbm,
    occ_hbm,
    near_ref,
    kept_ref,
    masked_ref,
    x_ref,
    g_ref,
    occ_ref,
    wide,
    boxes,
    nb_ref,
    sems,
):
    copies = [
        pltpu.make_async_copy(source, target, sems.at[number])
        for number, (source, target) in enumerate(
            ((occ_hbm, occ_ref), (g_hbm, g_ref), (x_hbm, x_ref), (nb_hbm, nb_ref))
        )
    ]
    for copy in copies:
        copy.start()
    me = me_ref[0]
    copies[0].wait()
    occupied = spread(occ_ref)
    copies[1].wait()
    copies[2].wait()
    for x in range(EDGE):
        both = []
        for brick in range(2):
            wide[brick, x * EDGE : (x + 1) * EDGE, :] = x_ref[brick, x].astype(F32)
            at = (2 * x + brick) * EDGE
            piece = g_ref[brick, x].astype(F32) * occupied[at : at + EDGE]
            wide[2 + brick, x * EDGE : (x + 1) * EDGE, :] = piece
            both.append(piece)
        masked_ref[x] = jnp.concatenate(both, axis=0).astype(BF16)
    copies[3].wait()
    for brick in range(2):
        first = face_values(wide, brick)
        second = face_values(wide, 2 + brick)
        packets = {}
        for key in first:
            packets[key] = jnp.concatenate([first[key], second[key]], axis=0).astype(BF16)
        for number, offset in enumerate(DIRECTIONS):
            boxes[send_place(nb_ref, me, brick, number)] = packets[face_kind(offset)]
    near_ref[...] = boxes[0:32].reshape(4, 128, WIDE)
    kept_ref[...] = boxes[32:36]


def route_kernel(me_ref, near_ref, longer_ref, shorter_ref):
    size = longer_ref.shape[1]
    own = me_ref[0] & 3
    longer_ref[...] = near_ref[:, size : 2 * size, :]
    for number in range(2):
        shorter_ref[number] = near_ref[(own & 2) + number, size : 2 * size, :]

    @pl.when(own >= 2)
    def _():
        longer_ref[own] = near_ref[own, 0:size, :]

    @pl.when(own < 2)
    def _():
        shorter_ref[own & 1] = near_ref[own, 0:size, :]


def beside(low, middle, high):
    return jnp.concatenate([low, middle, high], axis=1)


def fill_padded(padded, own, pick):
    def planes(along_x, along_y):
        return (
            pick((along_x, along_y, -1))[:, WIDE - 64 :],
            pick((along_x, along_y, 0)),
            pick((along_x, along_y, 1))[:, :64],
        )

    below, above = pick((0, 0, -1)), pick((0, 0, 1))
    for x in range(EDGE):
        lanes = slice(x * 64, (x + 1) * 64)
        start = (x + 1) * ROWS + 8
        padded[start : start + EDGE, :] = beside(below[:, lanes], own(x), above[:, lanes])
    for along_y, row in ((-1, 7), (1, 16)):
        value = beside(*planes(0, along_y))
        for x in range(EDGE):
            start = (x + 1) * ROWS + row
            padded[start : start + 1, :] = value[x : x + 1]
    for along_x, at in ((-1, 0), (1, 9)):
        start = at * ROWS + 8
        padded[start : start + EDGE, :] = beside(*planes(along_x, 0))
        for along_y, row, source in ((-1, 7, 7), (1, 16, 0)):
            value = beside(*planes(along_x, along_y))
            padded[at * ROWS + row : at * ROWS + row + 1, :] = value[source : source + 1]


def fill_windows(first, second, shifted, windows):
    for along_y in range(3):
        for x in range(10):
            start = x * ROWS + 7 + along_y
            shifted[along_y, x] = jnp.concatenate(
                [first[start : start + EDGE, :], second[start : start + EDGE, :]], axis=0
            ).astype(BF16)
    for pair in range(4):
        for along_y in range(3):
            windows[pair * 160 : (pair + 1) * 160, along_y * 256 : along_y * 256 + 256] = shifted[
                along_y, :, :, pair * 128 : pair * 128 + 256
            ].reshape(160, 256)


def add_shifted(product):
    pairs = []
    for pair in range(4):
        total = None
        for along_x in range(3):
            at = pair * 160 + along_x * 16
            part = product[at : at + 128, along_x * 128 : along_x * 128 + 128]
            total = part if total is None else total + part
        pairs.append(total)
    return jnp.concatenate(pairs, axis=0)


def fill_direct(kernel_ref, direct):
    for group in range(9):
        block = kernel_ref[group * 192 : (group + 1) * 192, :]
        none = jnp.zeros((64, 64), BF16)
        along_x, along_y = group // 3, group % 3
        direct[
            along_y * 256 : along_y * 256 + 256, along_x * 128 : along_x * 128 + 128
        ] = jnp.concatenate(
            [
                jnp.concatenate([block, none], axis=0),
                jnp.concatenate([none, block], axis=0),
            ],
            axis=1,
        )


def fill_flipped(kernel_ref, flipped):
    none = jnp.zeros((64, 64), BF16)
    for group in range(9):
        base = 3 * (8 - group)
        blocks = [kernel_ref[(base + z) * 64 : (base + z + 1) * 64, :] for z in (2, 1, 0)]
        row = group // 3 * 128
        lanes = slice(group % 3 * 256, group % 3 * 256 + 256)
        flipped[row : row + 64, lanes] = jnp.concatenate(blocks + [none], axis=1)
        flipped[row + 64 : row + 128, lanes] = jnp.concatenate([none] + blocks, axis=1)


def spread_kernel(
    first_ref,
    second_ref,
    occ_ref,
    nb_ref,
    direct_ref,
    flipped_ref,
    first_flipped_ref,
    occupied_ref,
    near_nb_ref,
):
    near_nb_ref[...] = nb_ref[...]
    occupied_ref[...] = spread(occ_ref)
    fill_direct(first_ref, direct_ref)
    fill_flipped(second_ref, flipped_ref)
    fill_flipped(first_ref, first_flipped_ref)


def times_flipped(windows, flipped):
    return lax.dot_general(
        windows, flipped, (((1,), (1,)), ((), ())), preferred_element_type=F32
    )


def paired(natural):
    return jnp.concatenate([natural[:, p * 128 : (p + 1) * 128] for p in range(4)], axis=0)


def unpaired(value):
    return jnp.concatenate([value[p * 128 : (p + 1) * 128] for p in range(4)], axis=1)


def gather_blocks(product):
    pieces = []
    for group in range(9):
        at = group * 256
        pieces.append(product[0:64, at : at + 192] + product[64:128, at + 64 : at + 256])
    pieces.append(jnp.zeros((64, PACKED - 27 * 64), F32))
    return jnp.concatenate(pieces, axis=1)


def tile_place(chunk, tile):
    row, lane = EDGE * (tile // 4), 128 * (tile % 4)
    if row < 96:
        return 32 * chunk + row % 32, WIDE * (row // 32) + lane
    return 32 * chunk + row - 96 + 16 * (lane // 256), 3 * WIDE + lane % 256


def main_kernel(
    me_ref,
    nb_ref,
    x_ref,
    masked_ref,
    occupied_ref,
    near_ref,
    longer_ref,
    shorter_ref,
    kept_in,
    direct,
    flipped,
    grads_ref,
    out_ref,
    kept_ref,
    taken,
    padded,
    shifted,
    windows,
    product,
    wide,
    boxes,
):
    me = me_ref[0]
    for member in range(4):
        at = 4 * member
        taken[at : at + 4] = near_ref[member, 0:64, :].reshape(4, 16, WIDE)
        taken[at + 16 : at + 20] = longer_ref[member].reshape(4, 16, WIDE)
    for number in range(2):
        taken[32 + 4 * number : 36 + 4 * number] = shorter_ref[number].reshape(4, 16, WIDE)
    taken[40:44] = kept_in[...]
    for brick in range(2):
        values = {}
        for number, offset in enumerate(DIRECTIONS):
            present, place = take_place(nb_ref, me, brick, number)
            values[offset] = jnp.where(present, taken[place].astype(F32), 0.0)

        def own_first(x):
            return x_ref[brick, x].astype(F32)

        def own_second(x):
            return masked_ref[x].astype(F32)[brick * EDGE : (brick + 1) * EDGE]

        fill_padded(padded.at[0, brick], own_first, lambda offset: values[offset][0:8])
        fill_padded(padded.at[1, brick], own_second, lambda offset: values[offset][8:16])
    for field in range(2):
        fill_windows(padded.at[field, 0], padded.at[field, 1], shifted.at[field], windows.at[field])
    occupied = paired(occupied_ref[...])
    pre_act = add_shifted(jnp.dot(windows[0], direct[...], preferred_element_type=F32))
    logistic = 1.0 / (1.0 + jnp.exp(-pre_act))
    hidden = (pre_act * logistic * occupied).astype(BF16)
    slope = logistic * (1.0 + pre_act * (1.0 - logistic))
    hidden_grad = add_shifted(times_flipped(windows[1], flipped[...]))
    pre_grads = (hidden_grad * slope * occupied).astype(BF16)

    natural = unpaired(pre_grads.astype(F32))
    for x in range(EDGE):
        grads_ref[x] = natural[16 * x : 16 * x + 16].astype(BF16)
        for brick in range(2):
            at = 16 * x + EDGE * brick
            wide[brick, x * EDGE : (x + 1) * EDGE, :] = natural[at : at + EDGE]
    for brick in range(2):
        faces = face_values(wide, brick)
        for number, offset in enumerate(DIRECTIONS):
            boxes[send_place(nb_ref, me, brick, number)] = faces[face_kind(offset)]
    for member in range(4):
        out_ref[member, 0:64, :] = (
            boxes[8 * member : 8 * member + 8].reshape(64, WIDE).astype(BF16)
        )
    kept_ref[...] = boxes[32:36]

    for half, own, field in ((0, hidden, 1), (1, pre_grads, 0)):
        turned = own.astype(F32).T.astype(BF16)
        for along_x in range(3):
            rows = [160 * pair + 16 * along_x for pair in range(4)]
            moved = jnp.concatenate([windows[field, at : at + 128, :] for at in rows], axis=0)
            product[:, along_x * 768 : along_x * 768 + 768] = jnp.dot(
                turned, moved, preferred_element_type=F32
            )
        packed = gather_blocks(product).astype(BF16)
        for chunk in range(2):
            start = 32 * chunk
            for part in range(3):
                at = 64 + 32 * part
                out_ref[2 * half + chunk, at : at + 32, :] = packed[
                    start : start + 32, part * WIDE : (part + 1) * WIDE
                ]
            rest = packed[start : start + 32, 3 * WIDE :]
            out_ref[2 * half + chunk, 160:176, :] = jnp.concatenate(
                [rest[0:16], rest[16:32]], axis=1
            )


def first_sum_kernel(parts_ref, pieces_ref):
    total = parts_ref[0, 64:176, :].astype(F32)
    for member in range(1, 4):
        total = total + parts_ref[member, 64:176, :].astype(F32)
    count = pieces_ref.shape[1]
    for tile in range(56):
        row, lane = EDGE * (tile // 4), 128 * (tile % 4)
        pieces_ref[tile // count, tile % count] = total[
            row : row + EDGE, lane : lane + 128
        ].astype(BF16)


def next_sum_kernel(scaling, parts_ref, copies_ref):
    total = parts_ref[0].astype(F32)
    for member in range(1, parts_ref.shape[0]):
        total = total + parts_ref[member].astype(F32)
    total = total * scaling
    for member in range(copies_ref.shape[0]):
        copies_ref[member] = total.astype(copies_ref.dtype)


def input_grads_kernel(
    me_ref,
    nb_ref,
    grads_ref,
    occupied_ref,
    near_ref,
    longer_ref,
    shorter_ref,
    kept_ref,
    flipped,
    out_ref,
    taken,
    padded,
    shifted,
    windows,
):
    me = me_ref[0]
    for member in range(4):
        at = 4 * member
        taken[at : at + 4] = near_ref[member, 0:32, :].astype(F32).reshape(4, EDGE, WIDE)
        taken[at + 16 : at + 20] = longer_ref[member].astype(F32).reshape(4, EDGE, WIDE)
    for number in range(2):
        taken[32 + 4 * number : 36 + 4 * number] = (
            shorter_ref[number].astype(F32).reshape(4, EDGE, WIDE)
        )
    taken[40:44] = kept_ref[...]
    for brick in range(2):
        values = {}
        for number, offset in enumerate(DIRECTIONS):
            present, place = take_place(nb_ref, me, brick, number)
            values[offset] = jnp.where(present, taken[place], 0.0)

        def own(x):
            return grads_ref[x].astype(F32)[brick * EDGE : (brick + 1) * EDGE]

        fill_padded(padded.at[brick], own, lambda offset: values[offset])
    fill_windows(padded.at[0], padded.at[1], shifted, windows)
    result = unpaired(add_shifted(times_flipped(windows[...], flipped[...]))) * occupied_ref[...]
    for x in range(EDGE):
        for brick in range(2):
            at = 16 * x + EDGE * brick
            out_ref[brick, x] = result[at : at + EDGE].astype(BF16)


def unpack_kernel(parts_ref, first_hbm, second_hbm, first_out, second_out, halves, sems):
    count = parts_ref.shape[1]
    for chunk in (2, 3, 0, 1):
        for tile in range(56):
            row, lane = tile_place(chunk, tile)
            halves[row : row + EDGE, lane : lane + 128] = parts_ref[
                4 * (tile // count) + chunk, tile % count
            ].astype(F32)
    first_out[...] = halves[64:128, : 27 * 64]
    first_copy = pltpu.make_async_copy(first_out, first_hbm, sems.at[0])
    first_copy.start()
    blocks = []
    for pair in range(14):
        turned = halves[0:64, pair * 128 : pair * 128 + 128].T
        blocks += [turned[0:64], turned[64:128]]
    second_out[...] = jnp.concatenate(blocks[26::-1], axis=1)
    second_copy = pltpu.make_async_copy(second_out, second_hbm, sems.at[1])
    second_copy.start()
    first_copy.wait()
    second_copy.wait()


def call(kernel, shapes, scratch, arguments, scalars=0, outside=0, leaving=False, megabytes=40, flops=0):
    specs = [pl.BlockSpec(memory_space=pltpu.SMEM)] * scalars
    specs += [pl.BlockSpec(memory_space=pltpu.HBM)] * outside
    specs += [pl.BlockSpec(memory_space=pltpu.VMEM)] * (len(arguments) - len(specs))
    return pl.pallas_call(
        kernel,
        out_shape=[jax.ShapeDtypeStruct(shape, kind) for shape, kind in shapes],
        in_specs=specs,
        out_specs=[pl.BlockSpec(memory_space=pltpu.HBM if leaving else pltpu.VMEM)] * len(shapes),
        scratch_shapes=scratch,
        cost_estimate=pl.CostEstimate(flops=flops, bytes_accessed=2**19, transcendentals=0),
        compiler_params=pltpu.CompilerParams(vmem_limit_bytes=megabytes * 2**20),
    )(*arguments)


def per_device(inputs, occupancy, neighbours, first_kernel, second_kernel, out_grads):
    along_grp, along_dev = lax.axis_size("grp"), lax.axis_size("dev")
    devices = along_grp * along_dev
    scaling = 1.0 / math.sqrt(inputs.shape[0] * devices * EDGE**3)
    fours = [[4 * row + member for member in range(4)] for row in range(devices // 4)]
    rows = along_dev // 4
    stacks = [
        [along_dev * grp + 4 * row + member for row in range(rows)]
        for grp in range(along_grp)
        for member in range(4)
    ]
    planes = [
        [along_dev * grp + 4 * row + member for grp in range(along_grp) for member in range(4)]
        for row in range(rows)
    ]
    me = (lax.axis_index("grp") * along_dev + lax.axis_index("dev")).reshape(1)
    vmem = pltpu.VMEM

    def swap(value, members):
        return lax.all_to_all(value, AXES, 0, 0, axis_index_groups=members, tiled=True)

    longer_way = [(i, i + 4 if i & 2 == 0 else i - 4) for i in range(devices)]
    shorter_way = [(i, i - 4 if i & 2 == 0 else i + 4) for i in range(devices)]

    def send_on(near, size):
        longer, shorter = call(
            route_kernel,
            [((4, size, WIDE), BF16), ((2, size, WIDE), BF16)],
            [],
            [me, near],
            scalars=1,
        )
        return [
            lax.ppermute(value, AXES, [(i, j) for i, j in way if 0 <= j < devices])
            for value, way in ((longer, longer_way), (shorter, shorter_way))
        ]

    near, kept, masked = call(
        pack_kernel,
        [
            ((4, 128, WIDE), BF16),
            ((4, 16, WIDE), BF16),
            ((EDGE, 16, WIDE), BF16),
        ],
        [
            vmem((2, EDGE, EDGE, WIDE), BF16),
            vmem((2, EDGE, EDGE, WIDE), BF16),
            vmem((2, EDGE, 64), jnp.int32),
            vmem((4, 64, WIDE), F32),
            vmem((36, 16, WIDE), BF16),
            pltpu.SMEM((2, 26), jnp.int32),
            pltpu.SemaphoreType.DMA((4,)),
        ],
        [me, neighbours, inputs, out_grads, occupancy],
        scalars=1,
        outside=4,
        megabytes=60,
    )
    near = swap(near, fours)
    longer, shorter = send_on(near, 64)
    direct, flipped, first_flipped, occupied, near_nb = call(
        spread_kernel,
        [
            ((768, 384), BF16),
            ((384, 768), BF16),
            ((384, 768), BF16),
            ((128, WIDE), F32),
            ((2, 26), jnp.int32),
        ],
        [],
        [first_kernel, second_kernel, occupancy, neighbours],
    )
    pre_grads, near, kept = call(
        main_kernel,
        [((EDGE, 16, WIDE), BF16), ((4, 176, WIDE), BF16), ((4, EDGE, WIDE), F32)],
        [
            vmem((44, 16, WIDE), BF16),
            vmem((2, 2, 10 * ROWS, PADDED), F32),
            vmem((2, 3, 10, 16, PADDED), BF16),
            vmem((2, 640, 768), BF16),
            vmem((128, 2304), F32),
            vmem((2, 64, WIDE), F32),
            vmem((36, EDGE, WIDE), F32),
        ],
        [me, near_nb, inputs, masked, occupied, near, longer, shorter, kept, direct, flipped],
        scalars=2,
        flops=2**30,
    )
    near = swap(near, fours)
    longer, shorter = send_on(near, 32)
    piece = (56 // along_grp, EDGE, 128)
    (sums,) = call(first_sum_kernel, [((along_grp,) + piece, BF16)], [], [near])
    sums = lax.all_to_all(sums, "grp", 0, 0, tiled=True)
    (sums,) = call(functools.partial(next_sum_kernel, 1.0), [((rows,) + piece, BF16)], [], [sums])
    sums = swap(sums, stacks)
    (sums,) = call(
        functools.partial(next_sum_kernel, scaling), [((4 * along_grp,) + piece, BF16)], [], [sums]
    )
    sums = swap(sums, planes)
    (input_grads,) = call(
        input_grads_kernel,
        [((2, EDGE, EDGE, WIDE), BF16)],
        [
            vmem((44, EDGE, WIDE), F32),
            vmem((2, 10 * ROWS, PADDED), F32),
            vmem((3, 10, 16, PADDED), BF16),
            vmem((640, 768), BF16),
        ],
        [me, near_nb, pre_grads, occupied, near, longer, shorter, kept, first_flipped],
        scalars=2,
        flops=2**28,
    )
    first_grads, second_grads = call(
        unpack_kernel,
        [((64, 27 * 64), F32), ((64, 27 * 64), F32)],
        [
            vmem((64, 27 * 64), F32),
            vmem((64, 27 * 64), F32),
            vmem((128, PACKED), F32),
            pltpu.SemaphoreType.DMA((2,)),
        ],
        [sums],
        leaving=True,
    )
    return input_grads, first_grads.T, second_grads.T


def solution(mesh):
    in_specs = (
        P(("grp", "dev"), None, None, None),
        P(("grp", "dev"), None, None),
        P(("grp", "dev"), None),
        P(),
        P(),
        P(("grp", "dev"), None, None, None),
    )
    out_specs = (P(("grp", "dev"), None, None, None), P(), P())
    return jax.shard_map(
        per_device, mesh=mesh, in_specs=in_specs, out_specs=out_specs, check_vma=False
    )
```

```python
import functools
import math

import jax
import jax.numpy as jnp
from jax import lax
from jax.experimental import pallas as pl
from jax.experimental.pallas import tpu as pltpu
from jax.sharding import PartitionSpec as P

AXES = ("grp", "dev")
EDGE = 8
WIDE = 512
PADDED = 640
ROWS = 24
PACKED = 1792
BF16 = jnp.bfloat16
F32 = jnp.float32


def directions():
    result = []
    for along_x in (-1, 0, 1):
        for along_y in (-1, 0, 1):
            for along_z in (-1, 0, 1):
                if along_x != 0 or along_y != 0 or along_z != 0:
                    result.append((along_x, along_y, along_z))
    return result


DIRECTIONS = directions()
NUMBER = {offset: number for number, offset in enumerate(DIRECTIONS)}


def locate(nb_ref, me, brick, number):
    other = nb_ref[brick, number]
    present = other >= 0
    owner = jnp.maximum(other, 0) >> 1
    return present, owner & 3, (owner >> 2) - (me >> 2), owner == me, other & 1


def send_place(nb_ref, me, brick, number):
    present, member, up, own, slot = locate(nb_ref, me, brick, number)
    relayed = (up > 0) | ((up < 0) & (member != (me & 3)))
    place = jnp.where(own, 32, member * 8 + jnp.where(relayed, 4, 0))
    return jnp.where(present, place + brick * 2 + slot, 32)


def take_place(nb_ref, me, brick, number):
    present, member, up, own, slot = locate(nb_ref, me, brick, number)
    longer = (up < 0) == ((me & 3) < 2)
    relayed = jnp.where(longer, 16 + 4 * member, 32 + 4 * (member & 1))
    place = jnp.where(up == 0, 4 * member, relayed)
    return present, jnp.where(own, 40, place) + slot * 2 + brick


def face_kind(offset):
    for axis in range(3):
        if offset[axis] != 0:
            return axis, 1 if offset[axis] > 0 else 0


def face_values(wide, index):
    faces = {}
    for side, at in ((0, 0), (1, EDGE - 1)):
        faces[0, side] = wide[index, at * EDGE : (at + 1) * EDGE, :]
        faces[1, side] = jnp.concatenate(
            [wide[index, x * EDGE + at : x * EDGE + at + 1, :] for x in range(EDGE)], axis=0
        )
        faces[2, side] = jnp.concatenate(
            [
                wide[index, x * EDGE : (x + 1) * EDGE, at * 64 : (at + 1) * 64]
                for x in range(EDGE)
            ],
            axis=1,
        )
    return faces


def spread(occ_ref):
    rows = []
    for x in range(EDGE):
        for brick in range(2):
            rows.append(jnp.broadcast_to(occ_ref[brick, x : x + 1, :].astype(F32), (EDGE, 64)))
    stacked = jnp.concatenate(rows, axis=0)
    row = lax.broadcasted_iota(jnp.int32, stacked.shape, 0)
    lane = lax.broadcasted_iota(jnp.int32, stacked.shape, 1)
    own = jnp.where((row & 7) == (lane >> 3), stacked, 0.0).astype(BF16)
    source = lax.broadcasted_iota(jnp.int32, (64, WIDE), 0)
    target = lax.broadcasted_iota(jnp.int32, (64, WIDE), 1)
    select = jnp.where((source & 7) == (target >> 6), 1.0, 0.0).astype(BF16)
    return jnp.dot(own, select, preferred_element_type=F32)


def pack_kernel(
    me_ref,
    nb_hbm,
    x_hbm,
    g_hbm,
    occ_hbm,
    near_ref,
    kept_ref,
    masked_ref,
    x_ref,
    g_ref,
    occ_ref,
    wide,
    boxes,
    nb_ref,
    sems,
):
    copies = [
        pltpu.make_async_copy(source, target, sems.at[number])
        for number, (source, target) in enumerate(
            ((occ_hbm, occ_ref), (g_hbm, g_ref), (x_hbm, x_ref), (nb_hbm, nb_ref))
        )
    ]
    for copy in copies:
        copy.start()
    me = me_ref[0]
    copies[0].wait()
    occupied = spread(occ_ref)
    copies[1].wait()
    for x in range(EDGE):
        both = []
        for brick in range(2):
            at = (2 * x + brick) * EDGE
            piece = g_ref[brick, x].astype(F32) * occupied[at : at + EDGE]
            wide[2 + brick, x * EDGE : (x + 1) * EDGE, :] = piece
            both.append(piece)
        masked_ref[x] = jnp.concatenate(both, axis=0).astype(BF16)
    copies[2].wait()
    for brick in range(2):
        for x in range(EDGE):
            wide[brick, x * EDGE : (x + 1) * EDGE, :] = x_ref[brick, x].astype(F32)
    copies[3].wait()
    for brick in range(2):
        first = face_values(wide, brick)
        second = face_values(wide, 2 + brick)
        packets = {}
        for key in first:
            packets[key] = jnp.concatenate([first[key], second[key]], axis=0).astype(BF16)
        for number, offset in enumerate(DIRECTIONS):
            boxes[send_place(nb_ref, me, brick, number)] = packets[face_kind(offset)]
    near_ref[...] = boxes[0:32].reshape(4, 128, WIDE)
    kept_ref[...] = boxes[32:36]


def route_kernel(me_ref, near_ref, longer_ref, shorter_ref):
    size = longer_ref.shape[1]
    own = me_ref[0] & 3
    longer_ref[...] = near_ref[:, size : 2 * size, :]
    for number in range(2):
        shorter_ref[number] = near_ref[(own & 2) + number, size : 2 * size, :]

    @pl.when(own >= 2)
    def _():
        longer_ref[own] = near_ref[own, 0:size, :]

    @pl.when(own < 2)
    def _():
        shorter_ref[own & 1] = near_ref[own, 0:size, :]


def beside(low, middle, high):
    return jnp.concatenate([low, middle, high], axis=1)


def fill_padded(padded, own, pick):
    def planes(along_x, along_y):
        return (
            pick((along_x, along_y, -1))[:, WIDE - 64 :],
            pick((along_x, along_y, 0)),
            pick((along_x, along_y, 1))[:, :64],
        )

    below, above = pick((0, 0, -1)), pick((0, 0, 1))
    for x in range(EDGE):
        lanes = slice(x * 64, (x + 1) * 64)
        start = (x + 1) * ROWS + 8
        padded[start : start + EDGE, :] = beside(below[:, lanes], own(x), above[:, lanes])
    for along_y, row in ((-1, 7), (1, 16)):
        value = beside(*planes(0, along_y))
        for x in range(EDGE):
            start = (x + 1) * ROWS + row
            padded[start : start + 1, :] = value[x : x + 1]
    for along_x, at in ((-1, 0), (1, 9)):
        start = at * ROWS + 8
        padded[start : start + EDGE, :] = beside(*planes(along_x, 0))
        for along_y, row, source in ((-1, 7, 7), (1, 16, 0)):
            value = beside(*planes(along_x, along_y))
            padded[at * ROWS + row : at * ROWS + row + 1, :] = value[source : source + 1]


def fill_windows(first, second, shifted, windows):
    for along_y in range(3):
        for x in range(10):
            start = x * ROWS + 7 + along_y
            shifted[along_y, x] = jnp.concatenate(
                [first[start : start + EDGE, :], second[start : start + EDGE, :]], axis=0
            ).astype(BF16)
    for pair in range(4):
        for along_x in range(3):
            for along_y in range(3):
                place = (3 * along_x + along_y) * 256
                windows[pair * 128 : (pair + 1) * 128, place : place + 256] = shifted[
                    along_y, along_x : along_x + EDGE, :, pair * 128 : pair * 128 + 256
                ].reshape(128, 256)


def fill_direct(kernel_ref, direct):
    for group in range(9):
        block = kernel_ref[group * 192 : (group + 1) * 192, :]
        none = jnp.zeros((64, 64), BF16)
        direct[group * 256 : (group + 1) * 256, :] = jnp.concatenate(
            [
                jnp.concatenate([block, none], axis=0),
                jnp.concatenate([none, block], axis=0),
            ],
            axis=1,
        )


def fill_flipped(kernel_ref, flipped):
    none = jnp.zeros((64, 64), BF16)
    for group in range(9):
        base = 3 * (8 - group)
        blocks = [kernel_ref[(base + z) * 64 : (base + z + 1) * 64, :] for z in (2, 1, 0)]
        lanes = slice(group * 256, (group + 1) * 256)
        flipped[0:64, lanes] = jnp.concatenate(blocks + [none], axis=1)
        flipped[64:128, lanes] = jnp.concatenate([none] + blocks, axis=1)


def spread_kernel(
    first_ref,
    second_ref,
    occ_ref,
    nb_ref,
    direct_ref,
    flipped_ref,
    first_flipped_ref,
    occupied_ref,
    near_nb_ref,
):
    near_nb_ref[...] = nb_ref[...]
    occupied_ref[...] = spread(occ_ref)
    fill_direct(first_ref, direct_ref)
    fill_flipped(second_ref, flipped_ref)
    fill_flipped(first_ref, first_flipped_ref)


def times_flipped(windows, flipped):
    return lax.dot_general(
        windows, flipped, (((1,), (1,)), ((), ())), preferred_element_type=F32
    )


def paired(natural):
    return jnp.concatenate([natural[:, p * 128 : (p + 1) * 128] for p in range(4)], axis=0)


def unpaired(value):
    return jnp.concatenate([value[p * 128 : (p + 1) * 128] for p in range(4)], axis=1)


def gather_blocks(product):
    pieces = []
    for group in range(9):
        at = group * 256
        pieces.append(product[0:64, at : at + 192] + product[64:128, at + 64 : at + 256])
    pieces.append(jnp.zeros((64, PACKED - 27 * 64), F32))
    return jnp.concatenate(pieces, axis=1)


def tile_place(chunk, tile):
    row, lane = EDGE * (tile // 4), 128 * (tile % 4)
    if row < 96:
        return 32 * chunk + row % 32, WIDE * (row // 32) + lane
    return 32 * chunk + row - 96 + 16 * (lane // 256), 3 * WIDE + lane % 256


def main_kernel(
    me_ref,
    nb_ref,
    x_ref,
    masked_ref,
    occupied_ref,
    near_ref,
    longer_ref,
    shorter_ref,
    kept_in,
    direct,
    flipped,
    grads_ref,
    out_ref,
    kept_ref,
    taken,
    padded,
    shifted,
    windows,
    product,
    wide,
    boxes,
):
    me = me_ref[0]
    for member in range(4):
        at = 4 * member
        taken[at : at + 4] = near_ref[member, 0:64, :].reshape(4, 16, WIDE)
        taken[at + 16 : at + 20] = longer_ref[member].reshape(4, 16, WIDE)
    for number in range(2):
        taken[32 + 4 * number : 36 + 4 * number] = shorter_ref[number].reshape(4, 16, WIDE)
    taken[40:44] = kept_in[...]
    for brick in range(2):
        values = {}
        for number, offset in enumerate(DIRECTIONS):
            present, place = take_place(nb_ref, me, brick, number)
            values[offset] = jnp.where(present, taken[place].astype(F32), 0.0)

        def own_first(x):
            return x_ref[brick, x].astype(F32)

        def own_second(x):
            return masked_ref[x].astype(F32)[brick * EDGE : (brick + 1) * EDGE]

        fill_padded(padded.at[0, brick], own_first, lambda offset: values[offset][0:8])
        fill_padded(padded.at[1, brick], own_second, lambda offset: values[offset][8:16])
    for field in range(2):
        fill_windows(padded.at[field, 0], padded.at[field, 1], shifted.at[field], windows.at[field])
    occupied = paired(occupied_ref[...])
    pre_act = jnp.dot(windows[0], direct[...], preferred_element_type=F32)
    logistic = 1.0 / (1.0 + jnp.exp(-pre_act))
    hidden = (pre_act * logistic * occupied).astype(BF16)
    slope = logistic * (1.0 + pre_act * (1.0 - logistic))
    hidden_grad = times_flipped(windows[1], flipped[...])
    pre_grads = (hidden_grad * slope * occupied).astype(BF16)

    natural = unpaired(pre_grads.astype(F32))
    for x in range(EDGE):
        grads_ref[x] = natural[16 * x : 16 * x + 16].astype(BF16)
        for brick in range(2):
            at = 16 * x + EDGE * brick
            wide[brick, x * EDGE : (x + 1) * EDGE, :] = natural[at : at + EDGE]
    for brick in range(2):
        faces = face_values(wide, brick)
        for number, offset in enumerate(DIRECTIONS):
            boxes[send_place(nb_ref, me, brick, number)] = faces[face_kind(offset)]
    for member in range(4):
        out_ref[member, 0:64, :] = (
            boxes[8 * member : 8 * member + 8].reshape(64, WIDE).astype(BF16)
        )
    kept_ref[...] = boxes[32:36]

    for half, own, field in ((0, hidden, 1), (1, pre_grads, 0)):
        turned = own.astype(F32).T.astype(BF16)
        product[...] = jnp.dot(turned, windows[field], preferred_element_type=F32)
        packed = gather_blocks(product).astype(BF16)
        for chunk in range(2):
            start = 32 * chunk
            for part in range(3):
                at = 64 + 32 * part
                out_ref[2 * half + chunk, at : at + 32, :] = packed[
                    start : start + 32, part * WIDE : (part + 1) * WIDE
                ]
            rest = packed[start : start + 32, 3 * WIDE :]
            out_ref[2 * half + chunk, 160:176, :] = jnp.concatenate(
                [rest[0:16], rest[16:32]], axis=1
            )


def first_sum_kernel(parts_ref, pieces_ref):
    total = parts_ref[0, 64:176, :].astype(F32)
    for member in range(1, 4):
        total = total + parts_ref[member, 64:176, :].astype(F32)
    count = pieces_ref.shape[1]
    for tile in range(56):
        row, lane = EDGE * (tile // 4), 128 * (tile % 4)
        pieces_ref[tile // count, tile % count] = total[
            row : row + EDGE, lane : lane + 128
        ].astype(BF16)


def next_sum_kernel(scaling, parts_ref, copies_ref):
    total = parts_ref[0].astype(F32)
    for member in range(1, parts_ref.shape[0]):
        total = total + parts_ref[member].astype(F32)
    total = total * scaling
    for member in range(copies_ref.shape[0]):
        copies_ref[member] = total.astype(copies_ref.dtype)


def input_grads_kernel(
    me_ref,
    nb_ref,
    grads_ref,
    occupied_ref,
    near_ref,
    longer_ref,
    shorter_ref,
    kept_ref,
    flipped,
    out_ref,
    taken,
    padded,
    shifted,
    windows,
):
    me = me_ref[0]
    for member in range(4):
        at = 4 * member
        taken[at : at + 4] = near_ref[member, 0:32, :].astype(F32).reshape(4, EDGE, WIDE)
        taken[at + 16 : at + 20] = longer_ref[member].astype(F32).reshape(4, EDGE, WIDE)
    for number in range(2):
        taken[32 + 4 * number : 36 + 4 * number] = (
            shorter_ref[number].astype(F32).reshape(4, EDGE, WIDE)
        )
    taken[40:44] = kept_ref[...]
    for brick in range(2):
        values = {}
        for number, offset in enumerate(DIRECTIONS):
            present, place = take_place(nb_ref, me, brick, number)
            values[offset] = jnp.where(present, taken[place], 0.0)

        def own(x):
            return grads_ref[x].astype(F32)[brick * EDGE : (brick + 1) * EDGE]

        fill_padded(padded.at[brick], own, lambda offset: values[offset])
    fill_windows(padded.at[0], padded.at[1], shifted, windows)
    result = unpaired(times_flipped(windows[...], flipped[...])) * occupied_ref[...]
    for x in range(EDGE):
        for brick in range(2):
            at = 16 * x + EDGE * brick
            out_ref[brick, x] = result[at : at + EDGE].astype(BF16)


def unpack_kernel(parts_ref, first_hbm, second_hbm, first_out, second_out, halves, sems):
    count = parts_ref.shape[1]
    for chunk in (2, 3, 0, 1):
        for tile in range(56):
            row, lane = tile_place(chunk, tile)
            halves[row : row + EDGE, lane : lane + 128] = parts_ref[
                4 * (tile // count) + chunk, tile % count
            ].astype(F32)
    first_out[...] = halves[64:128, : 27 * 64]
    first_copy = pltpu.make_async_copy(first_out, first_hbm, sems.at[0])
    first_copy.start()
    blocks = []
    for pair in range(14):
        turned = halves[0:64, pair * 128 : pair * 128 + 128].T
        blocks += [turned[0:64], turned[64:128]]
    second_out[...] = jnp.concatenate(blocks[26::-1], axis=1)
    second_copy = pltpu.make_async_copy(second_out, second_hbm, sems.at[1])
    second_copy.start()
    first_copy.wait()
    second_copy.wait()


def call(kernel, shapes, scratch, arguments, scalars=0, outside=0, leaving=False, megabytes=40, flops=0):
    specs = [pl.BlockSpec(memory_space=pltpu.SMEM)] * scalars
    specs += [pl.BlockSpec(memory_space=pltpu.HBM)] * outside
    specs += [pl.BlockSpec(memory_space=pltpu.VMEM)] * (len(arguments) - len(specs))
    return pl.pallas_call(
        kernel,
        out_shape=[jax.ShapeDtypeStruct(shape, kind) for shape, kind in shapes],
        in_specs=specs,
        out_specs=[pl.BlockSpec(memory_space=pltpu.HBM if leaving else pltpu.VMEM)] * len(shapes),
        scratch_shapes=scratch,
        cost_estimate=pl.CostEstimate(flops=flops, bytes_accessed=2**19, transcendentals=0),
        compiler_params=pltpu.CompilerParams(vmem_limit_bytes=megabytes * 2**20),
    )(*arguments)


def per_device(inputs, occupancy, neighbours, first_kernel, second_kernel, out_grads):
    along_grp, along_dev = lax.axis_size("grp"), lax.axis_size("dev")
    devices = along_grp * along_dev
    scaling = 1.0 / math.sqrt(inputs.shape[0] * devices * EDGE**3)
    fours = [[4 * row + member for member in range(4)] for row in range(devices // 4)]
    rows = along_dev // 4
    stacks = [
        [along_dev * grp + 4 * row + member for row in range(rows)]
        for grp in range(along_grp)
        for member in range(4)
    ]
    planes = [
        [along_dev * grp + 4 * row + member for grp in range(along_grp) for member in range(4)]
        for row in range(rows)
    ]
    me = (lax.axis_index("grp") * along_dev + lax.axis_index("dev")).reshape(1)
    vmem = pltpu.VMEM

    def swap(value, members):
        return lax.all_to_all(value, AXES, 0, 0, axis_index_groups=members, tiled=True)

    longer_way = [(i, i + 4 if i & 2 == 0 else i - 4) for i in range(devices)]
    shorter_way = [(i, i - 4 if i & 2 == 0 else i + 4) for i in range(devices)]

    def send_on(near, size):
        longer, shorter = call(
            route_kernel,
            [((4, size, WIDE), BF16), ((2, size, WIDE), BF16)],
            [],
            [me, near],
            scalars=1,
        )
        return [
            lax.ppermute(value, AXES, [(i, j) for i, j in way if 0 <= j < devices])
            for value, way in ((longer, longer_way), (shorter, shorter_way))
        ]

    near, kept, masked = call(
        pack_kernel,
        [
            ((4, 128, WIDE), BF16),
            ((4, 16, WIDE), BF16),
            ((EDGE, 16, WIDE), BF16),
        ],
        [
            vmem((2, EDGE, EDGE, WIDE), BF16),
            vmem((2, EDGE, EDGE, WIDE), BF16),
            vmem((2, EDGE, 64), jnp.int32),
            vmem((4, 64, WIDE), F32),
            vmem((36, 16, WIDE), BF16),
            pltpu.SMEM((2, 26), jnp.int32),
            pltpu.SemaphoreType.DMA((4,)),
        ],
        [me, neighbours, inputs, out_grads, occupancy],
        scalars=1,
        outside=4,
        megabytes=60,
    )
    near = swap(near, fours)
    longer, shorter = send_on(near, 64)
    direct, flipped, first_flipped, occupied, near_nb = call(
        spread_kernel,
        [
            ((2304, 128), BF16),
            ((128, 2304), BF16),
            ((128, 2304), BF16),
            ((128, WIDE), F32),
            ((2, 26), jnp.int32),
        ],
        [],
        [first_kernel, second_kernel, occupancy, neighbours],
    )
    pre_grads, near, kept = call(
        main_kernel,
        [((EDGE, 16, WIDE), BF16), ((4, 176, WIDE), BF16), ((4, EDGE, WIDE), F32)],
        [
            vmem((44, 16, WIDE), BF16),
            vmem((2, 2, 10 * ROWS, PADDED), F32),
            vmem((2, 3, 10, 16, PADDED), BF16),
            vmem((2, 512, 2304), BF16),
            vmem((128, 2304), F32),
            vmem((2, 64, WIDE), F32),
            vmem((36, EDGE, WIDE), F32),
        ],
        [me, near_nb, inputs, masked, occupied, near, longer, shorter, kept, direct, flipped],
        scalars=2,
        flops=2**30,
    )
    near = swap(near, fours)
    longer, shorter = send_on(near, 32)
    piece = (56 // along_grp, EDGE, 128)
    (sums,) = call(first_sum_kernel, [((along_grp,) + piece, BF16)], [], [near])
    sums = lax.all_to_all(sums, "grp", 0, 0, tiled=True)
    (sums,) = call(functools.partial(next_sum_kernel, 1.0), [((rows,) + piece, BF16)], [], [sums])
    sums = swap(sums, stacks)
    (sums,) = call(
        functools.partial(next_sum_kernel, scaling), [((4 * along_grp,) + piece, BF16)], [], [sums]
    )
    sums = swap(sums, planes)
    (input_grads,) = call(
        input_grads_kernel,
        [((2, EDGE, EDGE, WIDE), BF16)],
        [
            vmem((44, EDGE, WIDE), F32),
            vmem((2, 10 * ROWS, PADDED), F32),
            vmem((3, 10, 16, PADDED), BF16),
            vmem((512, 2304), BF16),
        ],
        [me, near_nb, pre_grads, occupied, near, longer, shorter, kept, first_flipped],
        scalars=2,
        flops=2**28,
    )
    first_grads, second_grads = call(
        unpack_kernel,
        [((64, 27 * 64), F32), ((64, 27 * 64), F32)],
        [
            vmem((64, 27 * 64), F32),
            vmem((64, 27 * 64), F32),
            vmem((128, PACKED), F32),
            pltpu.SemaphoreType.DMA((2,)),
        ],
        [sums],
        leaving=True,
    )
    return input_grads, first_grads.T, second_grads.T


def solution(mesh):
    in_specs = (
        P(("grp", "dev"), None, None, None),
        P(("grp", "dev"), None, None),
        P(("grp", "dev"), None),
        P(),
        P(),
        P(("grp", "dev"), None, None, None),
    )
    out_specs = (P(("grp", "dev"), None, None, None), P(), P())
    return jax.shard_map(
        per_device, mesh=mesh, in_specs=in_specs, out_specs=out_specs, check_vma=False
    )
```
